32 devices in a mesh: col: 4 (over y, x), row: 8 (over z, core).
Axes of the slice: x: 2, y: 2, z: 4, core: 2. Of those that a mesh axis runs over, the one named last changes fastest.
Arguments:
- lengths: int32 [2, 32], P(None, ('col', 'row')), may hold values from 2 to 1024, as said below
- items: int32 [2, 32, 1024], P(None, ('col', 'row')), may hold values from 0 to 25599, as said below
- negatives: int32 [512], replicated, may hold values from 0 to 25599, as said below
- time_buckets: int32 [2, 32, 1024], P(None, ('col', 'row')), may hold values from 0 to 63, as said below
- table: float32 [25600, 512], P('row', 'col'), may hold values from -0.6 to 0.6
- table_m: float32 [25600, 512], P('row', 'col'), may hold values from -1.4305115e-06 to 1.4305115e-06
- table_v: float32 [25600, 512], P('row', 'col'), may hold values from 4.7683716e-15 to 1.9073486e-14
- w_in: float32 [512, 2048], P(('col', 'row')), may hold values from -0.25 to 0.25
- w_in_m: float32 [512, 2048], P(('col', 'row')), may hold values from -2.670288e-05 to 2.670288e-05
- w_in_v: float32 [512, 2048], P(('col', 'row')), may hold values from 1.5449524e-12 to 6.1798097e-12
- w_out: float32 [512, 512], P(('col', 'row')), may hold values from -0.0390625 to 0.0390625
- w_out_m: float32 [512, 512], P(('col', 'row')), may hold values from -2.670288e-05 to 2.670288e-05
- w_out_v: float32 [512, 512], P(('col', 'row')), may hold values from 1.5449524e-12 to 6.1798097e-12
- gains: float32 [3, 512], P(None, ('col', 'row')), may hold values from 0.28 to 2.6
- gains_m: float32 [3, 512], P(None, ('col', 'row')), may hold values from -5.340576e-05 to 5.340576e-05
- gains_v: float32 [3, 512], P(None, ('col', 'row')), may hold values from 6.1798097e-12 to 2.4719239e-11
- rab: float32 [8, 32], replicated, may hold values from -4 to 4
- rab_m: float32 [8, 32], replicated, may hold values from -7.6293945e-06 to 7.6293945e-06
- rab_v: float32 [8, 32], replicated, may hold values from 1.7166138e-13 to 6.866455e-13
Outputs:
- loss_sum: float32 [], replicated
- loss_count: float32 [], replicated
- grad_norm: float32 [], replicated
- table_new: float32 [25600, 512], P('row', 'col')
- table_m_new: float32 [25600, 512], P('row', 'col')
- table_v_new: float32 [25600, 512], P('row', 'col')
- table_low: bfloat16 [25600, 512], P('row', 'col')
- w_in_new: float32 [512, 2048], P(('col', 'row'))
- w_in_m_new: float32 [512, 2048], P(('col', 'row'))
- w_in_v_new: float32 [512, 2048], P(('col', 'row'))
- w_in_low: bfloat16 [512, 2048], P(('col', 'row'))
- w_out_new: float32 [512, 512], P(('col', 'row'))
- w_out_m_new: float32 [512, 512], P(('col', 'row'))
- w_out_v_new: float32 [512, 512], P(('col', 'row'))
- w_out_low: bfloat16 [512, 512], P(('col', 'row'))
- gains_new: float32 [3, 512], P(None, ('col', 'row'))
- gains_m_new: float32 [3, 512], P(None, ('col', 'row'))
- gains_v_new: float32 [3, 512], P(None, ('col', 'row'))
- rab_new: float32 [8, 32], replicated
- rab_m_new: float32 [8, 32], replicated
- rab_v_new: float32 [8, 32], replicated
The draws below stay inside these ranges and needn't reach their ends.
Inputs may be any that keep to these rules, and one draw needn't show every extreme that they name: lengths reach 1024 in every draw. In each history, exactly 128 events name items of each block of 3200 rows. negatives[j] lies in the block of 3200 rows number j // 64. `time_buckets`: nondecreasing along each history, 0 at its first slot.
All inputs are finite; a program needn't handle non-finite values.
Results may differ from the reference program's by a relative error of at most 0.0081.
Values may be sent and summed in bfloat16 or wider, within the bound.
No kernel may reach another device: no remote copies, remote signals or barrier semaphores. Data moves between devices by JAX's collectives and lax.ppermute only.
A program may use at most 192 MiB of HBM per device.

```python
from functools import partial
import jax
import jax.numpy as jnp
from jax import lax

D = 512
HEADS = 8
HEAD_DIM = 64
NEG = 512
ROWS_DEV = 3200
SEQ = 1024
NB = 32
NBT = 64
STEP = 10
MB = 2
B = 32
ITEMS = 25600
PER_OWNER = 128
NEG_OWN = 64
N_COL = 4
N_ROW = 8


def draw_lengths(key, part):
    key = jax.random.fold_in(key, 11)
    first_key, second_key = jax.random.split(key)
    samples = jnp.arange(B, dtype=jnp.int32)
    col_place = samples // N_ROW
    row_place = samples % N_ROW
    weight_col = 4 + 4 * col_place // max(N_COL - 1, 1)
    weight_row = 2 + 4 * row_place // max(N_ROW - 1, 1)
    factors = jax.random.randint(first_key, (MB, B), 100, 251)
    drawn = SEQ * weight_col[None, :] * weight_row[None, :] * factors // 5600
    chosen = jax.random.randint(second_key, (), 0, B)
    forced = (jnp.arange(MB)[:, None] == 0) & (samples[None, :] == chosen)
    drawn = jnp.where(forced, SEQ, drawn)
    return jnp.clip(drawn, 2, SEQ).astype(jnp.int32)


def draw_items(key, part):
    key = jax.random.fold_in(key, 12)
    owner_key, offset_key = jax.random.split(key)
    pattern = jnp.tile(jnp.arange(N_ROW, dtype=jnp.int32), PER_OWNER)
    owner_keys = jax.random.split(owner_key, MB * B)
    owners = jax.vmap(lambda one_key: jax.random.permutation(one_key, pattern))(owner_keys)
    offsets = jax.random.randint(offset_key, (MB * B, SEQ), 0, ROWS_DEV)
    return (owners * ROWS_DEV + offsets).reshape(MB, B, SEQ).astype(jnp.int32)


def draw_negatives(key, part):
    key = jax.random.fold_in(key, 13)
    owners = jnp.arange(NEG, dtype=jnp.int32) // NEG_OWN
    offsets = jax.random.randint(key, (NEG,), 0, ROWS_DEV)
    return (owners * ROWS_DEV + offsets).astype(jnp.int32)


def draw_time_buckets(key, part):
    key = jax.random.fold_in(key, 14)
    stepping = (jax.random.randint(key, (MB, B, SEQ), 0, SEQ) < min(SEQ // 2, 48)).astype(jnp.int32)
    stepping = stepping.at[:, :, 0].set(0)
    return jnp.minimum(jnp.cumsum(stepping, axis=-1), NBT - 1).astype(jnp.int32)


def draw_gains(key, part):
    key = jax.random.fold_in(key, 15)
    ramp_place = jnp.arange(D, dtype=jnp.float32) / (D - 1)
    ramp_gain = 0.5 + ramp_place
    spread = jax.random.uniform(key, (3, D), jnp.float32, 0.8, 1.25)
    return ramp_gain[None, :] * spread


def steps_of(rng, dims, cuts, low, largest):
    loudness, own = 1.0, jax.random.fold_in(rng, 6)
    for position, blocks in cuts:
        steps = jnp.exp(jax.random.uniform(jax.random.fold_in(own, position), (blocks,), jnp.float32, low / len(cuts), largest / len(cuts)))
        loudness = loudness * jnp.repeat(steps, dims[position] // blocks).reshape([-1 if axis == position else 1 for axis in range(len(dims))])
    return loudness


def centred(stream_key, shape, scale, reach, cuts=(), kind=jnp.bfloat16):
    loudness = steps_of(stream_key, shape, cuts, -0.22, 0.18) if cuts else 1.0
    result = jax.random.normal(stream_key, shape, jnp.float32) * scale * loudness
    return jnp.minimum(jnp.maximum(result, -reach), reach).astype(kind)


def setup_inputs(seed: int = 0) -> dict:
    streams_of = jax.random.split(jax.random.key(seed), 20)
    return {
        "lengths": draw_lengths(jax.random.fold_in(streams_of[19], 71), 0),
        "items": draw_items(jax.random.fold_in(streams_of[19], 71), 0),
        "negatives": draw_negatives(jax.random.fold_in(streams_of[19], 71), 0),
        "time_buckets": draw_time_buckets(jax.random.fold_in(streams_of[19], 71), 0),
        "table": centred(streams_of[4], (ITEMS, D), 0.1, 0.6, ((0, 8), (1, 4)), jnp.float32),
        "table_m": centred(streams_of[5], (ITEMS, D), (0.11 * 0.0025 * (5 * D * D) ** -0.5), 1.430511474609375e-06, ((0, 8), (1, 4)), jnp.float32),
        "table_v": jnp.clip(4.76837155305161e-15 + 1.430511465915483e-14 * jax.random.uniform(streams_of[6], (ITEMS, D), jnp.float32) ** steps_of(streams_of[6], (ITEMS, D), ((0, 8), (1, 4)), -0.2, 0.2), 4.76837155305161e-15, 1.907348621220644e-14),
        "w_in": centred(streams_of[7], (D, 4 * D), D ** -0.5, 0.25, ((0, 32),), jnp.float32),
        "w_in_m": centred(streams_of[8], (D, 4 * D), (0.11 * 0.045 * (5 * D * D) ** -0.5), 2.6702880859375e-05, ((0, 32),), jnp.float32),
        "w_in_v": jnp.clip(1.544952425540369e-12 + 4.634857276621107e-12 * jax.random.uniform(streams_of[9], (D, 4 * D), jnp.float32) ** steps_of(streams_of[9], (D, 4 * D), ((0, 32),), -0.2, 0.2), 1.544952425540369e-12, 6.179809702161476e-12),
        "w_out": centred(streams_of[10], (D, D), (0.16 * D ** -0.5), 0.0390625, ((0, 32),), jnp.float32),
        "w_out_m": centred(streams_of[11], (D, D), (0.11 * 0.045 * (5 * D * D) ** -0.5), 2.6702880859375e-05, ((0, 32),), jnp.float32),
        "w_out_v": jnp.clip(1.544952425540369e-12 + 4.634857276621107e-12 * jax.random.uniform(streams_of[12], (D, D), jnp.float32) ** steps_of(streams_of[12], (D, D), ((0, 32),), -0.2, 0.2), 1.544952425540369e-12, 6.179809702161476e-12),
        "gains": draw_gains(jax.random.fold_in(streams_of[19], 71), 0),
        "gains_m": centred(streams_of[14], (3, D), (0.11 * 0.09 * (5 * D * D) ** -0.5), 5.340576171875e-05, ((1, 32),), jnp.float32),
        "gains_v": jnp.clip(6.179809702161476e-12 + 1.853942910648443e-11 * jax.random.uniform(streams_of[15], (3, D), jnp.float32) ** steps_of(streams_of[15], (3, D), ((1, 32),), -0.2, 0.2), 6.179809702161476e-12, 2.4719238808645905e-11),
        "rab": centred(streams_of[16], (HEADS, NB), 1.0, 4.0, (), jnp.float32),
        "rab_m": centred(streams_of[17], (HEADS, NB), (0.11 * 0.015 * (5 * D * D) ** -0.5), 7.62939453125e-06, (), jnp.float32),
        "rab_v": jnp.clip(jax.random.uniform(streams_of[18], (HEADS, NB), jnp.float32, 1.7166137760392386e-13, 6.866455104156954e-13), 1.7166137760392386e-13, 6.866455104156954e-13),
    }


@jax.custom_vjp
def low(v):
    return lax.optimization_barrier(v.astype(jnp.bfloat16)).astype(jnp.float32)

@jax.custom_vjp
def low_back(v):
    return v

def low_keep(v):
    return (low(v), None)

def low_pass(kept, grad):
    return (grad,)

def back_keep(v):
    return (v, None)

def back_low(kept, grad):
    return (low(grad),)
low.defvjp(low_keep, low_pass)
low_back.defvjp(back_keep, back_low)
BETA_ONE = 0.9
BETA_TWO = 0.999
EPS_ADAM = 1e-08
EPS_NORM = 1e-06
WEIGHT_DECAY = 0.01
CLIP_NORM = 0.05
RATE_TABLE = 0.06
RATE_DENSE = 0.01
RATE_SMALL = 0.5
SCORE_SCALE = 0.5

def matmul(left, right):
    return jnp.dot(left, right, precision=lax.Precision.HIGHEST)

def rms_norm(values, gain):
    return values * lax.rsqrt(lax.optimization_barrier(jnp.mean(values * values, axis=-1, keepdims=True)) + EPS_NORM) * gain

def split_heads(values):
    return values.reshape(SEQ, HEADS, HEAD_DIM).transpose(1, 0, 2)

def history_loss(tab_low, w_big, w_small, gain_all, bias_table, neg_rows, item_ids, buckets, length):
    embedded = low_back(tab_low[item_ids])
    normed = rms_norm(embedded, gain_all[0])
    project = low_back(matmul(low(normed), w_big))
    active = project * jax.nn.sigmoid(project)
    gate_part = active[:, :D]
    value_part = low(active[:, D:2 * D])
    query_part = low(active[:, 2 * D:3 * D])
    keys_part = low(active[:, 3 * D:])
    relative = jnp.clip(buckets[:, None] - buckets[None, :], 0, NB - 1)
    scores = SCORE_SCALE * jnp.einsum('hid,hjd->hij', split_heads(query_part), split_heads(keys_part), precision=lax.Precision.HIGHEST) + bias_table[:, relative]
    scores = low_back(scores)
    places = jnp.arange(SEQ)
    visible = (places[None, :] <= places[:, None]) & (places[None, :] < length)
    attend = low(jnp.where(visible[None], scores * jax.nn.sigmoid(scores), 0.0) / SEQ)
    attended = low_back(jnp.einsum('hij,hjd->hid', attend, split_heads(value_part), precision=lax.Precision.HIGHEST))
    merged = attended.transpose(1, 0, 2).reshape(SEQ, D)
    mixed = low(rms_norm(merged, gain_all[1]) * gate_part)
    hidden = embedded + low_back(matmul(mixed, w_small))
    final_out = low(rms_norm(hidden, gain_all[2]))
    target = jnp.concatenate([embedded[1:], jnp.zeros((1, D), embedded.dtype)], axis=0)
    positive = lax.optimization_barrier(jnp.sum(final_out * target, axis=-1))
    negative = low_back(matmul(final_out, neg_rows.T))
    highest = jnp.maximum(lax.optimization_barrier(jnp.max(negative, axis=-1)), positive)
    totals = jnp.exp(positive - highest) + lax.optimization_barrier(jnp.sum(jnp.exp(negative - highest[:, None]), axis=-1))
    losses = highest + jnp.log(totals) - positive
    return jnp.sum(jnp.where(places < length - 1, losses, 0.0))

def adamw_update(weight, first, second, grad, rate):
    first = BETA_ONE * first + (1.0 - BETA_ONE) * grad
    second = BETA_TWO * second + (1.0 - BETA_TWO) * grad * grad
    fixed_first = first / (1.0 - BETA_ONE ** STEP)
    fixed_second = second / (1.0 - BETA_TWO ** STEP)
    weight = weight - rate * (fixed_first / (jnp.sqrt(fixed_second) + EPS_ADAM) + WEIGHT_DECAY * weight)
    return (weight, first, second)

def reference(lengths, items, negatives, time_buckets, table, table_m, table_v, w_in, w_in_m, w_in_v, w_out, w_out_m, w_out_v, gains, gains_m, gains_v, rab, rab_m, rab_v):

    def forward(tab, w_big, w_small, gain_all, bias_table):
        tab_low = low(tab)
        w_big = low(w_big)
        w_small = low(w_small)
        gain_all = low(gain_all)
        neg_rows = tab_low[negatives]
        one_history = jax.checkpoint(partial(history_loss, tab_low, w_big, w_small, gain_all, bias_table, neg_rows))
        loss_total = jnp.zeros((), tab.dtype)

        def scan_step(carry, inputs):
            return (carry + one_history(inputs[0], inputs[1], inputs[2]), None)
        for micro_batch in range(MB):
            loss_total, _ = lax.scan(scan_step, loss_total, (items[micro_batch], time_buckets[micro_batch], lengths[micro_batch]))
        return loss_total
    loss_sum, pull_back = jax.vjp(forward, table, w_in, w_out, gains, rab)
    grads = pull_back(jnp.ones((), loss_sum.dtype))
    loss_count = jnp.sum(jnp.maximum(lengths - 1, 0)).astype(table.dtype)
    grads = [grad / loss_count for grad in grads]
    squares = jnp.zeros((), table.dtype)
    for grad in grads:
        squares = squares + jnp.sum(grad * grad)
    grad_norm = jnp.sqrt(squares)
    factor = jnp.minimum(1.0, CLIP_NORM / grad_norm)
    clipped = [grad * factor for grad in grads]
    table_new, table_m_new, table_v_new = adamw_update(table, table_m, table_v, clipped[0], RATE_TABLE)
    w_in_new, w_in_m_new, w_in_v_new = adamw_update(w_in, w_in_m, w_in_v, clipped[1], RATE_DENSE)
    w_out_new, w_out_m_new, w_out_v_new = adamw_update(w_out, w_out_m, w_out_v, clipped[2], RATE_DENSE)
    gains_new, gains_m_new, gains_v_new = adamw_update(gains, gains_m, gains_v, clipped[3], RATE_SMALL)
    rab_new, rab_m_new, rab_v_new = adamw_update(rab, rab_m, rab_v, clipped[4], RATE_SMALL)
    return (loss_sum, loss_count, grad_norm, table_new, table_m_new, table_v_new, table_new.astype(jnp.bfloat16), w_in_new, w_in_m_new, w_in_v_new, w_in_new.astype(jnp.bfloat16), w_out_new, w_out_m_new, w_out_v_new, w_out_new.astype(jnp.bfloat16), gains_new, gains_m_new, gains_v_new, rab_new, rab_m_new, rab_v_new)
```

```python
import jax
import jax.numpy as jnp
from jax import lax
from jax.experimental import pallas as pl
from jax.experimental.pallas import tpu as pltpu
from jax.sharding import PartitionSpec as P

NB = 32
STEP = 10
BETA_ONE = 0.9
BETA_TWO = 0.999
EPS_ADAM = 1e-08
EPS_NORM = 1e-06
WEIGHT_DECAY = 0.01
CLIP_NORM = 0.05
RATE_TABLE = 0.06
RATE_DENSE = 0.01
RATE_SMALL = 0.5
BOTH = ("col", "row")
TILE = 256
BF = jnp.bfloat16
F32 = jnp.float32


def dot_nn(left, right):
    return lax.dot_general(left, right, (((1,), (0,)), ((), ())), preferred_element_type=F32)


def dot_nt(left, right):
    return lax.dot_general(left, right, (((1,), (1,)), ((), ())), preferred_element_type=F32)


def dot_tn(left, right):
    return lax.dot_general(left, right, (((0,), (0,)), ((), ())), preferred_element_type=F32)


def row_scale(values):
    return lax.rsqrt(jnp.mean(values * values, axis=-1, keepdims=True) + EPS_NORM)


def row_back(values, scale, grad):
    cubed = scale * scale * scale
    return scale * grad - values * (cubed * jnp.mean(grad * values, axis=-1, keepdims=True))


def silu_slope(values):
    half = 0.5 * jnp.tanh(0.5 * values)
    sigmoid = 0.5 + half
    active = values * sigmoid
    return active, sigmoid + active * (0.5 - half)


def history_kernel(
    len_ref,
    recv_ref,
    order_ref,
    bucket_ref,
    dense_ref,
    negs_ref,
    gains_ref,
    bias_ref,
    ge_ref,
    big_ref,
    small_ref,
    gneg_ref,
    misc_ref,
    rab_ref,
    rows_s,
    event_s,
    normed_s,
    gatein_s,
    slope_s,
    value_s,
    valuem_s,
    query_s,
    keys_s,
    keyst_s,
    hot_s,
    hott_s,
    orderc_s,
    out_s,
    gout_s,
    ggate_s,
    gevent_s,
    dvalue_s,
    dkeys_s,
    dqueryt_s,
    gslots_s,
    carry_s,
    pairs_s,
):
    pieces, seq, piece = recv_ref.shape
    width = event_s.shape[1]
    groups = width // 128
    heads = 2 * groups
    length = len_ref[0]
    tiles = lax.div(length + (TILE - 1), TILE)
    gain_in = gains_ref[0:1, :]
    gain_mid = gains_ref[1:2, :]
    gain_out = gains_ref[2:3, :]
    lane = lax.broadcasted_iota(jnp.int32, (TILE, 128), 1)
    low_lanes = lane < 64

    def place(step):
        return pl.ds(pl.multiple_of(step * TILE, TILE), TILE)

    for one in range(pieces):
        rows_s[:, one * piece : (one + 1) * piece] = recv_ref[one]
    lane_square = lax.broadcasted_iota(jnp.int32, (128, 128), 1)
    for part in range(seq // 128):
        span = slice(part * 128, (part + 1) * 128)
        spread = jnp.broadcast_to(order_ref[0:1, span].astype(F32), (128, 128))
        orderc_s[span, :] = spread.T.astype(jnp.int32)
        spread = jnp.broadcast_to(bucket_ref[0:1, span].astype(F32), (128, 128))
        column = spread.T.astype(jnp.int32)
        hot_s[span, :] = jnp.where(
            column == jnp.bitwise_and(lane_square, 63), 1.0, 0.0
        ).astype(BF)
        hott_s[:, span] = jnp.where(
            bucket_ref[0:1, span] == 63 - lax.broadcasted_iota(jnp.int32, (64, 128), 0), 1.0, 0.0
        ).astype(BF)
    big_ref[...] = jnp.zeros_like(big_ref)
    small_ref[...] = jnp.zeros_like(small_ref)
    gneg_ref[...] = jnp.zeros_like(gneg_ref)
    misc_ref[...] = jnp.zeros_like(misc_ref)
    gslots_s[...] = jnp.zeros_like(gslots_s)
    carry_s[...] = jnp.zeros_like(carry_s)
    pairs_s[...] = jnp.zeros_like(pairs_s)

    def project(step, _):
        span = place(step)
        hot = jnp.where(
            order_ref[0:1, :] == lax.broadcasted_iota(jnp.int32, (TILE, seq), 0) + step * TILE,
            1.0,
            0.0,
        ).astype(BF)
        event = dot_nn(hot, rows_s[...])
        event_s[span, :] = event.astype(BF)
        normed = (event * row_scale(event) * gain_in).astype(BF)
        normed_s[span, :] = normed
        gatein_s[span, :] = dot_nn(normed, dense_ref[:, 0:width])
        bucket = hot_s[span, :]
        active, slope = silu_slope(dot_nn(normed, dense_ref[:, width : 2 * width]))
        slope_s[0, span, :] = slope.astype(BF)
        scaled = active.astype(BF) * BF(1.0 / seq)
        for group in range(groups):
            part = scaled[:, group * 128 : (group + 1) * 128]
            value_s[group, span, :] = part
            valuem_s[2 * group, span, :] = jnp.where(low_lanes, part, BF(0))
            valuem_s[2 * group + 1, span, :] = jnp.where(low_lanes, BF(0), part)
        active, slope = silu_slope(dot_nn(normed, dense_ref[:, 2 * width : 3 * width]))
        slope_s[1, span, :] = slope.astype(BF)
        scaled = active.astype(BF) * BF(0.25)
        bias = dot_nn(bucket, bias_ref[...]).astype(BF)
        for group in range(groups):
            part = scaled[:, group * 128 : (group + 1) * 128]
            query_s[2 * group, span, 0:128] = jnp.where(low_lanes, part, BF(0))
            query_s[2 * group + 1, span, 0:128] = jnp.where(low_lanes, BF(0), part)
            query_s[2 * group, span, 128:256] = bias[:, group * 256 : group * 256 + 128]
            query_s[2 * group + 1, span, 128:256] = bias[:, group * 256 + 128 : group * 256 + 256]
        active, slope = silu_slope(dot_nn(normed, dense_ref[:, 3 * width : 4 * width]))
        slope_s[2, span, :] = slope.astype(BF)
        scaled = active.astype(BF)
        for group in range(groups):
            part = scaled[:, group * 128 : (group + 1) * 128]
            keys_s[group, span, 0:128] = part
            keys_s[group, span, 128:256] = bucket
            turned = part.T
            keyst_s[2 * group, :, span] = turned[0:64, :]
            keyst_s[2 * group + 1, :, span] = turned[64:128, :]
        for group in range(groups):
            dvalue_s[group, span, :] = jnp.zeros((TILE, 128), F32)
        for head in range(heads):
            dkeys_s[head, span, :] = jnp.zeros((TILE, 256), F32)
            dqueryt_s[head, :, span] = jnp.zeros((64, TILE), F32)
        return 0

    lax.fori_loop(0, tiles, project, 0)

    square_row = lax.broadcasted_iota(jnp.int32, (TILE, TILE), 0)
    square_col = lax.broadcasted_iota(jnp.int32, (TILE, TILE), 1)

    def attend_group(group, _):
        def attend_tile(step, _):
            span = place(step)

            def attend(other, masked):
                near = place(other)
                total = None
                for half in range(2):
                    scores = dot_nt(query_s[2 * group + half, span, :], keys_s[group, near, :])
                    weight = scores + scores * jnp.tanh(scores)
                    if masked:
                        weight = jnp.where(square_col <= square_row, weight, 0.0)
                    part = dot_nn(weight.astype(BF), valuem_s[2 * group + half, near, :])
                    total = part if total is None else total + part
                return total

            out_s[group, span, :] = attend(step, True)

            def before(other, _):
                out_s[group, span, :] += attend(other, False)
                return 0

            lax.fori_loop(0, step, before, 0)
            return 0

        lax.fori_loop(0, tiles, attend_tile, 0)
        return 0

    lax.fori_loop(0, groups, attend_group, 0)

    def middle(step, _):
        span = place(step)
        event = event_s[span, :].astype(F32)
        merged = jnp.concatenate([out_s[group, span, :] for group in range(groups)], axis=1)
        scale_mid = row_scale(merged)
        normed_mid = merged * scale_mid
        gate, gate_slope = silu_slope(gatein_s[span, :])
        mixed = (normed_mid * gain_mid * gate).astype(BF)
        hidden = event + dot_nn(mixed, dense_ref[:, 4 * width : 5 * width])
        scale_out = row_scale(hidden)
        final = (hidden * scale_out * gain_out).astype(BF)
        final_f = final.astype(F32)
        following = event_s[pl.ds(pl.multiple_of((step + 1) * TILE, TILE), 16), :][0:1, :].astype(F32)
        following = jnp.where(step + 1 < tiles, following, 0.0)
        row_id = lax.broadcasted_iota(jnp.int32, (TILE, width), 0)
        target = jnp.where(
            row_id == TILE - 1, following, pltpu.roll(event, TILE - 1, 0)
        )
        positive = jnp.sum(final_f * target, axis=-1, keepdims=True)
        negative = dot_nt(final, negs_ref[...])
        highest = jnp.maximum(jnp.max(negative, axis=-1, keepdims=True), positive)
        neg_exp = jnp.exp(negative - highest)
        pos_exp = jnp.exp(positive - highest)
        totals = pos_exp + jnp.sum(neg_exp, axis=-1, keepdims=True)
        counted = (
            lax.broadcasted_iota(jnp.int32, (TILE, 1), 0) + step * TILE < length - 1
        )
        losses = jnp.where(counted, highest + jnp.log(totals) - positive, 0.0)
        misc_ref[3:4, :] += jnp.broadcast_to(jnp.sum(losses, axis=0, keepdims=True), (1, width))
        share = jnp.where(counted, 1.0 / totals, 0.0)
        grad_neg = (neg_exp * share).astype(BF)
        grad_pos = jnp.where(counted, pos_exp * share - 1.0, 0.0)
        grad_final = dot_nn(grad_neg, negs_ref[...]) + grad_pos * target
        gneg_ref[...] += dot_tn(grad_neg, final)
        pushed = grad_pos * final_f
        grad_event = jnp.where(row_id == 0, carry_s[0:1, :], pltpu.roll(pushed, 1, 0))
        carry_s[0:1, :] = pushed[TILE - 1 : TILE, :]
        misc_ref[2:3, :] += jnp.sum(grad_final * hidden * scale_out, axis=0, keepdims=True)
        grad_hidden = row_back(hidden, scale_out, grad_final * gain_out)
        gevent_s[span, :] = grad_event + grad_hidden
        branch = grad_hidden.astype(BF)
        small_ref[...] += dot_tn(mixed, branch)
        grad_mixed = dot_nt(branch, dense_ref[:, 4 * width : 5 * width])
        gated = grad_mixed * gate
        misc_ref[1:2, :] += jnp.sum(gated * normed_mid, axis=0, keepdims=True)
        ggate_s[span, :] = (grad_mixed * normed_mid * gain_mid * gate_slope).astype(BF)
        grad_out = row_back(merged, scale_mid, gated * gain_mid).astype(BF) * BF(0.5)
        for group in range(groups):
            part = grad_out[:, group * 128 : (group + 1) * 128]
            gout_s[2 * group, span, :] = jnp.where(low_lanes, part, BF(0))
            gout_s[2 * group + 1, span, :] = jnp.where(low_lanes, BF(0), part)
        return 0

    lax.fori_loop(0, tiles, middle, 0)

    def retreat_group(group, _):
        def retreat_tile(step, _):
            near = place(step)

            def retreat(other, masked):
                span = place(other)
                keys = keys_s[group, near, :]
                value = value_s[group, near, :]
                total = None
                for half in range(2):
                    head = 2 * group + half
                    gout = gout_s[head, span, :]
                    query = query_s[head, span, :]
                    scores = dot_nt(keys, query)
                    grads = dot_nt(value, gout)
                    bent = 1.0 + jnp.tanh(scores)
                    weight = scores * bent
                    slope = bent * ((1.0 + (scores + scores)) - weight)
                    grads = grads * slope
                    if masked:
                        visible = square_row <= square_col
                        weight = jnp.where(visible, weight, 0.0)
                        grads = jnp.where(visible, grads, 0.0)
                    grads = grads.astype(BF)
                    part = dot_nn(weight.astype(BF), gout)
                    total = part if total is None else total + part
                    dkeys_s[head, near, :] += dot_nn(
                        grads, jnp.concatenate([query[:, 0:128], hot_s[span, :]], axis=1)
                    )
                    dqueryt_s[head, :, span] += dot_nn(keyst_s[head, :, near], grads)
                dvalue_s[group, near, :] += total

            retreat(step, True)

            def after(other, _):
                retreat(other, False)
                return 0

            lax.fori_loop(step + 1, tiles, after, 0)
            return 0

        lax.fori_loop(0, tiles, retreat_tile, 0)
        return 0

    lax.fori_loop(0, groups, retreat_group, 0)

    def finish(step, _):
        span = place(step)
        normed = normed_s[span, :]
        parts = [ggate_s[span, :]]
        grad = jnp.concatenate([dvalue_s[group, span, :] for group in range(groups)], axis=1)
        parts.append((grad * (2.0 / seq) * slope_s[0, span, :].astype(F32)).astype(BF))
        grad = jnp.concatenate(
            [
                jnp.concatenate([dqueryt_s[2 * group, :, span], dqueryt_s[2 * group + 1, :, span]], axis=0).T
                for group in range(groups)
            ],
            axis=1,
        )
        parts.append((grad * 0.5 * slope_s[1, span, :].astype(F32)).astype(BF))
        grad = jnp.concatenate(
            [
                dkeys_s[2 * group, span, 0:128] + dkeys_s[2 * group + 1, span, 0:128]
                for group in range(groups)
            ],
            axis=1,
        )
        parts.append((grad * 2.0 * slope_s[2, span, :].astype(F32)).astype(BF))
        grad_normed = None
        for index in range(4):
            columns = slice(index * width, (index + 1) * width)
            big_ref[:, columns] += dot_tn(normed, parts[index])
            part = dot_nt(parts[index], dense_ref[:, columns])
            grad_normed = part if grad_normed is None else grad_normed + part
        hott = hott_s[:, span]
        for head in range(heads):
            wide = dkeys_s[head, span, 128:256]
            upper = wide.astype(BF)
            lower = (wide - upper.astype(F32)).astype(BF)
            pairs_s[head] += dot_nn(hott, upper) + dot_nn(hott, lower)
        event = event_s[span, :].astype(F32)
        scale = row_scale(event)
        misc_ref[0:1, :] += jnp.sum(grad_normed * event * scale, axis=0, keepdims=True)
        total = gevent_s[span, :] + row_back(event, scale, grad_normed * gain_in)
        column = orderc_s[...]
        hot = jnp.where(
            jnp.concatenate([column] * (TILE // 128), axis=1)
            == lax.broadcasted_iota(jnp.int32, (seq, TILE), 1) + step * TILE,
            1.0,
            0.0,
        ).astype(BF)
        gslots_s[...] += dot_nn(hot, total.astype(BF))
        return 0

    lax.fori_loop(0, tiles, finish, 0)

    for one in range(pieces):
        ge_ref[one] = gslots_s[:, one * piece : (one + 1) * piece].astype(BF)
    lane_row = lax.broadcasted_iota(jnp.int32, (64, 128), 1)
    for head in range(heads):
        kept = jnp.where(lane_row < 64, pairs_s[head], 0.0)
        turned = pltpu.roll(kept, 0, 1, stride=1, stride_axis=0)
        rab_ref[head : head + 1, :] = jnp.sum(turned, axis=0, keepdims=True)


def history_call(length, recv, order, bucket, dense, negs, gains, bias):
    pieces, seq, piece = recv.shape
    width = pieces * piece
    heads = width // 64
    groups = heads // 2
    vmem = pl.BlockSpec(memory_space=pltpu.VMEM)
    return pl.pallas_call(
        history_kernel,
        out_shape=(
            jax.ShapeDtypeStruct(recv.shape, BF),
            jax.ShapeDtypeStruct((width, 4 * width), F32),
            jax.ShapeDtypeStruct((width, width), F32),
            jax.ShapeDtypeStruct(negs.shape, F32),
            jax.ShapeDtypeStruct((8, width), F32),
            jax.ShapeDtypeStruct((heads, 128), F32),
        ),
        in_specs=[pl.BlockSpec(memory_space=pltpu.SMEM)] + [vmem] * 7,
        out_specs=(vmem,) * 6,
        scratch_shapes=[
            pltpu.VMEM((seq, width), BF),
            pltpu.VMEM((seq + TILE, width), BF),
            pltpu.VMEM((seq, width), BF),
            pltpu.VMEM((seq, width), F32),
            pltpu.VMEM((3, seq, width), BF),
            pltpu.VMEM((groups, seq, 128), BF),
            pltpu.VMEM((heads, seq, 128), BF),
            pltpu.VMEM((heads, seq, 256), BF),
            pltpu.VMEM((groups, seq, 256), BF),
            pltpu.VMEM((heads, 64, seq), BF),
            pltpu.VMEM((seq, 128), BF),
            pltpu.VMEM((64, seq), BF),
            pltpu.VMEM((seq, 128), jnp.int32),
            pltpu.VMEM((groups, seq, 128), F32),
            pltpu.VMEM((heads, seq, 128), BF),
            pltpu.VMEM((seq, width), BF),
            pltpu.VMEM((seq, width), F32),
            pltpu.VMEM((groups, seq, 128), F32),
            pltpu.VMEM((heads, seq, 256), F32),
            pltpu.VMEM((heads, 64, seq), F32),
            pltpu.VMEM((seq, width), F32),
            pltpu.VMEM((8, width), F32),
            pltpu.VMEM((heads, 64, 128), F32),
        ],
        compiler_params=pltpu.CompilerParams(vmem_limit_bytes=60 * 1024 * 1024),
        name="history",
    )(length, recv, order, bucket, dense, negs, gains, bias)


def lookup_kernel(hist_ref, ids_ref, table_ref, found_ref, stage_s):
    count = hist_ref.shape[0]
    per = stage_s.shape[0]

    def one(place, _):
        base = hist_ref[place] * per
        for index in range(per):
            stage_s[index : index + 1, :] = table_ref[pl.ds(ids_ref[base + index], 1), :]
        found_ref[pl.ds(pl.multiple_of(place * per, per), per), :] = stage_s[...].astype(BF)
        return 0

    lax.fori_loop(0, count, one, 0)


def lookup_call(hist, ids, table, per):
    count = hist.shape[0]
    smem = pl.BlockSpec(memory_space=pltpu.SMEM)
    vmem = pl.BlockSpec(memory_space=pltpu.VMEM)
    return pl.pallas_call(
        lookup_kernel,
        out_shape=jax.ShapeDtypeStruct((count * per, table.shape[1]), BF),
        in_specs=[smem, smem, vmem],
        out_specs=vmem,
        scratch_shapes=[pltpu.VMEM((per, table.shape[1]), F32)],
        compiler_params=pltpu.CompilerParams(vmem_limit_bytes=16 * 1024 * 1024),
        name="lookup",
    )(hist, ids, table)


def scatter_kernel(hist_ref, ids_ref, grads_ref, init_ref, total_ref, stage_s, *sums):
    count = hist_ref.shape[0]
    per = stage_s.shape[0]
    for one in sums:
        one[...] = jnp.zeros_like(one)

    def one(place, _):
        base = hist_ref[place] * per
        stage_s[...] = grads_ref[pl.ds(pl.multiple_of(place * per, per), per), :].astype(F32)
        for index in range(per):
            held = sums[index % len(sums)]
            spot = pl.ds(ids_ref[base + index], 1)
            held[spot, :] = held[spot, :] + stage_s[index : index + 1, :]
        return 0

    lax.fori_loop(0, count, one, 0)
    total = init_ref[...]
    for one in sums:
        total = total + one[...]
    total_ref[...] = total


def scatter_call(hist, ids, grads, init, per):
    smem = pl.BlockSpec(memory_space=pltpu.SMEM)
    vmem = pl.BlockSpec(memory_space=pltpu.VMEM)
    return pl.pallas_call(
        scatter_kernel,
        out_shape=jax.ShapeDtypeStruct(init.shape, F32),
        in_specs=[smem, smem, vmem, vmem],
        out_specs=vmem,
        scratch_shapes=[pltpu.VMEM((per, init.shape[1]), F32)] + [pltpu.VMEM(init.shape, F32)] * 4,
        compiler_params=pltpu.CompilerParams(vmem_limit_bytes=32 * 1024 * 1024),
        name="scatter",
    )(hist, ids, grads, init)


def negs_kernel(spots_ref, share_ref, grads_ref, total_ref, square_ref):
    total_ref[...] = grads_ref[...]
    for index in range(spots_ref.shape[0]):
        spot = pl.ds(spots_ref[index], 1)
        total_ref[spot, :] = total_ref[spot, :] + share_ref[index : index + 1, :]
    total = total_ref[...]
    square_ref[...] = jnp.sum(total * total, axis=0, keepdims=True)


def negs_call(spots, share, grads):
    smem = pl.BlockSpec(memory_space=pltpu.SMEM)
    vmem = pl.BlockSpec(memory_space=pltpu.VMEM)
    return pl.pallas_call(
        negs_kernel,
        out_shape=(
            jax.ShapeDtypeStruct(grads.shape, F32),
            jax.ShapeDtypeStruct((1, grads.shape[1]), F32),
        ),
        in_specs=[smem, vmem, vmem],
        out_specs=(vmem, vmem),
        compiler_params=pltpu.CompilerParams(vmem_limit_bytes=32 * 1024 * 1024),
        name="negatives",
    )(spots, share, grads)


def bias_table(rab):
    place = jnp.arange(64)
    both = 0.5 * rab[:, jnp.clip(place[:, None] - place[None, :], 0, NB - 1)]
    upper = lax.reduce_precision(both, 8, 7)
    parts = jnp.concatenate([upper, both - upper], axis=2).astype(BF)
    parts = parts.transpose(1, 0, 2).reshape(64, -1)
    return jnp.concatenate([parts, jnp.zeros_like(parts)], axis=0)


def fold_bias(spread):
    return jnp.concatenate(
        [
            jnp.sum(spread[:, :64], axis=1, keepdims=True),
            spread[:, 64 : 62 + NB],
            jnp.sum(spread[:, 62 + NB :], axis=1, keepdims=True),
        ],
        axis=1,
    )


def adamw_update(weight, first, second, grad, rate):
    first = BETA_ONE * first + (1.0 - BETA_ONE) * grad
    second = BETA_TWO * second + (1.0 - BETA_TWO) * grad * grad
    fixed_first = first / (1.0 - BETA_ONE**STEP)
    fixed_second = second / (1.0 - BETA_TWO**STEP)
    weight = weight - rate * (
        fixed_first / (jnp.sqrt(fixed_second) + EPS_ADAM) + WEIGHT_DECAY * weight
    )
    return (weight, first, second)


def exchange(values, axes, groups=None):
    return lax.all_to_all(
        values, axes, split_axis=0, concat_axis=0, tiled=True, axis_index_groups=groups
    )


def spread_sum(values, devices):
    copies = jnp.broadcast_to(values[None], (devices,) + values.shape)
    return jnp.sum(exchange(copies, BOTH), axis=0)


def fold_dense(grads, col_count, row_count):
    rows, columns = grads.shape
    half = row_count // 2
    pairs = [[2 * index, 2 * index + 1] for index in range(half)]
    alike = [list(range(first, row_count, 2)) for first in range(2)]
    own = rows // (col_count * row_count)
    low = grads.astype(BF).reshape(col_count * half, 2, own, columns).transpose(1, 0, 2, 3)
    got = exchange(low.reshape(2, rows // 2, columns), "row", pairs)
    low = jnp.sum(got.astype(F32), axis=0).astype(BF)
    got = exchange(low.reshape(col_count, half * own, columns), "col")
    low = jnp.sum(got.astype(F32), axis=0).astype(BF)
    got = exchange(low.reshape(half, own, columns), "row", alike)
    return jnp.sum(got.astype(F32), axis=0)


def local(
    lengths,
    items,
    negatives,
    time_buckets,
    table,
    table_m,
    table_v,
    w_in,
    w_in_m,
    w_in_v,
    w_out,
    w_out_m,
    w_out_v,
    gains,
    gains_m,
    gains_v,
    rab,
    rab_m,
    rab_v,
):
    col_count = lax.axis_size("col")
    row_count = lax.axis_size("row")
    devices = col_count * row_count
    row_place = lax.axis_index("row")
    me = lax.axis_index("col") * row_count + row_place
    rows_dev, piece = table.shape
    own, width = w_out.shape
    slots, _, seq = items.shape
    per = seq // row_count
    neg_total = negatives.shape[0]
    neg_own = neg_total // row_count
    own_negs = (
        lax.dynamic_slice_in_dim(negatives, row_place * neg_own, neg_own) - row_place * rows_dev
    )
    dense = lax.all_gather(
        jnp.concatenate(
            [
                w_in.astype(BF),
                w_out.astype(BF),
                table[own_negs].astype(BF).reshape(own, -1),
                jnp.pad(gains.T, ((0, 0), (0, 128 - gains.shape[0]))).astype(BF),
            ],
            axis=1,
        ),
        BOTH,
        axis=0,
        tiled=True,
    )
    neg_rows = (
        dense[:, 5 * width : 6 * width]
        .reshape(col_count, row_count, neg_own, piece)
        .transpose(1, 2, 0, 3)
        .reshape(neg_total, width)
    )
    gain_all = dense[:, 6 * width : 6 * width + gains.shape[0]].T.astype(F32)
    bias = bias_table(rab)
    mine = items[:, 0]
    key, sorted_items = lax.sort(
        (mine // rows_dev * seq + jnp.arange(seq)[None, :], mine), dimension=1, num_keys=1
    )
    block = key // seq
    order = key - block * seq
    numbers = (sorted_items - block * rows_dev).reshape(slots, row_count, per).transpose(1, 0, 2)
    told = jnp.concatenate(
        [
            numbers.reshape(row_count, slots * per),
            jnp.broadcast_to(jnp.pad(lengths[:, 0], (0, 128 - slots))[None], (row_count, 128)),
        ],
        axis=1,
    )
    told = jnp.broadcast_to(told[None], (col_count,) + told.shape).reshape(devices, -1)
    heard = exchange(told, BOTH)
    ids = heard[:, : slots * per].reshape(-1)
    every_length = heard[:, slots * per : slots * per + slots].reshape(-1)
    total = devices * slots
    number = jnp.arange(total)
    ahead = (every_length[None, :] > every_length[:, None]) | (
        (every_length[None, :] == every_length[:, None]) & (number[None, :] < number[:, None])
    )
    rank = jnp.sum(ahead.astype(jnp.int32), axis=1)
    wanted = jnp.stack(
        [
            slot * devices + (jnp.arange(devices) if slot % 2 == 0 else devices - 1 - jnp.arange(devices))
            for slot in range(slots)
        ]
    )
    hist = jnp.sum(
        jnp.where(rank[None, None, :] == wanted[:, :, None], number[None, None, :], 0), axis=2
    )
    my_hist = lax.dynamic_slice_in_dim(hist, me, 1, axis=1)[:, 0]
    about = jnp.stack([order, time_buckets[:, 0]], axis=1)
    about = lax.all_gather(about, "row", axis=0, tiled=True)
    about = lax.all_gather(about, "col", axis=0, tiled=True)
    sent = []
    for slot in range(slots):
        found = lookup_call(hist[slot], ids, table, per)
        sent.append(exchange(found.reshape(devices, per, piece), BOTH))
    back = []
    dense_grads = None
    for slot in range(slots):
        own_about = lax.dynamic_slice_in_dim(about, my_hist[slot], 1, axis=0)[0]
        results = history_call(
            lax.dynamic_slice_in_dim(every_length, my_hist[slot], 1),
            sent[slot].reshape(col_count, seq, piece),
            own_about[0:1],
            own_about[1:2],
            dense,
            neg_rows,
            gain_all,
            bias,
        )
        back.append(exchange(results[0].reshape(devices, per, piece), BOTH))
        grads = results[1:]
        if dense_grads is None:
            dense_grads = grads
        else:
            dense_grads = tuple(first + second for first, second in zip(dense_grads, grads))
    grad_big, grad_small, grad_negs, grad_misc, grad_spread = dense_grads
    loss_count = jnp.sum(jnp.maximum(every_length - 1, 0)).astype(F32)
    packed = jnp.concatenate(
        [
            grad_big,
            grad_small,
            grad_negs.reshape(row_count, neg_own, col_count, piece)
            .transpose(2, 0, 1, 3)
            .reshape(width, -1),
            jnp.pad(grad_misc[:3].T, ((0, 0), (0, 125))),
        ],
        axis=1,
    )
    shard = fold_dense(packed, col_count, row_count)
    shared = jnp.concatenate(
        [fold_bias(grad_spread).reshape(-1), jnp.broadcast_to(grad_misc[3, 0], (128,))]
    )
    shared = spread_sum(shared, devices)
    rab_sum = shared[: rab.size].reshape(rab.shape)
    loss_sum = shared[rab.size]
    table_sum = jnp.zeros((rows_dev, piece), F32)
    for slot in range(slots):
        table_sum = scatter_call(
            hist[slot], ids, back[slot].reshape(devices * per, piece), table_sum, per
        )
    table_sum, squares = negs_call(
        own_negs, shard[:, 5 * width : 6 * width].reshape(neg_own, piece), table_sum
    )
    shard_big = shard[:, : 4 * width]
    shard_small = shard[:, 4 * width : 5 * width]
    shard_gain = shard[:, 6 * width : 6 * width + 3].T
    local_squares = (
        jnp.sum(squares)
        + jnp.sum(shard_big * shard_big)
        + jnp.sum(shard_small * shard_small)
        + jnp.sum(shard_gain * shard_gain)
    )
    all_squares = spread_sum(jnp.broadcast_to(local_squares, (128,)), devices)[0]
    grad_norm = jnp.sqrt(all_squares + jnp.sum(rab_sum * rab_sum)) / loss_count
    factor = jnp.minimum(1.0, CLIP_NORM / grad_norm) / loss_count
    table_new, table_m_new, table_v_new = adamw_update(
        table, table_m, table_v, table_sum * factor, RATE_TABLE
    )
    w_in_new, w_in_m_new, w_in_v_new = adamw_update(
        w_in, w_in_m, w_in_v, shard_big * factor, RATE_DENSE
    )
    w_out_new, w_out_m_new, w_out_v_new = adamw_update(
        w_out, w_out_m, w_out_v, shard_small * factor, RATE_DENSE
    )
    gains_new, gains_m_new, gains_v_new = adamw_update(
        gains, gains_m, gains_v, shard_gain * factor, RATE_SMALL
    )
    rab_new, rab_m_new, rab_v_new = adamw_update(rab, rab_m, rab_v, rab_sum * factor, RATE_SMALL)
    return (
        loss_sum,
        loss_count,
        grad_norm,
        table_new,
        table_m_new,
        table_v_new,
        table_new.astype(BF),
        w_in_new,
        w_in_m_new,
        w_in_v_new,
        w_in_new.astype(BF),
        w_out_new,
        w_out_m_new,
        w_out_v_new,
        w_out_new.astype(BF),
        gains_new,
        gains_m_new,
        gains_v_new,
        rab_new,
        rab_m_new,
        rab_v_new,
    )


def solution(mesh):
    placed = (
        P(None, ("col", "row")),
        P(None, ("col", "row"), None),
        P(),
        P(None, ("col", "row"), None),
        P("row", "col"),
        P("row", "col"),
        P("row", "col"),
        P(("col", "row"), None),
        P(("col", "row"), None),
        P(("col", "row"), None),
        P(("col", "row"), None),
        P(("col", "row"), None),
        P(("col", "row"), None),
        P(None, ("col", "row")),
        P(None, ("col", "row")),
        P(None, ("col", "row")),
        P(),
        P(),
        P(),
    )
    return jax.shard_map(
        local,
        mesh=mesh,
        in_specs=placed,
        out_specs=(
            P(),
            P(),
            P(),
            P("row", "col"),
            P("row", "col"),
            P("row", "col"),
            P("row", "col"),
            P(("col", "row"), None),
            P(("col", "row"), None),
            P(("col", "row"), None),
            P(("col", "row"), None),
            P(("col", "row"), None),
            P(("col", "row"), None),
            P(("col", "row"), None),
            P(("col", "row"), None),
            P(None, ("col", "row")),
            P(None, ("col", "row")),
            P(None, ("col", "row")),
            P(),
            P(),
            P(),
        ),
        check_vma=False,
    )
```

```python
import functools
import jax
import jax.numpy as jnp
from jax import lax
from jax.experimental import pallas as pl
from jax.experimental.pallas import tpu as pltpu
from jax.sharding import PartitionSpec as P

NB = 32
STEP = 10
BETA_ONE = 0.9
BETA_TWO = 0.999
EPS_ADAM = 1e-08
EPS_NORM = 1e-06
WEIGHT_DECAY = 0.01
CLIP_NORM = 0.05
RATE_TABLE = 0.06
RATE_DENSE = 0.01
RATE_SMALL = 0.5
BOTH = ("col", "row")
TILE = 256
BF = jnp.bfloat16
F32 = jnp.float32


def dot_nn(left, right):
    return lax.dot_general(left, right, (((1,), (0,)), ((), ())), preferred_element_type=F32)


def dot_nt(left, right):
    return lax.dot_general(left, right, (((1,), (1,)), ((), ())), preferred_element_type=F32)


def dot_tn(left, right):
    return lax.dot_general(left, right, (((0,), (0,)), ((), ())), preferred_element_type=F32)


def row_scale(values):
    return lax.rsqrt(jnp.mean(values * values, axis=-1, keepdims=True) + EPS_NORM)


def row_back(values, scale, grad):
    cubed = scale * scale * scale
    return scale * grad - values * (cubed * jnp.mean(grad * values, axis=-1, keepdims=True))


def silu_slope(values):
    half = 0.5 * jnp.tanh(0.5 * values)
    sigmoid = 0.5 + half
    active = values * sigmoid
    return active, sigmoid + active * (0.5 - half)


def history_kernel(last, blocked, *refs):
    if last:
        (len_ref, core_ref, recv_ref, dense_ref, bias_ref, misc0_ref, big0_ref, small0_ref, gneg0_ref) = refs[:9]
        (ge_ref, misc_ref, keep_ref, send_ref) = refs[9:13]
        (big_ref, small_ref, gneg_ref, load_sem) = refs[13:17]
        scratch = refs[17:]
    else:
        (len_ref, recv_ref, dense_ref, bias_ref) = refs[:4]
        (ge_ref, misc_ref, big_ref, small_ref, gneg_ref) = refs[4:9]
        scratch = refs[9:]
    (
        rows_s,
        event_s,
        normed_s,
        gatein_s,
        slope_s,
        valuem_s,
        query_s,
        keys_s,
        keyst_s,
        hot_s,
        hott_s,
        orderc_s,
        order_s,
        out_s,
        gout_s,
        ggate_s,
        dkeys_s,
        dqueryt_s,
        gslots_s,
        carry_s,
        pairs_s,
        gains_s,
        negs_s,
        bias_s,
    ) = scratch
    pieces, blocks, tall, piece = recv_ref.shape
    per = tall - 16
    seq, width = normed_s.shape
    groups = width // 128
    heads = 2 * groups
    devices = pieces * blocks
    own = width // devices
    length = len_ref[0]
    tiles = lax.div(length + (TILE - 1), TILE)
    lane = lax.broadcasted_iota(jnp.int32, (TILE, 128), 1)
    low_lanes = lane < 64
    if last:
        loads = [
            pltpu.make_async_copy(big0_ref, big_ref, load_sem.at[0]),
            pltpu.make_async_copy(small0_ref, small_ref, load_sem.at[1]),
            pltpu.make_async_copy(gneg0_ref, gneg_ref, load_sem.at[2]),
        ]
        for one in loads:
            one.start()
    else:
        big_ref[...] = jnp.zeros_like(big_ref)
        small_ref[...] = jnp.zeros_like(small_ref)
        gneg_ref[...] = jnp.zeros_like(gneg_ref)

    def place(step):
        return pl.ds(pl.multiple_of(step * TILE, TILE), TILE)

    for block in range(blocks):
        span = slice(block * per, (block + 1) * per)
        for one in range(pieces):
            rows_s[span, one * piece : (one + 1) * piece] = recv_ref[one, block, 0:per, :]
        about = recv_ref[0, block, per : per + 16, :].astype(F32)
        spot = about[0:1, 0:per] * 32.0 + about[1:2, 0:per]
        order_s[0:1, span] = spot.astype(jnp.int32)
        orderc_s[span, :] = jnp.broadcast_to(about[0:1, :] * 32.0 + about[1:2, :], (128, 128)).T[0:per, :].astype(jnp.int32)
        rows_s[span, width : width + 128] = jnp.broadcast_to(about[2:3, :], (128, 128)).T[0:per, :].astype(BF)
    if blocked:
        for one in range(pieces):
            for block in range(blocks):
                source = slice((one * blocks + block) * own, (one * blocks + block + 1) * own)
                for index in range(width // piece):
                    start = (block * (width // piece) + index) * own
                    negs_s[start : start + own, one * piece : (one + 1) * piece] = dense_ref[
                        source, 5 * width + index * piece : 5 * width + (index + 1) * piece
                    ]
    else:
        negs_s[...] = dense_ref[:, 5 * width : 6 * width]
    gains_s[...] = dense_ref[:, 6 * width : 6 * width + 128].astype(F32).T[0:8, :]
    lane_half = lax.broadcasted_iota(jnp.int32, (64, 128), 1) < 64
    for head in range(heads):
        line = jnp.broadcast_to(bias_ref[head : head + 1, :], (64, 128))
        wide = pltpu.roll(line, 0, 1, stride=1, stride_axis=0)
        again = pltpu.roll(wide, 64, 1)
        whole = jnp.where(lane_half, wide, again)
        upper = whole.astype(BF)
        lower = (whole - upper.astype(F32)).astype(BF)
        bias_s[0:64, head * 128 : (head + 1) * 128] = jnp.where(lane_half, upper, lower)
    bias_s[64:128, :] = jnp.zeros((64, heads * 128), BF)
    misc_ref[...] = misc0_ref[...] if last else jnp.zeros_like(misc_ref)
    gslots_s[...] = jnp.zeros_like(gslots_s)
    carry_s[...] = jnp.zeros_like(carry_s)
    pairs_s[...] = jnp.zeros_like(pairs_s)
    gain_in = gains_s[0:1, :]
    gain_mid = gains_s[1:2, :]
    gain_out = gains_s[2:3, :]

    def project(step, _):
        span = place(step)
        hot = jnp.where(
            order_s[0:1, :] == lax.broadcasted_iota(jnp.int32, (TILE, seq), 0) + step * TILE,
            1.0,
            0.0,
        ).astype(BF)
        wide = dot_nn(hot, rows_s[...])
        event = wide[:, 0:width]
        times = wide[:, width : width + 128].astype(jnp.int32)
        bucket = jnp.where(times == jnp.bitwise_and(lane, 63), 1.0, 0.0).astype(BF)
        hot_s[span, :] = bucket
        hott_s[:, span] = jnp.where(times == 63 - lane, 1.0, 0.0).T[0:64, :].astype(BF)
        event_s[span, :] = event.astype(BF)
        normed = (event * row_scale(event) * gain_in).astype(BF)
        normed_s[span, :] = normed
        gatein_s[span, :] = dot_nn(normed, dense_ref[:, 0:width])
        active, slope = silu_slope(dot_nn(normed, dense_ref[:, width : 2 * width]))
        slope_s[0, span, :] = slope.astype(BF)
        scaled = active.astype(BF) * BF(1.0 / seq)
        for group in range(groups):
            part = scaled[:, group * 128 : (group + 1) * 128]
            valuem_s[2 * group, span, :] = jnp.where(low_lanes, part, BF(0))
            valuem_s[2 * group + 1, span, :] = jnp.where(low_lanes, BF(0), part)
        active, slope = silu_slope(dot_nn(normed, dense_ref[:, 2 * width : 3 * width]))
        slope_s[1, span, :] = slope.astype(BF)
        scaled = active.astype(BF) * BF(0.25)
        bias = dot_nn(bucket, bias_s[...]).astype(BF)
        for group in range(groups):
            part = scaled[:, group * 128 : (group + 1) * 128]
            query_s[2 * group, span, 0:128] = jnp.where(low_lanes, part, BF(0))
            query_s[2 * group + 1, span, 0:128] = jnp.where(low_lanes, BF(0), part)
            query_s[2 * group, span, 128:256] = bias[:, group * 256 : group * 256 + 128]
            query_s[2 * group + 1, span, 128:256] = bias[:, group * 256 + 128 : group * 256 + 256]
        active, slope = silu_slope(dot_nn(normed, dense_ref[:, 3 * width : 4 * width]))
        slope_s[2, span, :] = slope.astype(BF)
        scaled = active.astype(BF)
        for group in range(groups):
            part = scaled[:, group * 128 : (group + 1) * 128]
            keys_s[group, span, 0:128] = part
            keys_s[group, span, 128:256] = bucket
            turned = part.T
            keyst_s[2 * group, :, span] = turned[0:64, :]
            keyst_s[2 * group + 1, :, span] = turned[64:128, :]
        for head in range(heads):
            dkeys_s[head, span, :] = jnp.zeros((TILE, 256), F32)
            dqueryt_s[head, :, span] = jnp.zeros((64, TILE), F32)
        return 0

    lax.fori_loop(0, tiles, project, 0)

    square_row = lax.broadcasted_iota(jnp.int32, (TILE, TILE), 0)
    square_col = lax.broadcasted_iota(jnp.int32, (TILE, TILE), 1)

    def attend_group(group, _):
        def attend_tile(step, _):
            span = place(step)

            def attend(other, masked):
                near = place(other)
                total = None
                for half in range(2):
                    scores = dot_nt(query_s[2 * group + half, span, :], keys_s[group, near, :])
                    weight = scores + scores * jnp.tanh(scores)
                    if masked:
                        weight = jnp.where(square_col <= square_row, weight, 0.0)
                    part = dot_nn(weight.astype(BF), valuem_s[2 * group + half, near, :])
                    total = part if total is None else total + part
                return total

            out_s[group, span, :] = attend(step, True)

            def before(other, _):
                out_s[group, span, :] += attend(other, False)
                return 0

            lax.fori_loop(0, step, before, 0)
            return 0

        lax.fori_loop(0, tiles, attend_tile, 0)
        return 0

    lax.fori_loop(0, groups, attend_group, 0)

    if last:
        for one in loads:
            one.wait()

    def middle(step, _):
        span = place(step)
        event = event_s[span, :].astype(F32)
        merged = jnp.concatenate([out_s[group, span, :] for group in range(groups)], axis=1)
        for group in range(groups):
            out_s[group, span, :] = jnp.zeros((TILE, 128), F32)
        scale_mid = row_scale(merged)
        normed_mid = merged * scale_mid
        gate, gate_slope = silu_slope(gatein_s[span, :])
        mixed = (normed_mid * gain_mid * gate).astype(BF)
        hidden = event + dot_nn(mixed, dense_ref[:, 4 * width : 5 * width])
        scale_out = row_scale(hidden)
        final = (hidden * scale_out * gain_out).astype(BF)
        final_f = final.astype(F32)
        following = event_s[pl.ds(pl.multiple_of((step + 1) * TILE, TILE), 16), :][0:1, :].astype(F32)
        following = jnp.where(step + 1 < tiles, following, 0.0)
        row_id = lax.broadcasted_iota(jnp.int32, (TILE, width), 0)
        target = jnp.where(
            row_id == TILE - 1, following, pltpu.roll(event, TILE - 1, 0)
        )
        positive = jnp.sum(final_f * target, axis=-1, keepdims=True)
        negative = dot_nt(final, negs_s[...])
        highest = jnp.maximum(jnp.max(negative, axis=-1, keepdims=True), positive)
        neg_exp = jnp.exp(negative - highest)
        pos_exp = jnp.exp(positive - highest)
        totals = pos_exp + jnp.sum(neg_exp, axis=-1, keepdims=True)
        counted = (
            lax.broadcasted_iota(jnp.int32, (TILE, 1), 0) + step * TILE < length - 1
        )
        losses = jnp.where(counted, highest + jnp.log(totals) - positive, 0.0)
        misc_ref[3:4, :] += jnp.broadcast_to(jnp.sum(losses, axis=0, keepdims=True), (1, width))
        share = jnp.where(counted, 1.0 / totals, 0.0)
        grad_neg = (neg_exp * share).astype(BF)
        grad_pos = jnp.where(counted, pos_exp * share - 1.0, 0.0)
        grad_final = dot_nn(grad_neg, negs_s[...]) + grad_pos * target
        gneg_ref[...] += dot_tn(grad_neg, final)
        pushed = grad_pos * final_f
        grad_event = jnp.where(row_id == 0, carry_s[0:1, :], pltpu.roll(pushed, 1, 0))
        carry_s[0:1, :] = pushed[TILE - 1 : TILE, :]
        misc_ref[2:3, :] += jnp.sum(grad_final * hidden * scale_out, axis=0, keepdims=True)
        grad_hidden = row_back(hidden, scale_out, grad_final * gain_out)
        gatein_s[span, :] = grad_event + grad_hidden
        branch = grad_hidden.astype(BF)
        small_ref[...] += dot_tn(mixed, branch)
        grad_mixed = dot_nt(branch, dense_ref[:, 4 * width : 5 * width])
        gated = grad_mixed * gate
        misc_ref[1:2, :] += jnp.sum(gated * normed_mid, axis=0, keepdims=True)
        ggate_s[span, :] = (grad_mixed * normed_mid * gain_mid * gate_slope).astype(BF)
        grad_out = row_back(merged, scale_mid, gated * gain_mid).astype(BF) * BF(0.5)
        for group in range(groups):
            part = grad_out[:, group * 128 : (group + 1) * 128]
            gout_s[2 * group, span, :] = jnp.where(low_lanes, part, BF(0))
            gout_s[2 * group + 1, span, :] = jnp.where(low_lanes, BF(0), part)
        return 0

    lax.fori_loop(0, tiles, middle, 0)

    def retreat_group(group, _):
        def retreat_tile(step, _):
            near = place(step)

            def retreat(other, masked):
                span = place(other)
                keys = keys_s[group, near, :]
                total = None
                for half in range(2):
                    head = 2 * group + half
                    gout = gout_s[head, span, :]
                    query = query_s[head, span, :]
                    scores = dot_nt(keys, query)
                    grads = dot_nt(valuem_s[head, near, :], gout)
                    bent = 1.0 + jnp.tanh(scores)
                    weight = scores * bent
                    slope = bent * ((1.0 + (scores + scores)) - weight)
                    grads = grads * slope
                    if masked:
                        visible = square_row <= square_col
                        weight = jnp.where(visible, weight, 0.0)
                        grads = jnp.where(visible, grads, 0.0)
                    grads = grads.astype(BF)
                    part = dot_nn(weight.astype(BF), gout)
                    total = part if total is None else total + part
                    dkeys_s[head, near, :] += dot_nn(
                        grads, jnp.concatenate([query[:, 0:128], hot_s[span, :]], axis=1)
                    )
                    dqueryt_s[head, :, span] += dot_nn(keyst_s[head, :, near], grads)
                out_s[group, near, :] += total

            retreat(step, True)

            def after(other, _):
                retreat(other, False)
                return 0

            lax.fori_loop(step + 1, tiles, after, 0)
            return 0

        lax.fori_loop(0, tiles, retreat_tile, 0)
        return 0

    lax.fori_loop(0, groups, retreat_group, 0)

    def finish(step, _):
        span = place(step)
        normed = normed_s[span, :]
        parts = [ggate_s[span, :]]
        grad = jnp.concatenate([out_s[group, span, :] for group in range(groups)], axis=1)
        parts.append((grad * (2.0 / seq) * slope_s[0, span, :].astype(F32)).astype(BF))
        grad = jnp.concatenate(
            [
                jnp.concatenate([dqueryt_s[2 * group, :, span], dqueryt_s[2 * group + 1, :, span]], axis=0).T
                for group in range(groups)
            ],
            axis=1,
        )
        parts.append((grad * 0.5 * slope_s[1, span, :].astype(F32)).astype(BF))
        grad = jnp.concatenate(
            [
                dkeys_s[2 * group, span, 0:128] + dkeys_s[2 * group + 1, span, 0:128]
                for group in range(groups)
            ],
            axis=1,
        )
        parts.append((grad * 2.0 * slope_s[2, span, :].astype(F32)).astype(BF))
        grad_normed = None
        for index in range(4):
            columns = slice(index * width, (index + 1) * width)
            big_ref[:, columns] += dot_tn(normed, parts[index])
            part = dot_nt(parts[index], dense_ref[:, columns])
            grad_normed = part if grad_normed is None else grad_normed + part
        hott = hott_s[:, span]
        for head in range(heads):
            wide = dkeys_s[head, span, 128:256]
            upper = wide.astype(BF)
            lower = (wide - upper.astype(F32)).astype(BF)
            pairs_s[head] += dot_nn(hott, upper) + dot_nn(hott, lower)
        event = event_s[span, :].astype(F32)
        scale = row_scale(event)
        misc_ref[0:1, :] += jnp.sum(grad_normed * event * scale, axis=0, keepdims=True)
        total = gatein_s[span, :] + row_back(event, scale, grad_normed * gain_in)
        column = orderc_s[...]
        hot = jnp.where(
            jnp.concatenate([column] * (TILE // 128), axis=1)
            == lax.broadcasted_iota(jnp.int32, (seq, TILE), 1) + step * TILE,
            1.0,
            0.0,
        ).astype(BF)
        gslots_s[...] += dot_nn(hot, total.astype(BF))
        return 0

    lax.fori_loop(0, tiles, finish, 0)

    for block in range(blocks):
        span = slice(block * per, (block + 1) * per)
        for one in range(pieces):
            ge_ref[one, block] = gslots_s[span, one * piece : (one + 1) * piece].astype(BF)
    lane_row = lax.broadcasted_iota(jnp.int32, (64, 128), 1)
    for head in range(heads):
        kept = jnp.where(lane_row < 64, pairs_s[head], 0.0)
        turned = pltpu.roll(kept, 0, 1, stride=1, stride_axis=0)
        misc_ref[8 + head : 9 + head, 0:128] += jnp.sum(turned, axis=0, keepdims=True)
    if last:
        kept = jnp.where(lax.broadcasted_iota(jnp.int32, (8, width), 0) < 3, misc_ref[0:8, :], 0.0)
        gain_rows = jnp.concatenate([kept, jnp.zeros((120, width), F32)], axis=0)
        gain_rows = gain_rows.T.astype(BF)

        def pack(out_ref, target, source, one, block):
            out_ref[target, 0 : 4 * width] = big_ref[source, :].astype(BF)
            out_ref[target, 4 * width : 5 * width] = small_ref[source, :].astype(BF)
            if blocked:
                for index in range(width // piece):
                    start = (block * (width // piece) + index) * own
                    out_ref[target, 5 * width + index * piece : 5 * width + (index + 1) * piece] = gneg_ref[
                        start : start + own, one * piece : (one + 1) * piece
                    ].astype(BF)
            else:
                out_ref[target, 5 * width : 6 * width] = gneg_ref[source, :].astype(BF)
            out_ref[target, 6 * width : 6 * width + 128] = gain_rows[source, :]

        if blocked:
            for core in range(2):

                @pl.when(core_ref[0] == core)
                def _(core=core):
                    for device in range(devices):
                        one, block = device // blocks, device % blocks
                        source = slice(device * own, (device + 1) * own)
                        target = slice(device // 2 * own, (device // 2 + 1) * own)
                        pack(keep_ref if device % 2 == core else send_ref, target, source, one, block)

        else:
            half = width // 2
            pack(keep_ref, slice(0, half), slice(0, half), 0, 0)
            pack(send_ref, slice(0, half), slice(half, width), 0, 0)


def history_call(length, recv, dense, bias, core, before, blocked):
    last = before is not None
    pieces, blocks, tall, piece = recv.shape
    per = tall - 16
    seq = blocks * per
    width = pieces * piece
    heads = width // 64
    groups = heads // 2
    neg_total = width
    vmem = pl.BlockSpec(memory_space=pltpu.VMEM)
    smem = pl.BlockSpec(memory_space=pltpu.SMEM)
    anywhere = pl.BlockSpec(memory_space=pl.ANY)
    shapes = [
        jax.ShapeDtypeStruct((pieces, blocks, per, piece), BF),
        jax.ShapeDtypeStruct((16, width), F32),
    ]
    sums = [(width, 4 * width), (width, width), (neg_total, width)]
    if last:
        operands = (length, core, recv, dense, bias, *before)
        specs = [smem, smem, vmem, vmem, vmem, vmem, anywhere, anywhere, anywhere]
        shapes += [jax.ShapeDtypeStruct((width // 2, 6 * width + 128), BF)] * 2
        extra = [pltpu.VMEM(one, F32) for one in sums] + [pltpu.SemaphoreType.DMA((3,))]
    else:
        operands = (length, recv, dense, bias)
        specs = [smem, vmem, vmem, vmem]
        shapes += [jax.ShapeDtypeStruct(one, F32) for one in sums]
        extra = []
    return pl.pallas_call(
        functools.partial(history_kernel, last, blocked),
        out_shape=tuple(shapes),
        in_specs=specs,
        out_specs=(vmem,) * len(shapes),
        scratch_shapes=extra
        + [
            pltpu.VMEM((seq, width + 128), BF),
            pltpu.VMEM((seq + TILE, width), BF),
            pltpu.VMEM((seq, width), BF),
            pltpu.VMEM((seq, width), F32),
            pltpu.VMEM((3, seq, width), BF),
            pltpu.VMEM((heads, seq, 128), BF),
            pltpu.VMEM((heads, seq, 256), BF),
            pltpu.VMEM((groups, seq, 256), BF),
            pltpu.VMEM((heads, 64, seq), BF),
            pltpu.VMEM((seq, 128), BF),
            pltpu.VMEM((64, seq), BF),
            pltpu.VMEM((seq, 128), jnp.int32),
            pltpu.VMEM((8, seq), jnp.int32),
            pltpu.VMEM((groups, seq, 128), F32),
            pltpu.VMEM((heads, seq, 128), BF),
            pltpu.VMEM((seq, width), BF),
            pltpu.VMEM((heads, seq, 256), F32),
            pltpu.VMEM((heads, 64, seq), F32),
            pltpu.VMEM((seq, width), F32),
            pltpu.VMEM((8, width), F32),
            pltpu.VMEM((heads, 64, 128), F32),
            pltpu.VMEM((8, width), F32),
            pltpu.VMEM((neg_total, width), BF),
            pltpu.VMEM((128, heads * 128), BF),
        ],
        compiler_params=pltpu.CompilerParams(vmem_limit_bytes=60 * 1024 * 1024),
        cost_estimate=pl.CostEstimate(
            flops=40_000_000_000, bytes_accessed=20_000_000, transcendentals=10_000_000
        ),
        name="history_last" if last else "history_first",
    )(*operands)


def lookup_kernel(hist_ref, ids_ref, about_ref, table_ref, found_ref, stage_s):
    count, tall, piece = found_ref.shape
    per = tall - 16

    def one(place, _):
        number = hist_ref[place]
        for index in range(per):
            stage_s[index : index + 1, :] = table_ref[pl.ds(ids_ref[number, index], 1), :]
        found_ref[place, 0:per, :] = stage_s[...].astype(BF)
        spot = about_ref[number, 1:2, :]
        upper = lax.shift_right_logical(spot, 5)
        rows = [upper, spot - upper * 32, about_ref[number, 2:3, :], jnp.zeros((13, piece), jnp.int32)]
        found_ref[place, per:tall, :] = jnp.concatenate(rows, axis=0).astype(F32).astype(BF)
        return 0

    lax.fori_loop(0, count, one, 0)


def lookup_call(hist, ids, about, table, per):
    count = hist.shape[0]
    smem = pl.BlockSpec(memory_space=pltpu.SMEM)
    vmem = pl.BlockSpec(memory_space=pltpu.VMEM)
    return pl.pallas_call(
        lookup_kernel,
        out_shape=jax.ShapeDtypeStruct((count, per + 16, table.shape[1]), BF),
        in_specs=[smem, smem, vmem, vmem],
        out_specs=vmem,
        scratch_shapes=[pltpu.VMEM((per, table.shape[1]), F32)],
        compiler_params=pltpu.CompilerParams(vmem_limit_bytes=60 * 1024 * 1024),
        cost_estimate=pl.CostEstimate(
            flops=5_000_000_000, bytes_accessed=4_000_000, transcendentals=0
        ),
        name="lookup",
    )(hist, ids, about, table)


def add_rows(hist_ref, ids_ref, grads_ref, stage_s, sums):
    count = hist_ref.shape[0]
    per = stage_s.shape[0]
    for held in sums:
        held[...] = jnp.zeros_like(held)

    def one(place, _):
        number = hist_ref[place]
        stage_s[...] = grads_ref[pl.ds(pl.multiple_of(place * per, per), per), :].astype(F32)
        for index in range(per):
            held = sums[index % len(sums)]
            spot = pl.ds(ids_ref[number, index], 1)
            held[spot, :] = held[spot, :] + stage_s[index : index + 1, :]
        return 0

    lax.fori_loop(0, count, one, 0)


def scatter_kernel(hist_ref, ids_ref, grads_ref, *refs):
    total_ref, stage_s = refs[-6:-4]
    add_rows(hist_ref, ids_ref, grads_ref, stage_s, refs[-4:])
    total = refs[-4][...]
    for held in refs[-3:]:
        total = total + held[...]
    for init_ref in refs[:-6]:
        total = total + init_ref[...]
    total_ref[...] = total


def scatter_call(hist, ids, grads, rows, per, *init):
    smem = pl.BlockSpec(memory_space=pltpu.SMEM)
    vmem = pl.BlockSpec(memory_space=pltpu.VMEM)
    piece = grads.shape[1]
    return pl.pallas_call(
        scatter_kernel,
        out_shape=jax.ShapeDtypeStruct((rows, piece), F32),
        in_specs=[smem, smem, vmem] + [vmem] * len(init),
        out_specs=vmem,
        scratch_shapes=[pltpu.VMEM((per, piece), F32)] + [pltpu.VMEM((rows, piece), F32)] * 4,
        compiler_params=pltpu.CompilerParams(vmem_limit_bytes=60 * 1024 * 1024),
        cost_estimate=pl.CostEstimate(
            flops=6_000_000_000, bytes_accessed=4_000_000, transcendentals=0
        ),
        name="scatter",
    )(hist, ids, grads, *init)


def gather_up_kernel(width, spots_ref, table_ref, misc_ref, base_ref, *refs):
    total_ref, shard_ref, gain_ref, told_ref = refs[-4:]
    shard = base_ref[...]
    for got in refs[:-4]:
        shard = shard + got[...].astype(F32)
    shard_ref[...] = shard
    own = shard.shape[0]
    total_ref[...] = table_ref[...]
    for index in range(spots_ref.shape[0]):
        spot = pl.ds(spots_ref[index], 1)
        row = index % own
        start = 5 * width + index // own * 128
        total_ref[spot, :] = total_ref[spot, :] + shard_ref[row : row + 1, start : start + 128]
    total = total_ref[...]
    squares = jnp.sum(total * total, axis=0, keepdims=True)
    for index in range(5 * width // 128):
        part = shard_ref[:, index * 128 : (index + 1) * 128]
        squares = squares + jnp.sum(part * part, axis=0, keepdims=True)
    part = shard_ref[:, 6 * width : 6 * width + 128]
    squares = squares + jnp.sum(part * part, axis=0, keepdims=True)
    turned = jnp.concatenate([part, jnp.zeros((128 - own, 128), F32)], axis=0).T
    gain_ref[...] = turned[0:8, :]
    spread = misc_ref[8:16, 0:128]
    lane = lax.broadcasted_iota(jnp.int32, (8, 128), 1)
    low = jnp.sum(jnp.where(lane < 63, spread, 0.0), axis=1, keepdims=True)
    high = jnp.sum(jnp.where(lane >= 62 + NB, spread, 0.0), axis=1, keepdims=True)
    folded = jnp.where(lane < NB - 1, pltpu.roll(spread, 65, 1), 0.0)
    folded = folded + jnp.where(lane == 0, low, 0.0) + jnp.where(lane == NB - 1, high, 0.0)
    rows = []
    for half in range(2):
        row = folded[4 * half : 4 * half + 1, :]
        for index in range(1, 4):
            row = row + pltpu.roll(folded[4 * half + index : 4 * half + index + 1, :], NB * index, 1)
        rows.append(row)
    rows += [misc_ref[3:4, 0:128], squares]
    told_ref[...] = jnp.broadcast_to(jnp.concatenate(rows, axis=0)[None], told_ref.shape)


def gather_up_call(spots, table_sum, misc, base, gots, devices):
    vmem = pl.BlockSpec(memory_space=pltpu.VMEM)
    return pl.pallas_call(
        functools.partial(gather_up_kernel, misc.shape[1]),
        out_shape=(
            jax.ShapeDtypeStruct(table_sum.shape, F32),
            jax.ShapeDtypeStruct(base.shape, F32),
            jax.ShapeDtypeStruct((8, 128), F32),
            jax.ShapeDtypeStruct((devices, 4, 128), F32),
        ),
        in_specs=[pl.BlockSpec(memory_space=pltpu.SMEM)] + [vmem] * (3 + len(gots)),
        out_specs=(vmem,) * 4,
        compiler_params=pltpu.CompilerParams(vmem_limit_bytes=60 * 1024 * 1024),
        name="gather_up",
    )(spots, table_sum, misc, base, *gots)


def fold_kernel(parts, place_ref, base_ref, *refs):
    gots = refs[: len(refs) - parts]
    own_ref = refs[len(refs) - parts]
    sends = refs[len(refs) - parts + 1 :]
    tall = own_ref.shape[0]
    for offset in range(parts):
        span = pl.ds(pl.multiple_of(lax.bitwise_xor(place_ref[0], offset) * tall, tall), tall)
        total = base_ref[span, :].astype(F32)
        for got in gots:
            total = total + got[span, :].astype(F32)
        if offset == 0:
            own_ref[...] = total
        else:
            sends[offset - 1][...] = total.astype(BF)


def fold_call(place, base, gots, parts):
    tall = base.shape[0] // parts
    vmem = pl.BlockSpec(memory_space=pltpu.VMEM)
    shapes = [jax.ShapeDtypeStruct((tall, base.shape[1]), F32)]
    shapes += [jax.ShapeDtypeStruct((tall, base.shape[1]), BF)] * (parts - 1)
    return pl.pallas_call(
        functools.partial(fold_kernel, parts),
        out_shape=tuple(shapes),
        in_specs=[pl.BlockSpec(memory_space=pltpu.SMEM)] + [vmem] * (1 + len(gots)),
        out_specs=(vmem,) * parts,
        compiler_params=pltpu.CompilerParams(vmem_limit_bytes=60 * 1024 * 1024),
        name="fold",
    )(place, base, *gots)


def update_kernel(
    width,
    count_ref,
    heard_ref,
    shard_ref,
    sum_ref,
    table_ref,
    table_m_ref,
    table_v_ref,
    w_in_ref,
    w_in_m_ref,
    w_in_v_ref,
    w_out_ref,
    w_out_m_ref,
    w_out_v_ref,
    gain_grad_ref,
    gains_ref,
    gains_m_ref,
    gains_v_ref,
    rab_ref,
    rab_m_ref,
    rab_v_ref,
    scalars_ref,
    table_new_ref,
    table_m_new_ref,
    table_v_new_ref,
    table_low_ref,
    w_in_new_ref,
    w_in_m_new_ref,
    w_in_v_new_ref,
    w_in_low_ref,
    w_out_new_ref,
    w_out_m_new_ref,
    w_out_v_new_ref,
    w_out_low_ref,
    gains_new_ref,
    gains_m_new_ref,
    gains_v_new_ref,
    rab_new_ref,
    rab_m_new_ref,
    rab_v_new_ref,
    factor_s,
    rab_s,
):
    def update(weight_ref, first_ref, second_ref, grad, rate, outs):
        weight, first, second = adamw_update(
            weight_ref[...], first_ref[...], second_ref[...], grad, rate
        )
        outs[0][...] = weight
        outs[1][...] = first
        outs[2][...] = second
        if len(outs) > 3:
            outs[3][...] = weight.astype(BF)

    @pl.when(pl.program_id(0) == 0)
    def _():
        heard = jnp.sum(heard_ref[...], axis=0)
        for head in range(rab_s.shape[0]):
            rab_s[head : head + 1, :] = heard[
                head // 4 : head // 4 + 1, head % 4 * NB : (head % 4 + 1) * NB
            ]
        count = jnp.full((1, 1), count_ref[0].astype(F32))
        squares = jnp.sum(heard[3:4, :], axis=1, keepdims=True)
        squares = squares + jnp.sum(jnp.sum(heard[0:2, :] * heard[0:2, :], axis=1, keepdims=True), axis=0, keepdims=True)
        norm = jnp.sqrt(squares) / count
        factor = jnp.minimum(1.0, CLIP_NORM / norm) / count
        factor_s[...] = jnp.broadcast_to(factor, factor_s.shape)
        scalars_ref[...] = jnp.concatenate([jnp.broadcast_to(one, (1, 128)) for one in (heard[2:3, 0:1], count, norm)] + [jnp.zeros((5, 128), F32)], axis=0)
        update(
            w_in_ref,
            w_in_m_ref,
            w_in_v_ref,
            shard_ref[:, 0 : 4 * width] * factor,
            RATE_DENSE,
            (w_in_new_ref, w_in_m_new_ref, w_in_v_new_ref, w_in_low_ref),
        )
        update(
            w_out_ref,
            w_out_m_ref,
            w_out_v_ref,
            shard_ref[:, 4 * width : 5 * width] * factor,
            RATE_DENSE,
            (w_out_new_ref, w_out_m_new_ref, w_out_v_new_ref, w_out_low_ref),
        )
        update(
            gains_ref,
            gains_m_ref,
            gains_v_ref,
            gain_grad_ref[0:3, 0 : gains_ref.shape[1]] * factor,
            RATE_SMALL,
            (gains_new_ref, gains_m_new_ref, gains_v_new_ref),
        )
        update(
            rab_ref,
            rab_m_ref,
            rab_v_ref,
            rab_s[...] * factor,
            RATE_SMALL,
            (rab_new_ref, rab_m_new_ref, rab_v_new_ref),
        )

    update(
        table_ref,
        table_m_ref,
        table_v_ref,
        sum_ref[...] * factor_s[0:1, :],
        RATE_TABLE,
        (table_new_ref, table_m_new_ref, table_v_new_ref, table_low_ref),
    )


def update_call(count, heard, shard, table_sum, tables, w_ins, w_outs, gain_grad, gains, rabs):
    steps = 5
    rows, piece = table_sum.shape

    def whole(array):
        zeros = (0,) * len(array.shape)
        return pl.BlockSpec(array.shape, lambda step: zeros)

    def block(array):
        return pl.BlockSpec((rows // steps, piece), lambda step: (step, 0))

    operands = [heard, shard, table_sum, *tables, *w_ins, *w_outs, gain_grad, *gains, *rabs]
    specs = [pl.BlockSpec(memory_space=pltpu.SMEM)]
    specs += [block(one) if one.shape == (rows, piece) else whole(one) for one in operands]

    def like(array, kind=F32):
        return jax.ShapeDtypeStruct(array.shape, kind)

    shapes = [jax.ShapeDtypeStruct((8, 128), F32)]
    for group in (tables, w_ins, w_outs, gains, rabs):
        shapes += [like(group[0])] * 3
        if group is tables or group is w_ins or group is w_outs:
            shapes.append(like(group[0], BF))
    return pl.pallas_call(
        functools.partial(update_kernel, shard.shape[1] // 6 // 128 * 128),
        out_shape=tuple(shapes),
        grid=(steps,),
        in_specs=specs,
        out_specs=tuple(block(one) if one.shape == (rows, piece) else whole(one) for one in shapes),
        scratch_shapes=[pltpu.VMEM((8, 128), F32), pltpu.VMEM(rabs[0].shape, F32)],
        compiler_params=pltpu.CompilerParams(vmem_limit_bytes=60 * 1024 * 1024),
        name="update",
    )(count, *operands)


def bias_line(rab):
    first = jnp.broadcast_to(rab[:, :1], (rab.shape[0], 64))
    final = jnp.broadcast_to(rab[:, NB - 1 :], (rab.shape[0], 65 - NB))
    return 0.5 * jnp.concatenate([first, final, rab[:, NB - 1 : 0 : -1]], axis=1)


def adamw_update(weight, first, second, grad, rate):
    first = BETA_ONE * first + (1.0 - BETA_ONE) * grad
    second = BETA_TWO * second + (1.0 - BETA_TWO) * grad * grad
    fixed_first = first / (1.0 - BETA_ONE**STEP)
    fixed_second = second / (1.0 - BETA_TWO**STEP)
    weight = weight - rate * (
        fixed_first / (jnp.sqrt(fixed_second) + EPS_ADAM) + WEIGHT_DECAY * weight
    )
    return (weight, first, second)


def exchange(values, axes, groups=None):
    return lax.all_to_all(
        values, axes, split_axis=0, concat_axis=0, tiled=True, axis_index_groups=groups
    )


def swap_sum(values, axis, count, stride, parts):
    mine = (lax.axis_index(axis) // stride) % parts

    def part(index):
        return lax.dynamic_index_in_dim(values, index, axis=0, keepdims=False)

    total = part(mine).astype(F32)
    for offset in range(1, parts):
        pairs = []
        for place in range(count):
            spot = (place // stride) % parts
            pairs.append((place, place + ((spot ^ offset) - spot) * stride))
        got = lax.ppermute(part(mine ^ offset).astype(BF), axis, pairs)
        total = total + got.astype(F32)
    return total


def swap_parts(sends, axis, count, stride):
    gots = []
    for offset, send in enumerate(sends, 1):
        pairs = []
        for place in range(count):
            spot = place // stride
            pairs.append((place, place + ((spot ^ offset) - spot) * stride))
        gots.append(lax.ppermute(send, axis, pairs))
    return gots


def fold_dense(keep, send, col_count, row_count, blocked, between):
    columns = keep.shape[1]
    half = row_count // 2
    own = keep.shape[0] // (col_count * half)
    got = lax.ppermute(send, "row", [(place, place ^ 1) for place in range(row_count)])
    if blocked:
        total, *sends = fold_call(lax.axis_index("col").reshape(1), keep, [got], col_count)
        gots = swap_parts(sends, "col", col_count, 1)
        gots[0] = between(gots[0])
        total, *sends = fold_call((lax.axis_index("row") // 2).reshape(1), total, gots, half)
        return total, swap_parts(sends, "row", row_count, 2)
    total = (keep.astype(F32) + got.astype(F32)).reshape(col_count, half * own, columns)
    total = swap_sum(total, "col", col_count, 1, col_count)
    return swap_sum(total.reshape(half, own, columns), "row", row_count, 2, half), []


def local(
    lengths,
    items,
    negatives,
    time_buckets,
    table,
    table_m,
    table_v,
    w_in,
    w_in_m,
    w_in_v,
    w_out,
    w_out_m,
    w_out_v,
    gains,
    gains_m,
    gains_v,
    rab,
    rab_m,
    rab_v,
):
    col_count = lax.axis_size("col")
    row_count = lax.axis_size("row")
    devices = col_count * row_count
    row_place = lax.axis_index("row")
    me = lax.axis_index("col") * row_count + row_place
    rows_dev, piece = table.shape
    own, width = w_out.shape
    slots, _, seq = items.shape
    per = seq // row_count
    neg_total = negatives.shape[0]
    neg_own = neg_total // row_count
    blocked = own % 16 == 0
    own_negs = (
        lax.dynamic_slice_in_dim(negatives, row_place * neg_own, neg_own) - row_place * rows_dev
    )
    neg_rows = table[own_negs].astype(BF)
    neg_rows = neg_rows.reshape(neg_own // own, own, piece).transpose(1, 0, 2)
    dense = lax.all_gather(
        jnp.concatenate(
            [
                w_in.astype(BF),
                w_out.astype(BF),
                neg_rows.reshape(own, -1),
                jnp.pad(gains.T, ((0, 0), (0, 128 - gains.shape[0]))).astype(BF),
            ],
            axis=1,
        ),
        BOTH,
        axis=0,
        tiled=True,
    )
    if not blocked:
        neg_rows = (
            dense[:, 5 * width : 6 * width]
            .reshape(col_count, row_count, own, neg_own // own, piece)
            .transpose(1, 3, 2, 0, 4)
            .reshape(neg_total, width)
        )
        dense = jnp.concatenate([dense[:, : 5 * width], neg_rows, dense[:, 6 * width :]], axis=1)
    bias = bias_line(rab)
    mine = items[:, 0]
    key, sorted_items, sorted_times = lax.sort(
        (mine // rows_dev * seq + jnp.arange(seq)[None, :], mine, time_buckets[:, 0]),
        dimension=1,
        num_keys=1,
    )
    block = key // seq
    about = jnp.stack([sorted_items - block * rows_dev, key - block * seq, sorted_times], axis=1)
    about = about.reshape(slots, 3, row_count, per).transpose(2, 0, 1, 3)
    about = jnp.pad(about, ((0, 0), (0, 0), (0, 0), (0, 128 - per))).reshape(row_count, -1, 128)
    told = jnp.concatenate(
        [
            about,
            jnp.broadcast_to(
                jnp.pad(lengths[:, 0], (0, 128 - slots))[None, None], (row_count, 1, 128)
            ),
        ],
        axis=1,
    )
    told = jnp.broadcast_to(told[None], (col_count,) + told.shape).reshape(devices, -1, 128)
    heard = exchange(told, BOTH)
    about = heard[:, : 3 * slots].reshape(devices * slots, 3, 128)
    ids = about[:, 0]
    every_length = heard[:, 3 * slots, :slots].reshape(-1)
    total = devices * slots
    number = jnp.arange(total)
    ahead = (every_length[None, :] > every_length[:, None]) | (
        (every_length[None, :] == every_length[:, None]) & (number[None, :] < number[:, None])
    )
    rank = jnp.sum(ahead.astype(jnp.int32), axis=1)
    wanted = jnp.stack(
        [
            slot * devices + (jnp.arange(devices) if slot % 2 == 0 else devices - 1 - jnp.arange(devices))
            for slot in range(slots)
        ]
    )
    hist = jnp.sum(
        jnp.where(rank[None, None, :] == wanted[:, :, None], number[None, None, :], 0), axis=2
    )
    my_length = jnp.sum(
        jnp.where(
            rank[None, :] == lax.dynamic_slice_in_dim(wanted, me, 1, axis=1),
            every_length[None, :],
            0,
        ),
        axis=1,
    )
    sent = []
    for slot in range(slots):
        found = lookup_call(hist[slot], ids, about, table, per)
        sent.append(exchange(found, BOTH).reshape(col_count, row_count, per + 16, piece))
    core = (row_place % 2).reshape(1)
    first = history_call(my_length[0:1], sent[0], dense, bias, core, None, blocked)
    back = [exchange(first[0].reshape(devices, per, piece), BOTH)]
    final = history_call(my_length[1:2], sent[1], dense, bias, core, first[1:], blocked)
    final_rows, back[0] = lax.optimization_barrier((final[0], back[0]))
    back.append(exchange(final_rows.reshape(devices, per, piece), BOTH))
    grad_misc, keep, send = final[1:]
    if not blocked:
        packed = jnp.concatenate([keep, send], axis=0)
        neg_part = (
            packed[:, 5 * width : 6 * width]
            .reshape(row_count, neg_own // own, own, col_count, piece)
            .transpose(3, 0, 2, 1, 4)
            .reshape(width, width)
        )
        packed = jnp.concatenate(
            [packed[:, : 5 * width], neg_part, packed[:, 6 * width :]], axis=1
        ).reshape(devices // 2, 2, own, -1)
        keep = lax.dynamic_index_in_dim(packed, core[0], axis=1, keepdims=False)
        send = lax.dynamic_index_in_dim(packed, 1 - core[0], axis=1, keepdims=False)
        keep = keep.reshape(width // 2, -1)
        send = send.reshape(width // 2, -1)
    loss_count = jnp.sum(jnp.maximum(every_length - 1, 0)).reshape(1)
    table_part = scatter_call(hist[0], ids, back[0].reshape(devices * per, piece), rows_dev, per)
    base, gots = fold_dense(
        keep,
        send,
        col_count,
        row_count,
        blocked,
        lambda value: lax.optimization_barrier((value, table_part))[0],
    )
    table_sum = scatter_call(
        hist[1], ids, back[1].reshape(devices * per, piece), rows_dev, per, table_part
    )
    table_sum, shard, gain_grad, told = gather_up_call(
        own_negs, table_sum, grad_misc, base, gots, devices
    )
    heard = exchange(told, BOTH)
    scalars, *updated = update_call(
        loss_count,
        heard,
        shard,
        table_sum,
        (table, table_m, table_v),
        (w_in, w_in_m, w_in_v),
        (w_out, w_out_m, w_out_v),
        gain_grad,
        (gains, gains_m, gains_v),
        (rab, rab_m, rab_v),
    )
    return (scalars[0, 0], scalars[1, 0], scalars[2, 0], *updated)


def solution(mesh):
    placed = (
        P(None, ("col", "row")),
        P(None, ("col", "row"), None),
        P(),
        P(None, ("col", "row"), None),
        P("row", "col"),
        P("row", "col"),
        P("row", "col"),
        P(("col", "row"), None),
        P(("col", "row"), None),
        P(("col", "row"), None),
        P(("col", "row"), None),
        P(("col", "row"), None),
        P(("col", "row"), None),
        P(None, ("col", "row")),
        P(None, ("col", "row")),
        P(None, ("col", "row")),
        P(),
        P(),
        P(),
    )
    return jax.shard_map(
        local,
        mesh=mesh,
        in_specs=placed,
        out_specs=(
            P(),
            P(),
            P(),
            P("row", "col"),
            P("row", "col"),
            P("row", "col"),
            P("row", "col"),
            P(("col", "row"), None),
            P(("col", "row"), None),
            P(("col", "row"), None),
            P(("col", "row"), None),
            P(("col", "row"), None),
            P(("col", "row"), None),
            P(("col", "row"), None),
            P(("col", "row"), None),
            P(None, ("col", "row")),
            P(None, ("col", "row")),
            P(None, ("col", "row")),
            P(),
            P(),
            P(),
        ),
        check_vma=False,
    )
```

```python
import functools
import jax
import jax.numpy as jnp
from jax import lax
from jax.experimental import pallas as pl
from jax.experimental.pallas import tpu as pltpu
from jax.sharding import PartitionSpec as P

NB = 32
STEP = 10
BETA_ONE = 0.9
BETA_TWO = 0.999
EPS_ADAM = 1e-08
EPS_NORM = 1e-06
WEIGHT_DECAY = 0.01
CLIP_NORM = 0.05
RATE_TABLE = 0.06
RATE_DENSE = 0.01
RATE_SMALL = 0.5
BOTH = ("col", "row")
TILE = 256
WIDE = 4
BF = jnp.bfloat16
F32 = jnp.float32


def dot_nn(left, right):
    return lax.dot_general(left, right, (((1,), (0,)), ((), ())), preferred_element_type=F32)


def dot_nt(left, right):
    return lax.dot_general(left, right, (((1,), (1,)), ((), ())), preferred_element_type=F32)


def dot_tn(left, right):
    return lax.dot_general(left, right, (((0,), (0,)), ((), ())), preferred_element_type=F32)


def row_scale(values):
    return lax.rsqrt(jnp.mean(values * values, axis=-1, keepdims=True) + EPS_NORM)


def row_back(values, scale, grad):
    cubed = scale * scale * scale
    return scale * grad - values * (cubed * jnp.mean(grad * values, axis=-1, keepdims=True))


def silu_slope(values):
    half = 0.5 * jnp.tanh(0.5 * values)
    sigmoid = 0.5 + half
    active = values * sigmoid
    return active, sigmoid + active * (0.5 - half)


def history_kernel(last, blocked, *refs):
    if last:
        (len_ref, spot_ref, recv_ref, same_ref, other_ref, bias_ref) = refs[:6]
        (misc0_ref, big0_ref, small0_ref, gneg0_ref) = refs[6:10]
        (ge_ref, misc_ref, keep_ref, send_ref) = refs[10:14]
        (big_ref, small_ref, gneg_ref, load_sem) = refs[14:18]
        scratch = refs[18:]
    else:
        (len_ref, spot_ref, recv_ref, same_ref, other_ref, bias_ref) = refs[:6]
        (ge_ref, misc_ref, big_ref, small_ref, gneg_ref) = refs[6:11]
        scratch = refs[11:]
    (
        rows_s,
        event_s,
        normed_s,
        gatein_s,
        slope_s,
        valuem_s,
        query_s,
        keys_s,
        keyst_s,
        hot_s,
        hott_s,
        orderc_s,
        order_s,
        out_s,
        gout_s,
        ggate_s,
        dkeys_s,
        dqueryt_s,
        gslots_s,
        carry_s,
        pairs_s,
        gains_s,
        negs_s,
        bias_s,
        dense_ref,
        dense_sem,
    ) = scratch
    pieces, blocks, tall, piece = recv_ref.shape
    per = tall - 16
    seq, width = normed_s.shape
    groups = width // 128
    heads = 2 * groups
    devices = pieces * blocks
    own = width // devices
    length = len_ref[0]
    tiles = lax.div(length + (TILE - 1), TILE)
    lane = lax.broadcasted_iota(jnp.int32, (TILE, 128), 1)
    low_lanes = lane < 64
    pulls = []
    if blocked:
        for index in range(devices // 2):
            far_col, far_z = index // (blocks // 2), index % (blocks // 2)
            base = lax.bitwise_xor(spot_ref[0], far_col) * blocks
            base = base + lax.bitwise_xor(spot_ref[1], far_z) * 2
            for which, source in enumerate((same_ref, other_ref)):
                core = spot_ref[2] if which == 0 else 1 - spot_ref[2]
                target = pl.ds(pl.multiple_of((base + core) * own, own), own)
                pulls.append(
                    pltpu.make_async_copy(
                        source.at[index], dense_ref.at[target, :], dense_sem.at[2 * index + which]
                    )
                )
    else:
        pulls.append(pltpu.make_async_copy(same_ref, dense_ref, dense_sem.at[0]))
    for one in pulls:
        one.start()
    if last:
        loads = [
            pltpu.make_async_copy(big0_ref, big_ref, load_sem.at[0]),
            pltpu.make_async_copy(small0_ref, small_ref, load_sem.at[1]),
            pltpu.make_async_copy(gneg0_ref, gneg_ref, load_sem.at[2]),
        ]
        for one in loads:
            one.start()
    else:
        big_ref[...] = jnp.zeros_like(big_ref)
        small_ref[...] = jnp.zeros_like(small_ref)
        gneg_ref[...] = jnp.zeros_like(gneg_ref)

    def place(step):
        return pl.ds(pl.multiple_of(step * TILE, TILE), TILE)

    for block in range(blocks):
        span = slice(block * per, (block + 1) * per)
        for one in range(pieces):
            rows_s[span, one * piece : (one + 1) * piece] = recv_ref[one, block, 0:per, :]
        about = recv_ref[0, block, per : per + 16, :].astype(F32)
        spot = about[0:1, 0:per] * 32.0 + about[1:2, 0:per]
        order_s[0:1, span] = spot.astype(jnp.int32)
        orderc_s[span, :] = jnp.broadcast_to(about[0:1, :] * 32.0 + about[1:2, :], (128, 128)).T[0:per, :].astype(jnp.int32)
        rows_s[span, width : width + 128] = jnp.broadcast_to(about[2:3, :], (128, 128)).T[0:per, :].astype(BF)
    for one in pulls:
        one.wait()
    if blocked:
        for one in range(pieces):
            for block in range(blocks):
                source = slice((one * blocks + block) * own, (one * blocks + block + 1) * own)
                for index in range(width // piece):
                    start = (block * (width // piece) + index) * own
                    negs_s[start : start + own, one * piece : (one + 1) * piece] = dense_ref[
                        source, 5 * width + index * piece : 5 * width + (index + 1) * piece
                    ]
    else:
        negs_s[...] = dense_ref[:, 5 * width : 6 * width]
    gains_s[...] = dense_ref[:, 6 * width : 6 * width + 128].astype(F32).T[0:8, :]
    lane_half = lax.broadcasted_iota(jnp.int32, (64, 128), 1) < 64
    for head in range(heads):
        line = jnp.broadcast_to(bias_ref[head : head + 1, :], (64, 128))
        wide = pltpu.roll(line, 0, 1, stride=1, stride_axis=0)
        again = pltpu.roll(wide, 64, 1)
        whole = jnp.where(lane_half, wide, again)
        upper = whole.astype(BF)
        lower = (whole - upper.astype(F32)).astype(BF)
        bias_s[0:64, head * 128 : (head + 1) * 128] = jnp.where(lane_half, upper, lower)
    bias_s[64:128, :] = jnp.zeros((64, heads * 128), BF)
    misc_ref[...] = misc0_ref[...] if last else jnp.zeros_like(misc_ref)
    gslots_s[...] = jnp.zeros_like(gslots_s)
    carry_s[...] = jnp.zeros_like(carry_s)
    pairs_s[...] = jnp.zeros_like(pairs_s)
    gain_in = gains_s[0:1, :]
    gain_mid = gains_s[1:2, :]
    gain_out = gains_s[2:3, :]

    def project(step, _):
        span = place(step)
        hot = jnp.where(
            order_s[0:1, :] == lax.broadcasted_iota(jnp.int32, (TILE, seq), 0) + step * TILE,
            1.0,
            0.0,
        ).astype(BF)
        wide = dot_nn(hot, rows_s[...])
        event = wide[:, 0:width]
        times = wide[:, width : width + 128].astype(jnp.int32)
        bucket = jnp.where(times == jnp.bitwise_and(lane, 63), 1.0, 0.0).astype(BF)
        hot_s[span, :] = bucket
        hott_s[:, span] = jnp.where(times == 63 - lane, 1.0, 0.0).T[0:64, :].astype(BF)
        event_s[span, :] = event.astype(BF)
        normed = (event * row_scale(event) * gain_in).astype(BF)
        normed_s[span, :] = normed
        gatein_s[span, :] = dot_nn(normed, dense_ref[:, 0:width])
        active, slope = silu_slope(dot_nn(normed, dense_ref[:, width : 2 * width]))
        slope_s[0, span, :] = slope.astype(BF)
        scaled = active.astype(BF) * BF(1.0 / seq)
        for group in range(groups):
            part = scaled[:, group * 128 : (group + 1) * 128]
            valuem_s[2 * group, span, :] = jnp.where(low_lanes, part, BF(0))
            valuem_s[2 * group + 1, span, :] = jnp.where(low_lanes, BF(0), part)
        active, slope = silu_slope(dot_nn(normed, dense_ref[:, 2 * width : 3 * width]))
        slope_s[1, span, :] = slope.astype(BF)
        scaled = active.astype(BF) * BF(0.25)
        bias = dot_nn(bucket, bias_s[...]).astype(BF)
        for group in range(groups):
            part = scaled[:, group * 128 : (group + 1) * 128]
            query_s[2 * group, span, 0:128] = jnp.where(low_lanes, part, BF(0))
            query_s[2 * group + 1, span, 0:128] = jnp.where(low_lanes, BF(0), part)
            query_s[2 * group, span, 128:256] = bias[:, group * 256 : group * 256 + 128]
            query_s[2 * group + 1, span, 128:256] = bias[:, group * 256 + 128 : group * 256 + 256]
        active, slope = silu_slope(dot_nn(normed, dense_ref[:, 3 * width : 4 * width]))
        slope_s[2, span, :] = slope.astype(BF)
        scaled = active.astype(BF)
        for group in range(groups):
            part = scaled[:, group * 128 : (group + 1) * 128]
            keys_s[group, span, 0:128] = part
            keys_s[group, span, 128:256] = bucket
            turned = part.T
            keyst_s[2 * group, :, span] = turned[0:64, :]
            keyst_s[2 * group + 1, :, span] = turned[64:128, :]
        for head in range(heads):
            dkeys_s[head, span, :] = jnp.zeros((TILE, 256), F32)
            dqueryt_s[head, :, span] = jnp.zeros((64, TILE), F32)
        return 0

    lax.fori_loop(0, tiles, project, 0)

    square_row = lax.broadcasted_iota(jnp.int32, (TILE, TILE), 0)
    square_col = lax.broadcasted_iota(jnp.int32, (TILE, TILE), 1)

    def attend_tile(step, _):
        span = place(step)

        def attend(other, masked):
            near = place(other)

            def attend_heads(base, _):
                for extra in range(WIDE):
                    group = base * WIDE + extra
                    total = None
                    for half in range(2):
                        head = 2 * group + half
                        scores = dot_nt(query_s[head, span, :], keys_s[group, near, :])
                        weight = scores + scores * jnp.tanh(scores)
                        if masked:
                            weight = jnp.where(square_col <= square_row, weight, 0.0)
                        part = dot_nn(weight.astype(BF), valuem_s[head, near, :])
                        total = part if total is None else total + part
                    if masked:
                        out_s[group, span, :] = total
                    else:
                        out_s[group, span, :] += total
                return 0

            lax.fori_loop(0, groups // WIDE, attend_heads, 0)

        attend(step, True)

        def before(other, _):
            attend(other, False)
            return 0

        lax.fori_loop(0, step, before, 0)
        return 0

    lax.fori_loop(0, tiles, attend_tile, 0)

    if last:
        for one in loads:
            one.wait()

    def middle(step, _):
        span = place(step)
        event = event_s[span, :].astype(F32)
        merged = jnp.concatenate([out_s[group, span, :] for group in range(groups)], axis=1)
        for group in range(groups):
            out_s[group, span, :] = jnp.zeros((TILE, 128), F32)
        scale_mid = row_scale(merged)
        normed_mid = merged * scale_mid
        gate, gate_slope = silu_slope(gatein_s[span, :])
        mixed = (normed_mid * gain_mid * gate).astype(BF)
        hidden = event + dot_nn(mixed, dense_ref[:, 4 * width : 5 * width])
        scale_out = row_scale(hidden)
        final = (hidden * scale_out * gain_out).astype(BF)
        final_f = final.astype(F32)
        following = event_s[pl.ds(pl.multiple_of((step + 1) * TILE, TILE), 16), :][0:1, :].astype(F32)
        following = jnp.where(step + 1 < tiles, following, 0.0)
        row_id = lax.broadcasted_iota(jnp.int32, (TILE, width), 0)
        target = jnp.where(
            row_id == TILE - 1, following, pltpu.roll(event, TILE - 1, 0)
        )
        positive = jnp.sum(final_f * target, axis=-1, keepdims=True)
        negative = dot_nt(final, negs_s[...])
        highest = jnp.maximum(jnp.max(negative, axis=-1, keepdims=True), positive)
        neg_exp = jnp.exp(negative - highest)
        pos_exp = jnp.exp(positive - highest)
        totals = pos_exp + jnp.sum(neg_exp, axis=-1, keepdims=True)
        counted = (
            lax.broadcasted_iota(jnp.int32, (TILE, 1), 0) + step * TILE < length - 1
        )
        losses = jnp.where(counted, highest + jnp.log(totals) - positive, 0.0)
        misc_ref[3:4, :] += jnp.broadcast_to(jnp.sum(losses, axis=0, keepdims=True), (1, width))
        share = jnp.where(counted, 1.0 / totals, 0.0)
        grad_neg = (neg_exp * share).astype(BF)
        grad_pos = jnp.where(counted, pos_exp * share - 1.0, 0.0)
        grad_final = dot_nn(grad_neg, negs_s[...]) + grad_pos * target
        gneg_ref[...] += dot_tn(grad_neg, final)
        pushed = grad_pos * final_f
        grad_event = jnp.where(row_id == 0, carry_s[0:1, :], pltpu.roll(pushed, 1, 0))
        carry_s[0:1, :] = pushed[TILE - 1 : TILE, :]
        misc_ref[2:3, :] += jnp.sum(grad_final * hidden * scale_out, axis=0, keepdims=True)
        grad_hidden = row_back(hidden, scale_out, grad_final * gain_out)
        gatein_s[span, :] = grad_event + grad_hidden
        branch = grad_hidden.astype(BF)
        small_ref[...] += dot_tn(mixed, branch)
        grad_mixed = dot_nt(branch, dense_ref[:, 4 * width : 5 * width])
        gated = grad_mixed * gate
        misc_ref[1:2, :] += jnp.sum(gated * normed_mid, axis=0, keepdims=True)
        ggate_s[span, :] = (grad_mixed * normed_mid * gain_mid * gate_slope).astype(BF)
        grad_out = row_back(merged, scale_mid, gated * gain_mid).astype(BF) * BF(0.5)
        for group in range(groups):
            part = grad_out[:, group * 128 : (group + 1) * 128]
            gout_s[2 * group, span, :] = jnp.where(low_lanes, part, BF(0))
            gout_s[2 * group + 1, span, :] = jnp.where(low_lanes, BF(0), part)
        return 0

    lax.fori_loop(0, tiles, middle, 0)

    def retreat_tile(step, _):
        near = place(step)

        def retreat(other, masked):
            span = place(other)

            def retreat_heads(base, _):
                for extra in range(WIDE):
                    group = base * WIDE + extra
                    keys = keys_s[group, near, :]
                    total = None
                    for half in range(2):
                        head = 2 * group + half
                        gout = gout_s[head, span, :]
                        query = query_s[head, span, :]
                        scores = dot_nt(keys, query)
                        grads = dot_nt(valuem_s[head, near, :], gout)
                        bent = 1.0 + jnp.tanh(scores)
                        weight = scores * bent
                        slope = bent * ((1.0 + (scores + scores)) - weight)
                        grads = grads * slope
                        if masked:
                            visible = square_row <= square_col
                            weight = jnp.where(visible, weight, 0.0)
                            grads = jnp.where(visible, grads, 0.0)
                        grads = grads.astype(BF)
                        part = dot_nn(weight.astype(BF), gout)
                        total = part if total is None else total + part
                        dkeys_s[head, near, :] += dot_nn(
                            grads, jnp.concatenate([query[:, 0:128], hot_s[span, :]], axis=1)
                        )
                        dqueryt_s[head, :, span] += dot_nn(keyst_s[head, :, near], grads)
                    out_s[group, near, :] += total
                return 0

            lax.fori_loop(0, groups // WIDE, retreat_heads, 0)

        retreat(step, True)

        def after(other, _):
            retreat(other, False)
            return 0

        lax.fori_loop(step + 1, tiles, after, 0)
        return 0

    lax.fori_loop(0, tiles, retreat_tile, 0)

    def finish(step, _):
        span = place(step)
        normed = normed_s[span, :]
        parts = [ggate_s[span, :]]
        grad = jnp.concatenate([out_s[group, span, :] for group in range(groups)], axis=1)
        parts.append((grad * (2.0 / seq) * slope_s[0, span, :].astype(F32)).astype(BF))
        grad = jnp.concatenate(
            [
                jnp.concatenate([dqueryt_s[2 * group, :, span], dqueryt_s[2 * group + 1, :, span]], axis=0).T
                for group in range(groups)
            ],
            axis=1,
        )
        parts.append((grad * 0.5 * slope_s[1, span, :].astype(F32)).astype(BF))
        grad = jnp.concatenate(
            [
                dkeys_s[2 * group, span, 0:128] + dkeys_s[2 * group + 1, span, 0:128]
                for group in range(groups)
            ],
            axis=1,
        )
        parts.append((grad * 2.0 * slope_s[2, span, :].astype(F32)).astype(BF))
        grad_normed = None
        for index in range(4):
            columns = slice(index * width, (index + 1) * width)
            big_ref[:, columns] += dot_tn(normed, parts[index])
            part = dot_nt(parts[index], dense_ref[:, columns])
            grad_normed = part if grad_normed is None else grad_normed + part
        hott = hott_s[:, span]
        for head in range(heads):
            wide = dkeys_s[head, span, 128:256]
            upper = wide.astype(BF)
            lower = (wide - upper.astype(F32)).astype(BF)
            pairs_s[head] += dot_nn(hott, upper) + dot_nn(hott, lower)
        event = event_s[span, :].astype(F32)
        scale = row_scale(event)
        misc_ref[0:1, :] += jnp.sum(grad_normed * event * scale, axis=0, keepdims=True)
        total = gatein_s[span, :] + row_back(event, scale, grad_normed * gain_in)
        column = orderc_s[...]
        hot = jnp.where(
            jnp.concatenate([column] * (TILE // 128), axis=1)
            == lax.broadcasted_iota(jnp.int32, (seq, TILE), 1) + step * TILE,
            1.0,
            0.0,
        ).astype(BF)
        gslots_s[...] += dot_nn(hot, total.astype(BF))
        return 0

    lax.fori_loop(0, tiles, finish, 0)

    for block in range(blocks):
        span = slice(block * per, (block + 1) * per)
        for one in range(pieces):
            ge_ref[one, block] = gslots_s[span, one * piece : (one + 1) * piece].astype(BF)
    lane_row = lax.broadcasted_iota(jnp.int32, (64, 128), 1)
    for head in range(heads):
        kept = jnp.where(lane_row < 64, pairs_s[head], 0.0)
        turned = pltpu.roll(kept, 0, 1, stride=1, stride_axis=0)
        misc_ref[8 + head : 9 + head, 0:128] += jnp.sum(turned, axis=0, keepdims=True)
    if last:
        kept = jnp.where(lax.broadcasted_iota(jnp.int32, (8, width), 0) < 3, misc_ref[0:8, :], 0.0)
        gain_rows = jnp.concatenate([kept, jnp.zeros((120, width), F32)], axis=0)
        gain_rows = gain_rows.T.astype(BF)

        def pack(out_ref, target, source, one, block):
            out_ref[target, 0 : 4 * width] = big_ref[source, :].astype(BF)
            out_ref[target, 4 * width : 5 * width] = small_ref[source, :].astype(BF)
            if blocked:
                for index in range(width // piece):
                    start = (block * (width // piece) + index) * own
                    out_ref[target, 5 * width + index * piece : 5 * width + (index + 1) * piece] = gneg_ref[
                        start : start + own, one * piece : (one + 1) * piece
                    ].astype(BF)
            else:
                out_ref[target, 5 * width : 6 * width] = gneg_ref[source, :].astype(BF)
            out_ref[target, 6 * width : 6 * width + 128] = gain_rows[source, :]

        if blocked:
            for core in range(2):

                @pl.when(spot_ref[2] == core)
                def _(core=core):
                    for device in range(devices):
                        one, block = device // blocks, device % blocks
                        source = slice(device * own, (device + 1) * own)
                        target = slice(device // 2 * own, (device // 2 + 1) * own)
                        pack(keep_ref if device % 2 == core else send_ref, target, source, one, block)

        else:
            half = width // 2
            pack(keep_ref, slice(0, half), slice(0, half), 0, 0)
            pack(send_ref, slice(0, half), slice(half, width), 0, 0)


def history_call(length, spot, recv, same, other, bias, before, blocked):
    last = before is not None
    pieces, blocks, tall, piece = recv.shape
    per = tall - 16
    seq = blocks * per
    width = pieces * piece
    heads = width // 64
    groups = heads // 2
    neg_total = width
    vmem = pl.BlockSpec(memory_space=pltpu.VMEM)
    smem = pl.BlockSpec(memory_space=pltpu.SMEM)
    anywhere = pl.BlockSpec(memory_space=pl.ANY)
    shapes = [
        jax.ShapeDtypeStruct((pieces, blocks, per, piece), BF),
        jax.ShapeDtypeStruct((16, width), F32),
    ]
    sums = [(width, 4 * width), (width, width), (neg_total, width)]
    operands = (length, spot, recv, same, other, bias)
    specs = [smem, smem, vmem, anywhere, anywhere, vmem]
    if last:
        operands += tuple(before)
        specs += [vmem, anywhere, anywhere, anywhere]
        shapes += [jax.ShapeDtypeStruct((width // 2, 6 * width + 128), BF)] * 2
        extra = [pltpu.VMEM(one, F32) for one in sums] + [pltpu.SemaphoreType.DMA((3,))]
    else:
        shapes += [jax.ShapeDtypeStruct(one, F32) for one in sums]
        extra = []
    return pl.pallas_call(
        functools.partial(history_kernel, last, blocked),
        out_shape=tuple(shapes),
        in_specs=specs,
        out_specs=(vmem,) * len(shapes),
        scratch_shapes=extra
        + [
            pltpu.VMEM((seq, width + 128), BF),
            pltpu.VMEM((seq + TILE, width), BF),
            pltpu.VMEM((seq, width), BF),
            pltpu.VMEM((seq, width), F32),
            pltpu.VMEM((3, seq, width), BF),
            pltpu.VMEM((heads, seq, 128), BF),
            pltpu.VMEM((heads, seq, 256), BF),
            pltpu.VMEM((groups, seq, 256), BF),
            pltpu.VMEM((heads, 64, seq), BF),
            pltpu.VMEM((seq, 128), BF),
            pltpu.VMEM((64, seq), BF),
            pltpu.VMEM((seq, 128), jnp.int32),
            pltpu.VMEM((8, seq), jnp.int32),
            pltpu.VMEM((groups, seq, 128), F32),
            pltpu.VMEM((heads, seq, 128), BF),
            pltpu.VMEM((seq, width), BF),
            pltpu.VMEM((heads, seq, 256), F32),
            pltpu.VMEM((heads, 64, seq), F32),
            pltpu.VMEM((seq, width), F32),
            pltpu.VMEM((8, width), F32),
            pltpu.VMEM((heads, 64, 128), F32),
            pltpu.VMEM((8, width), F32),
            pltpu.VMEM((neg_total, width), BF),
            pltpu.VMEM((128, heads * 128), BF),
            pltpu.VMEM((width, same.shape[-1]), BF),
            pltpu.SemaphoreType.DMA((pieces * blocks,)),
        ],
        compiler_params=pltpu.CompilerParams(vmem_limit_bytes=60 * 1024 * 1024),
        cost_estimate=pl.CostEstimate(
            flops=40_000_000_000, bytes_accessed=20_000_000, transcendentals=10_000_000
        ),
        name="history_last" if last else "history_first",
    )(*operands)


def prepare_kernel(
    rows_dev,
    col_count,
    len_ref,
    spots_ref,
    items_ref,
    times_ref,
    table_ref,
    w_in_ref,
    w_out_ref,
    gains_ref,
    told_ref,
    payload_ref,
    stage_s,
):
    slots, seq = items_ref.shape
    own, width = w_out_ref.shape
    blocks = told_ref.shape[0] // col_count
    per = seq // blocks
    payload_ref[:, 0 : 4 * width] = w_in_ref[...].astype(BF)
    payload_ref[:, 4 * width : 5 * width] = w_out_ref[...].astype(BF)
    for index in range(spots_ref.shape[0]):
        stage_s[index : index + 1, :] = table_ref[pl.ds(spots_ref[index], 1), :]
    for index in range(spots_ref.shape[0] // own):
        payload_ref[:, 5 * width + index * 128 : 5 * width + (index + 1) * 128] = stage_s[
            index * own : (index + 1) * own, :
        ].astype(BF)
    square = jnp.zeros((128, 128), F32)
    stage_s[...] = jnp.zeros_like(stage_s)
    stage_s[0 : gains_ref.shape[0], 0:own] = gains_ref[...]
    square = stage_s[0:128, :].T
    payload_ref[:, 6 * width : 6 * width + 128] = square[0:own, :].astype(BF)
    before = jnp.where(
        lax.broadcasted_iota(jnp.int32, (128, 128), 0) < lax.broadcasted_iota(jnp.int32, (128, 128), 1),
        1.0,
        0.0,
    ).astype(BF)
    block_row = lax.broadcasted_iota(jnp.int32, (blocks, seq), 0)
    time = lax.broadcasted_iota(jnp.int32, (1, seq), 1)
    lane = lax.broadcasted_iota(jnp.int32, (1, 128), 1)
    lengths = jnp.zeros((1, 128), jnp.int32)
    for slot in range(slots):
        lengths = jnp.where(lane == slot, len_ref[slot], lengths)
        item = items_ref[slot : slot + 1, :]
        block = jnp.zeros((1, seq), jnp.int32)
        for index in range(1, blocks):
            block = block + jnp.where(item >= index * rows_dev, 1, 0)
        place = item - block * rows_dev
        member = jnp.where(block_row == block, 1.0, 0.0)
        counts = []
        running = jnp.zeros((blocks, 1), F32)
        for part in range(seq // 128):
            piece = member[:, part * 128 : (part + 1) * 128]
            counts.append(dot_nn(piece.astype(BF), before) + running)
            running = running + jnp.sum(piece, axis=1, keepdims=True)
        rank = jnp.sum(member * jnp.concatenate(counts, axis=1), axis=0, keepdims=True)
        target = block * per + rank.astype(jnp.int32)
        upper = lax.shift_right_logical(place, 6)
        late = lax.shift_right_logical(time, 5)
        values = [upper, place - upper * 64, late, time - late * 32, times_ref[slot : slot + 1, :]]
        values = jnp.concatenate(values + [jnp.zeros((11, seq), jnp.int32)], axis=0)
        values = values.astype(F32).astype(BF)
        for index in range(seq // 256):
            span = slice(index * 256, (index + 1) * 256)
            hot = jnp.where(
                lax.broadcasted_iota(jnp.int32, (256, seq), 0) + index * 256 == target, 1.0, 0.0
            ).astype(BF)
            moved = dot_nt(values, hot).astype(jnp.int32)
            rows = [moved[0:1] * 64 + moved[1:2], moved[2:3] * 32 + moved[3:4], moved[4:5]]
            for inner in range(256 // per):
                cut = slice(inner * per, (inner + 1) * per)
                row = jnp.concatenate([one[:, cut] for one in rows], axis=0)
                if per < 128:
                    row = jnp.concatenate([row, jnp.zeros((3, 128 - per), jnp.int32)], axis=1)
                for one in range(col_count):
                    told_ref[one * blocks + index * (256 // per) + inner, 3 * slot : 3 * slot + 3, :] = row
    for index in range(told_ref.shape[0]):
        told_ref[index, 3 * slots : 3 * slots + 1, :] = lengths


def prepare_call(lengths, spots, items, times, table, w_in, w_out, gains, devices, col_count):
    slots = items.shape[0]
    own, width = w_out.shape
    smem = pl.BlockSpec(memory_space=pltpu.SMEM)
    vmem = pl.BlockSpec(memory_space=pltpu.VMEM)
    return pl.pallas_call(
        functools.partial(prepare_kernel, table.shape[0], col_count),
        out_shape=(
            jax.ShapeDtypeStruct((devices, 3 * slots + 1, 128), jnp.int32),
            jax.ShapeDtypeStruct((own, 6 * width + 128), BF),
        ),
        in_specs=[smem, smem] + [vmem] * 6,
        out_specs=(vmem, vmem),
        scratch_shapes=[pltpu.VMEM((128, 128), F32)],
        compiler_params=pltpu.CompilerParams(vmem_limit_bytes=60 * 1024 * 1024),
        name="prepare",
    )(lengths, spots, items, times, table, w_in, w_out, gains)


def lookup_kernel(hist_ref, ids_ref, about_ref, table_ref, found_ref, stage_s):
    count, tall, piece = found_ref.shape
    per = tall - 16

    def one(place, _):
        number = hist_ref[place]
        for index in range(per):
            stage_s[index : index + 1, :] = table_ref[pl.ds(ids_ref[number, index], 1), :]
        found_ref[place, 0:per, :] = stage_s[...].astype(BF)
        spot = about_ref[number, 1:2, :]
        upper = lax.shift_right_logical(spot, 5)
        rows = [upper, spot - upper * 32, about_ref[number, 2:3, :], jnp.zeros((13, piece), jnp.int32)]
        found_ref[place, per:tall, :] = jnp.concatenate(rows, axis=0).astype(F32).astype(BF)
        return 0

    lax.fori_loop(0, count, one, 0)


def lookup_call(hist, ids, about, table, per):
    count = hist.shape[0]
    smem = pl.BlockSpec(memory_space=pltpu.SMEM)
    vmem = pl.BlockSpec(memory_space=pltpu.VMEM)
    return pl.pallas_call(
        lookup_kernel,
        out_shape=jax.ShapeDtypeStruct((count, per + 16, table.shape[1]), BF),
        in_specs=[smem, smem, vmem, vmem],
        out_specs=vmem,
        scratch_shapes=[pltpu.VMEM((per, table.shape[1]), F32)],
        compiler_params=pltpu.CompilerParams(vmem_limit_bytes=60 * 1024 * 1024),
        cost_estimate=pl.CostEstimate(
            flops=5_000_000_000, bytes_accessed=4_000_000, transcendentals=0
        ),
        name="lookup",
    )(hist, ids, about, table)


def add_rows(hist_ref, ids_ref, grads_ref, stage_s, sums):
    count = hist_ref.shape[0]
    per = stage_s.shape[0]
    for held in sums:
        held[...] = jnp.zeros_like(held)

    def one(place, _):
        number = hist_ref[place]
        stage_s[...] = grads_ref[pl.ds(pl.multiple_of(place * per, per), per), :].astype(F32)
        for index in range(per):
            held = sums[index % len(sums)]
            spot = pl.ds(ids_ref[number, index], 1)
            held[spot, :] = held[spot, :] + stage_s[index : index + 1, :]
        return 0

    lax.fori_loop(0, count, one, 0)


def scatter_kernel(hist_ref, ids_ref, grads_ref, *refs):
    total_ref, stage_s = refs[-6:-4]
    add_rows(hist_ref, ids_ref, grads_ref, stage_s, refs[-4:])
    total = refs[-4][...]
    for held in refs[-3:]:
        total = total + held[...]
    for init_ref in refs[:-6]:
        total = total + init_ref[...]
    total_ref[...] = total


def scatter_call(hist, ids, grads, rows, per, *init):
    smem = pl.BlockSpec(memory_space=pltpu.SMEM)
    vmem = pl.BlockSpec(memory_space=pltpu.VMEM)
    piece = grads.shape[1]
    return pl.pallas_call(
        scatter_kernel,
        out_shape=jax.ShapeDtypeStruct((rows, piece), F32),
        in_specs=[smem, smem, vmem] + [vmem] * len(init),
        out_specs=vmem,
        scratch_shapes=[pltpu.VMEM((per, piece), F32)] + [pltpu.VMEM((rows, piece), F32)] * 4,
        compiler_params=pltpu.CompilerParams(vmem_limit_bytes=60 * 1024 * 1024),
        cost_estimate=pl.CostEstimate(
            flops=6_000_000_000, bytes_accessed=4_000_000, transcendentals=0
        ),
        name="scatter",
    )(hist, ids, grads, *init)


def gather_up_kernel(width, spots_ref, table_ref, misc_ref, base_ref, *refs):
    total_ref, shard_ref, gain_ref, told_ref = refs[-4:]
    shard = base_ref[...]
    for got in refs[:-4]:
        shard = shard + got[...].astype(F32)
    shard_ref[...] = shard
    own = shard.shape[0]
    total_ref[...] = table_ref[...]
    for index in range(spots_ref.shape[0]):
        spot = pl.ds(spots_ref[index], 1)
        row = index % own
        start = 5 * width + index // own * 128
        total_ref[spot, :] = total_ref[spot, :] + shard_ref[row : row + 1, start : start + 128]
    total = total_ref[...]
    squares = jnp.sum(total * total, axis=0, keepdims=True)
    for index in range(5 * width // 128):
        part = shard_ref[:, index * 128 : (index + 1) * 128]
        squares = squares + jnp.sum(part * part, axis=0, keepdims=True)
    part = shard_ref[:, 6 * width : 6 * width + 128]
    squares = squares + jnp.sum(part * part, axis=0, keepdims=True)
    turned = jnp.concatenate([part, jnp.zeros((128 - own, 128), F32)], axis=0).T
    gain_ref[...] = turned[0:8, :]
    spread = misc_ref[8:16, 0:128]
    lane = lax.broadcasted_iota(jnp.int32, (8, 128), 1)
    low = jnp.sum(jnp.where(lane < 63, spread, 0.0), axis=1, keepdims=True)
    high = jnp.sum(jnp.where(lane >= 62 + NB, spread, 0.0), axis=1, keepdims=True)
    folded = jnp.where(lane < NB - 1, pltpu.roll(spread, 65, 1), 0.0)
    folded = folded + jnp.where(lane == 0, low, 0.0) + jnp.where(lane == NB - 1, high, 0.0)
    rows = []
    for half in range(2):
        row = folded[4 * half : 4 * half + 1, :]
        for index in range(1, 4):
            row = row + pltpu.roll(folded[4 * half + index : 4 * half + index + 1, :], NB * index, 1)
        rows.append(row)
    rows += [misc_ref[3:4, 0:128], squares]
    told_ref[...] = jnp.broadcast_to(jnp.concatenate(rows, axis=0)[None], told_ref.shape)


def gather_up_call(spots, table_sum, misc, base, gots, devices):
    vmem = pl.BlockSpec(memory_space=pltpu.VMEM)
    return pl.pallas_call(
        functools.partial(gather_up_kernel, misc.shape[1]),
        out_shape=(
            jax.ShapeDtypeStruct(table_sum.shape, F32),
            jax.ShapeDtypeStruct(base.shape, F32),
            jax.ShapeDtypeStruct((8, 128), F32),
            jax.ShapeDtypeStruct((devices, 4, 128), F32),
        ),
        in_specs=[pl.BlockSpec(memory_space=pltpu.SMEM)] + [vmem] * (3 + len(gots)),
        out_specs=(vmem,) * 4,
        compiler_params=pltpu.CompilerParams(vmem_limit_bytes=60 * 1024 * 1024),
        name="gather_up",
    )(spots, table_sum, misc, base, *gots)


def fold_kernel(parts, place_ref, base_ref, *refs):
    gots = refs[: len(refs) - parts]
    own_ref = refs[len(refs) - parts]
    sends = refs[len(refs) - parts + 1 :]
    tall = own_ref.shape[0]
    for offset in range(parts):
        span = pl.ds(pl.multiple_of(lax.bitwise_xor(place_ref[0], offset) * tall, tall), tall)
        total = base_ref[span, :].astype(F32)
        for got in gots:
            total = total + got[span, :].astype(F32)
        if offset == 0:
            own_ref[...] = total
        else:
            sends[offset - 1][...] = total.astype(BF)


def fold_call(place, base, gots, parts):
    tall = base.shape[0] // parts
    vmem = pl.BlockSpec(memory_space=pltpu.VMEM)
    shapes = [jax.ShapeDtypeStruct((tall, base.shape[1]), F32)]
    shapes += [jax.ShapeDtypeStruct((tall, base.shape[1]), BF)] * (parts - 1)
    return pl.pallas_call(
        functools.partial(fold_kernel, parts),
        out_shape=tuple(shapes),
        in_specs=[pl.BlockSpec(memory_space=pltpu.SMEM)] + [vmem] * (1 + len(gots)),
        out_specs=(vmem,) * parts,
        compiler_params=pltpu.CompilerParams(vmem_limit_bytes=60 * 1024 * 1024),
        name="fold",
    )(place, base, *gots)


def update_kernel(
    width,
    count_ref,
    heard_ref,
    shard_ref,
    sum_ref,
    table_ref,
    table_m_ref,
    table_v_ref,
    w_in_ref,
    w_in_m_ref,
    w_in_v_ref,
    w_out_ref,
    w_out_m_ref,
    w_out_v_ref,
    gain_grad_ref,
    gains_ref,
    gains_m_ref,
    gains_v_ref,
    rab_ref,
    rab_m_ref,
    rab_v_ref,
    scalars_ref,
    table_new_ref,
    table_m_new_ref,
    table_v_new_ref,
    table_low_ref,
    w_in_new_ref,
    w_in_m_new_ref,
    w_in_v_new_ref,
    w_in_low_ref,
    w_out_new_ref,
    w_out_m_new_ref,
    w_out_v_new_ref,
    w_out_low_ref,
    gains_new_ref,
    gains_m_new_ref,
    gains_v_new_ref,
    rab_new_ref,
    rab_m_new_ref,
    rab_v_new_ref,
    factor_s,
    rab_s,
):
    def update(weight_ref, first_ref, second_ref, grad, rate, outs):
        weight, first, second = adamw_update(
            weight_ref[...], first_ref[...], second_ref[...], grad, rate
        )
        outs[0][...] = weight
        outs[1][...] = first
        outs[2][...] = second
        if len(outs) > 3:
            outs[3][...] = weight.astype(BF)

    @pl.when(pl.program_id(0) == 0)
    def _():
        heard = jnp.sum(heard_ref[...], axis=0)
        for head in range(rab_s.shape[0]):
            rab_s[head : head + 1, :] = heard[
                head // 4 : head // 4 + 1, head % 4 * NB : (head % 4 + 1) * NB
            ]
        count = jnp.full((1, 1), count_ref[0].astype(F32))
        squares = jnp.sum(heard[3:4, :], axis=1, keepdims=True)
        squares = squares + jnp.sum(jnp.sum(heard[0:2, :] * heard[0:2, :], axis=1, keepdims=True), axis=0, keepdims=True)
        norm = jnp.sqrt(squares) / count
        factor = jnp.minimum(1.0, CLIP_NORM / norm) / count
        factor_s[...] = jnp.broadcast_to(factor, factor_s.shape)
        scalars_ref[...] = jnp.concatenate([jnp.broadcast_to(one, (1, 128)) for one in (heard[2:3, 0:1], count, norm)] + [jnp.zeros((5, 128), F32)], axis=0)
        update(
            w_in_ref,
            w_in_m_ref,
            w_in_v_ref,
            shard_ref[:, 0 : 4 * width] * factor,
            RATE_DENSE,
            (w_in_new_ref, w_in_m_new_ref, w_in_v_new_ref, w_in_low_ref),
        )
        update(
            w_out_ref,
            w_out_m_ref,
            w_out_v_ref,
            shard_ref[:, 4 * width : 5 * width] * factor,
            RATE_DENSE,
            (w_out_new_ref, w_out_m_new_ref, w_out_v_new_ref, w_out_low_ref),
        )
        update(
            gains_ref,
            gains_m_ref,
            gains_v_ref,
            gain_grad_ref[0:3, 0 : gains_ref.shape[1]] * factor,
            RATE_SMALL,
            (gains_new_ref, gains_m_new_ref, gains_v_new_ref),
        )
        update(
            rab_ref,
            rab_m_ref,
            rab_v_ref,
            rab_s[...] * factor,
            RATE_SMALL,
            (rab_new_ref, rab_m_new_ref, rab_v_new_ref),
        )

    update(
        table_ref,
        table_m_ref,
        table_v_ref,
        sum_ref[...] * factor_s[0:1, :],
        RATE_TABLE,
        (table_new_ref, table_m_new_ref, table_v_new_ref, table_low_ref),
    )


def update_call(count, heard, shard, table_sum, tables, w_ins, w_outs, gain_grad, gains, rabs):
    steps = 5
    rows, piece = table_sum.shape

    def whole(array):
        zeros = (0,) * len(array.shape)
        return pl.BlockSpec(array.shape, lambda step: zeros)

    def block(array):
        return pl.BlockSpec((rows // steps, piece), lambda step: (step, 0))

    operands = [heard, shard, table_sum, *tables, *w_ins, *w_outs, gain_grad, *gains, *rabs]
    specs = [pl.BlockSpec(memory_space=pltpu.SMEM)]
    specs += [block(one) if one.shape == (rows, piece) else whole(one) for one in operands]

    def like(array, kind=F32):
        return jax.ShapeDtypeStruct(array.shape, kind)

    shapes = [jax.ShapeDtypeStruct((8, 128), F32)]
    for group in (tables, w_ins, w_outs, gains, rabs):
        shapes += [like(group[0])] * 3
        if group is tables or group is w_ins or group is w_outs:
            shapes.append(like(group[0], BF))
    return pl.pallas_call(
        functools.partial(update_kernel, shard.shape[1] // 6 // 128 * 128),
        out_shape=tuple(shapes),
        grid=(steps,),
        in_specs=specs,
        out_specs=tuple(block(one) if one.shape == (rows, piece) else whole(one) for one in shapes),
        scratch_shapes=[pltpu.VMEM((8, 128), F32), pltpu.VMEM(rabs[0].shape, F32)],
        compiler_params=pltpu.CompilerParams(vmem_limit_bytes=60 * 1024 * 1024),
        name="update",
    )(count, *operands)


def bias_line(rab):
    first = jnp.broadcast_to(rab[:, :1], (rab.shape[0], 64))
    final = jnp.broadcast_to(rab[:, NB - 1 :], (rab.shape[0], 65 - NB))
    return 0.5 * jnp.concatenate([first, final, rab[:, NB - 1 : 0 : -1]], axis=1)


def adamw_update(weight, first, second, grad, rate):
    first = BETA_ONE * first + (1.0 - BETA_ONE) * grad
    second = BETA_TWO * second + (1.0 - BETA_TWO) * grad * grad
    fixed_first = first / (1.0 - BETA_ONE**STEP)
    fixed_second = second / (1.0 - BETA_TWO**STEP)
    weight = weight - rate * (
        fixed_first / (jnp.sqrt(fixed_second) + EPS_ADAM) + WEIGHT_DECAY * weight
    )
    return (weight, first, second)


def exchange(values, axes, groups=None):
    return lax.all_to_all(
        values, axes, split_axis=0, concat_axis=0, tiled=True, axis_index_groups=groups
    )


def swap_sum(values, axis, count, stride, parts):
    mine = (lax.axis_index(axis) // stride) % parts

    def part(index):
        return lax.dynamic_index_in_dim(values, index, axis=0, keepdims=False)

    total = part(mine).astype(F32)
    for offset in range(1, parts):
        pairs = []
        for place in range(count):
            spot = (place // stride) % parts
            pairs.append((place, place + ((spot ^ offset) - spot) * stride))
        got = lax.ppermute(part(mine ^ offset).astype(BF), axis, pairs)
        total = total + got.astype(F32)
    return total


def swap_parts(sends, axis, count, stride):
    gots = []
    for offset, send in enumerate(sends, 1):
        pairs = []
        for place in range(count):
            spot = place // stride
            pairs.append((place, place + ((spot ^ offset) - spot) * stride))
        gots.append(lax.ppermute(send, axis, pairs))
    return gots


def fold_dense(keep, send, col_count, row_count, blocked, between):
    columns = keep.shape[1]
    half = row_count // 2
    own = keep.shape[0] // (col_count * half)
    got = lax.ppermute(send, "row", [(place, place ^ 1) for place in range(row_count)])
    if blocked:
        total, *sends = fold_call(lax.axis_index("col").reshape(1), keep, [got], col_count)
        gots = swap_parts(sends, "col", col_count, 1)
        gots[0] = between(gots[0])
        total, *sends = fold_call((lax.axis_index("row") // 2).reshape(1), total, gots, half)
        return total, swap_parts(sends, "row", row_count, 2)
    total = (keep.astype(F32) + got.astype(F32)).reshape(col_count, half * own, columns)
    total = swap_sum(total, "col", col_count, 1, col_count)
    return swap_sum(total.reshape(half, own, columns), "row", row_count, 2, half), []


def local(
    lengths,
    items,
    negatives,
    time_buckets,
    table,
    table_m,
    table_v,
    w_in,
    w_in_m,
    w_in_v,
    w_out,
    w_out_m,
    w_out_v,
    gains,
    gains_m,
    gains_v,
    rab,
    rab_m,
    rab_v,
):
    col_count = lax.axis_size("col")
    row_count = lax.axis_size("row")
    devices = col_count * row_count
    row_place = lax.axis_index("row")
    me = lax.axis_index("col") * row_count + row_place
    rows_dev, piece = table.shape
    own, width = w_out.shape
    slots, _, seq = items.shape
    per = seq // row_count
    neg_total = negatives.shape[0]
    neg_own = neg_total // row_count
    blocked = own % 16 == 0
    own_negs = (
        lax.dynamic_slice_in_dim(negatives, row_place * neg_own, neg_own) - row_place * rows_dev
    )
    told, payload = prepare_call(
        lengths[:, 0],
        own_negs,
        items[:, 0],
        time_buckets[:, 0],
        table,
        w_in,
        w_out,
        gains,
        devices,
        col_count,
    )
    bias = bias_line(rab)
    heard = exchange(told, BOTH)
    if blocked:
        half = row_count // 2
        same = jnp.stack([payload] + swap_parts([payload] * (half - 1), "row", row_count, 2))
        same = jnp.stack([same] + swap_parts([same] * (col_count - 1), "col", col_count, 1))
        same = same.reshape(devices // 2, own, -1)
        other = lax.ppermute(same, "row", [(place, place ^ 1) for place in range(row_count)])
    else:
        dense = lax.all_gather(payload, BOTH, axis=0, tiled=True)
        neg_rows = (
            dense[:, 5 * width : 6 * width]
            .reshape(col_count, row_count, own, neg_own // own, piece)
            .transpose(1, 3, 2, 0, 4)
            .reshape(neg_total, width)
        )
        same = jnp.concatenate([dense[:, : 5 * width], neg_rows, dense[:, 6 * width :]], axis=1)
        other = same
    about = heard[:, : 3 * slots].reshape(devices * slots, 3, 128)
    ids = about[:, 0]
    every_length = heard[:, 3 * slots, :slots].reshape(-1)
    total = devices * slots
    number = jnp.arange(total)
    ahead = (every_length[None, :] > every_length[:, None]) | (
        (every_length[None, :] == every_length[:, None]) & (number[None, :] < number[:, None])
    )
    rank = jnp.sum(ahead.astype(jnp.int32), axis=1)
    wanted = jnp.stack(
        [
            slot * devices + (jnp.arange(devices) if slot % 2 == 0 else devices - 1 - jnp.arange(devices))
            for slot in range(slots)
        ]
    )
    hist = jnp.sum(
        jnp.where(rank[None, None, :] == wanted[:, :, None], number[None, None, :], 0), axis=2
    )
    my_length = jnp.sum(
        jnp.where(
            rank[None, :] == lax.dynamic_slice_in_dim(wanted, me, 1, axis=1),
            every_length[None, :],
            0,
        ),
        axis=1,
    )
    sent = []
    for slot in range(slots):
        found = lookup_call(hist[slot], ids, about, table, per)
        sent.append(exchange(found, BOTH).reshape(col_count, row_count, per + 16, piece))
    core = (row_place % 2).reshape(1)
    spot = jnp.stack([lax.axis_index("col"), row_place // 2, row_place % 2])
    first = history_call(my_length[0:1], spot, sent[0], same, other, bias, None, blocked)
    back = [exchange(first[0].reshape(devices, per, piece), BOTH)]
    final = history_call(my_length[1:2], spot, sent[1], same, other, bias, first[1:], blocked)
    final_rows, back[0] = lax.optimization_barrier((final[0], back[0]))
    back.append(exchange(final_rows.reshape(devices, per, piece), BOTH))
    grad_misc, keep, send = final[1:]
    if not blocked:
        packed = jnp.concatenate([keep, send], axis=0)
        neg_part = (
            packed[:, 5 * width : 6 * width]
            .reshape(row_count, neg_own // own, own, col_count, piece)
            .transpose(3, 0, 2, 1, 4)
            .reshape(width, width)
        )
        packed = jnp.concatenate(
            [packed[:, : 5 * width], neg_part, packed[:, 6 * width :]], axis=1
        ).reshape(devices // 2, 2, own, -1)
        keep = lax.dynamic_index_in_dim(packed, core[0], axis=1, keepdims=False)
        send = lax.dynamic_index_in_dim(packed, 1 - core[0], axis=1, keepdims=False)
        keep = keep.reshape(width // 2, -1)
        send = send.reshape(width // 2, -1)
    loss_count = jnp.sum(jnp.maximum(every_length - 1, 0)).reshape(1)
    table_part = scatter_call(hist[0], ids, back[0].reshape(devices * per, piece), rows_dev, per)
    base, gots = fold_dense(
        keep,
        send,
        col_count,
        row_count,
        blocked,
        lambda value: lax.optimization_barrier((value, table_part))[0],
    )
    table_sum = scatter_call(
        hist[1], ids, back[1].reshape(devices * per, piece), rows_dev, per, table_part
    )
    table_sum, shard, gain_grad, told = gather_up_call(
        own_negs, table_sum, grad_misc, base, gots, devices
    )
    heard = exchange(told, BOTH)
    scalars, *updated = update_call(
        loss_count,
        heard,
        shard,
        table_sum,
        (table, table_m, table_v),
        (w_in, w_in_m, w_in_v),
        (w_out, w_out_m, w_out_v),
        gain_grad,
        (gains, gains_m, gains_v),
        (rab, rab_m, rab_v),
    )
    return (scalars[0, 0], scalars[1, 0], scalars[2, 0], *updated)


def solution(mesh):
    placed = (
        P(None, ("col", "row")),
        P(None, ("col", "row"), None),
        P(),
        P(None, ("col", "row"), None),
        P("row", "col"),
        P("row", "col"),
        P("row", "col"),
        P(("col", "row"), None),
        P(("col", "row"), None),
        P(("col", "row"), None),
        P(("col", "row"), None),
        P(("col", "row"), None),
        P(("col", "row"), None),
        P(None, ("col", "row")),
        P(None, ("col", "row")),
        P(None, ("col", "row")),
        P(),
        P(),
        P(),
    )
    return jax.shard_map(
        local,
        mesh=mesh,
        in_specs=placed,
        out_specs=(
            P(),
            P(),
            P(),
            P("row", "col"),
            P("row", "col"),
            P("row", "col"),
            P("row", "col"),
            P(("col", "row"), None),
            P(("col", "row"), None),
            P(("col", "row"), None),
            P(("col", "row"), None),
            P(("col", "row"), None),
            P(("col", "row"), None),
            P(("col", "row"), None),
            P(("col", "row"), None),
            P(None, ("col", "row")),
            P(None, ("col", "row")),
            P(None, ("col", "row")),
            P(),
            P(),
            P(),
        ),
        check_vma=False,
    )
```

```python
import functools
import jax
import jax.numpy as jnp
from jax import lax
from jax.experimental import pallas as pl
from jax.experimental.pallas import tpu as pltpu
from jax.sharding import PartitionSpec as P

NB = 32
STEP = 10
BETA_ONE = 0.9
BETA_TWO = 0.999
EPS_ADAM = 1e-08
EPS_NORM = 1e-06
WEIGHT_DECAY = 0.01
CLIP_NORM = 0.05
RATE_TABLE = 0.06
RATE_DENSE = 0.01
RATE_SMALL = 0.5
BOTH = ("col", "row")
TILE = 256
WIDE = 4
PARTS = 1
BF = jnp.bfloat16
F32 = jnp.float32


def dot_nn(left, right):
    return lax.dot_general(left, right, (((1,), (0,)), ((), ())), preferred_element_type=F32)


def dot_nt(left, right):
    return lax.dot_general(left, right, (((1,), (1,)), ((), ())), preferred_element_type=F32)


def dot_tn(left, right):
    return lax.dot_general(left, right, (((0,), (0,)), ((), ())), preferred_element_type=F32)


def row_scale(values):
    return lax.rsqrt(jnp.mean(values * values, axis=-1, keepdims=True) + EPS_NORM)


def row_back(values, scale, grad):
    cubed = scale * scale * scale
    return scale * grad - values * (cubed * jnp.mean(grad * values, axis=-1, keepdims=True))


def silu_slope(values):
    half = 0.5 * jnp.tanh(0.5 * values)
    sigmoid = 0.5 + half
    active = values * sigmoid
    return active, sigmoid + active * (0.5 - half)


def history_kernel(last, blocked, *refs):
    if last:
        (len_ref, spot_ref, recv_ref, same_ref, other_ref, bias_ref) = refs[:6]
        (misc0_ref, big0_ref, small0_ref, gneg0_ref) = refs[6:10]
        (ge_ref, misc_ref, keep_ref, send_ref) = refs[10:14]
        (big_ref, small_ref, gneg_ref, load_sem) = refs[14:18]
        scratch = refs[18:]
    else:
        (len_ref, spot_ref, recv_ref, same_ref, other_ref, bias_ref) = refs[:6]
        (ge_ref, misc_ref, big_ref, small_ref, gneg_ref) = refs[6:11]
        scratch = refs[11:]
    (
        rows_s,
        event_s,
        normed_s,
        gatein_s,
        slope_s,
        valuem_s,
        query_s,
        keys_s,
        keyst_s,
        hot_s,
        hott_s,
        orderc_s,
        order_s,
        out_s,
        gout_s,
        ggate_s,
        dkeys_s,
        dqueryt_s,
        carry_s,
        pairs_s,
        gains_s,
        negs_s,
        bias_s,
        dense_ref,
        dense_sem,
    ) = scratch
    pieces, blocks, tall, piece = recv_ref.shape
    per = tall - 16
    seq, width = normed_s.shape
    groups = width // 128
    heads = 2 * groups
    devices = pieces * blocks
    own = width // devices
    length = len_ref[0]
    tiles = lax.div(length + (TILE - 1), TILE)
    lane = lax.broadcasted_iota(jnp.int32, (TILE, 128), 1)
    low_lanes = lane < 64
    pulls = []
    if blocked:
        for index in range(devices // 2):
            far_col, far_z = index // (blocks // 2), index % (blocks // 2)
            base = lax.bitwise_xor(spot_ref[0], far_col) * blocks
            base = base + lax.bitwise_xor(spot_ref[1], far_z) * 2
            for which, source in enumerate((same_ref, other_ref)):
                core = spot_ref[2] if which == 0 else 1 - spot_ref[2]
                target = pl.ds(pl.multiple_of((base + core) * own, own), own)
                pulls.append(
                    pltpu.make_async_copy(
                        source.at[index], dense_ref.at[target, :], dense_sem.at[2 * index + which]
                    )
                )
    else:
        pulls.append(pltpu.make_async_copy(same_ref, dense_ref, dense_sem.at[0]))
    for one in pulls:
        one.start()
    if last:
        loads = [
            pltpu.make_async_copy(big0_ref, big_ref, load_sem.at[0]),
            pltpu.make_async_copy(small0_ref, small_ref, load_sem.at[1]),
            pltpu.make_async_copy(gneg0_ref, gneg_ref, load_sem.at[2]),
        ]
        for one in loads:
            one.start()
    else:
        big_ref[...] = jnp.zeros_like(big_ref)
        small_ref[...] = jnp.zeros_like(small_ref)
        gneg_ref[...] = jnp.zeros_like(gneg_ref)

    def rows_of(step, count):
        return pl.ds(pl.multiple_of(step * TILE, TILE), count * TILE)

    def sweep(function):
        def pair(index, _):
            function(2 * index, 2)
            return 0

        lax.fori_loop(0, lax.div(tiles, 2), pair, 0)

        @pl.when(lax.bitwise_and(tiles, 1) == 1)
        def _():
            function(tiles - 1, 1)

    def place(step):
        return pl.ds(pl.multiple_of(step * TILE, TILE), TILE)

    for block in range(blocks):
        span = slice(block * per, (block + 1) * per)
        for one in range(pieces):
            rows_s[span, one * piece : (one + 1) * piece] = recv_ref[one, block, 0:per, :]
        about = recv_ref[0, block, per : per + 16, :].astype(F32)
        spot = about[0:1, 0:per] * 32.0 + about[1:2, 0:per]
        order_s[0:1, span] = spot.astype(jnp.int32)
        orderc_s[span, :] = jnp.broadcast_to(about[0:1, :] * 32.0 + about[1:2, :], (128, 128)).T[0:per, :].astype(jnp.int32)
        rows_s[span, width : width + 128] = jnp.broadcast_to(about[2:3, :], (128, 128)).T[0:per, :].astype(BF)
    for one in pulls:
        one.wait()
    if blocked:
        for one in range(pieces):
            for block in range(blocks):
                source = slice((one * blocks + block) * own, (one * blocks + block + 1) * own)
                for index in range(width // piece):
                    start = (block * (width // piece) + index) * own
                    negs_s[start : start + own, one * piece : (one + 1) * piece] = dense_ref[
                        source, 5 * width + index * piece : 5 * width + (index + 1) * piece
                    ]
    else:
        negs_s[...] = dense_ref[:, 5 * width : 6 * width]
    gains_s[...] = dense_ref[:, 6 * width : 6 * width + 128].astype(F32).T[0:8, :]
    lane_half = lax.broadcasted_iota(jnp.int32, (64, 128), 1) < 64
    for head in range(heads):
        line = jnp.broadcast_to(bias_ref[head : head + 1, :], (64, 128))
        wide = pltpu.roll(line, 0, 1, stride=1, stride_axis=0)
        again = pltpu.roll(wide, 64, 1)
        whole = jnp.where(lane_half, wide, again)
        upper = whole.astype(BF)
        lower = (whole - upper.astype(F32)).astype(BF)
        bias_s[0:64, head * 128 : (head + 1) * 128] = jnp.where(lane_half, upper, lower)
    bias_s[64:128, :] = jnp.zeros((64, heads * 128), BF)
    misc_ref[...] = misc0_ref[...] if last else jnp.zeros_like(misc_ref)
    ge_ref[...] = jnp.zeros_like(ge_ref)
    carry_s[...] = jnp.zeros_like(carry_s)
    pairs_s[...] = jnp.zeros_like(pairs_s)
    gain_in = gains_s[0:1, :]
    gain_mid = gains_s[1:2, :]
    gain_out = gains_s[2:3, :]

    def project(step, count):
        span = rows_of(step, count)
        tall = count * TILE
        lane = lax.broadcasted_iota(jnp.int32, (tall, 128), 1)
        low_lanes = lane < 64
        hot = jnp.where(
            order_s[0:1, :] == lax.broadcasted_iota(jnp.int32, (tall, seq), 0) + step * TILE,
            1.0,
            0.0,
        ).astype(BF)
        wide = dot_nn(hot, rows_s[...])
        event = wide[:, 0:width]
        times = wide[:, width : width + 128].astype(jnp.int32)
        bucket = jnp.where(times == jnp.bitwise_and(lane, 63), 1.0, 0.0).astype(BF)
        hot_s[span, :] = bucket
        hott_s[:, span] = jnp.where(times == 63 - lane, 1.0, 0.0).T[0:64, :].astype(BF)
        event_s[span, :] = event.astype(BF)
        normed = (event * row_scale(event) * gain_in).astype(BF)
        normed_s[span, :] = normed
        gatein_s[span, :] = dot_nn(normed, dense_ref[:, 0:width])
        active, slope = silu_slope(dot_nn(normed, dense_ref[:, width : 2 * width]))
        slope_s[0, span, :] = slope.astype(BF)
        scaled = active.astype(BF) * BF(1.0 / seq)
        for group in range(groups):
            part = scaled[:, group * 128 : (group + 1) * 128]
            valuem_s[2 * group, span, :] = jnp.where(low_lanes, part, BF(0))
            valuem_s[2 * group + 1, span, :] = jnp.where(low_lanes, BF(0), part)
        active, slope = silu_slope(dot_nn(normed, dense_ref[:, 2 * width : 3 * width]))
        slope_s[1, span, :] = slope.astype(BF)
        scaled = active.astype(BF) * BF(0.25)
        bias = dot_nn(bucket, bias_s[...]).astype(BF)
        for group in range(groups):
            part = scaled[:, group * 128 : (group + 1) * 128]
            query_s[2 * group, span, 0:128] = jnp.where(low_lanes, part, BF(0))
            query_s[2 * group + 1, span, 0:128] = jnp.where(low_lanes, BF(0), part)
            query_s[2 * group, span, 128:256] = bias[:, group * 256 : group * 256 + 128]
            query_s[2 * group + 1, span, 128:256] = bias[:, group * 256 + 128 : group * 256 + 256]
        active, slope = silu_slope(dot_nn(normed, dense_ref[:, 3 * width : 4 * width]))
        slope_s[2, span, :] = slope.astype(BF)
        scaled = active.astype(BF)
        for group in range(groups):
            part = scaled[:, group * 128 : (group + 1) * 128]
            keys_s[group, span, 0:128] = part
            keys_s[group, span, 128:256] = bucket
            turned = part.T
            keyst_s[2 * group, :, span] = turned[0:64, :]
            keyst_s[2 * group + 1, :, span] = turned[64:128, :]
        for group in range(groups):
            out_s[group, span, :] = jnp.zeros((tall, 128), F32)
        for head in range(heads):
            dkeys_s[head, span, :] = jnp.zeros((tall, 256), F32)
            dqueryt_s[head, :, span] = jnp.zeros((64, tall), F32)

    sweep(project)

    def corner(count):
        rows = lax.broadcasted_iota(jnp.int32, (count * TILE, TILE), 0)
        return rows, lax.broadcasted_iota(jnp.int32, (count * TILE, TILE), 1)

    def attend(near_step, step, count, masked):
        near = place(near_step)
        span = rows_of(step, count)
        wide = WIDE

        def attend_heads(base, _):
            for extra in range(wide):
                group = base * wide + extra
                total = None
                for half in range(2):
                    head = 2 * group + half
                    scores = dot_nt(query_s[head, span, :], keys_s[group, near, :])
                    weight = scores + scores * jnp.tanh(scores)
                    if masked:
                        rows, columns = corner(count)
                        weight = jnp.where(columns <= rows, weight, 0.0)
                    part = dot_nn(weight.astype(BF), valuem_s[head, near, :])
                    total = part if total is None else total + part
                out_s[group, span, :] += total
            return 0

        lax.fori_loop(0, groups // wide, attend_heads, 0)

    def attend_tile(near_step, _):
        odd = lax.bitwise_and(tiles - near_step, 1)

        @pl.when(odd == 1)
        def _():
            attend(near_step, near_step, 1, True)

        @pl.when(odd == 0)
        def _():
            attend(near_step, near_step, 2, True)

        first = near_step + 2 - odd

        def beyond(index, _):
            attend(near_step, first + 2 * index, 2, False)
            return 0

        lax.fori_loop(0, lax.div(tiles - first, 2), beyond, 0)
        return 0

    lax.fori_loop(0, tiles, attend_tile, 0)

    if last:
        for one in loads:
            one.wait()

    def middle(step, count):
        part_rows = count * TILE // PARTS
        row_id = lax.broadcasted_iota(jnp.int32, (part_rows, width), 0)
        row_one = lax.broadcasted_iota(jnp.int32, (part_rows, 1), 0)
        low_part = lax.broadcasted_iota(jnp.int32, (part_rows, 128), 1) < 64
        w_small = dense_ref[:, 4 * width : 5 * width]
        starts = [step * TILE + part * part_rows for part in range(PARTS)]
        spans = [pl.ds(pl.multiple_of(start, part_rows), part_rows) for start in starts]

        def each(function, *lists):
            return [function(*values) for values in zip(*lists)]

        event = each(lambda span: event_s[span, :].astype(F32), spans)
        merged = each(
            lambda span: jnp.concatenate([out_s[group, span, :] for group in range(groups)], axis=1),
            spans,
        )
        for group in range(groups):
            out_s[group, rows_of(step, count), :] = jnp.zeros((count * TILE, 128), F32)
        scale_mid = each(row_scale, merged)
        normed_mid = each(lambda one, scale: one * scale, merged, scale_mid)
        gates = each(lambda span: silu_slope(gatein_s[span, :]), spans)
        mixed = each(
            lambda one, gate: (one * gain_mid * gate[0]).astype(BF), normed_mid, gates
        )
        hidden = each(lambda one, low: one + dot_nn(low, w_small), event, mixed)
        scale_out = each(row_scale, hidden)
        normed_out = each(lambda one, scale: one * scale, hidden, scale_out)
        final = each(lambda one: (one * gain_out).astype(BF), normed_out)
        following = event_s[pl.ds(pl.multiple_of((step + count) * TILE, TILE), 16), :][0:1, :].astype(F32)
        following = jnp.where(step + count < tiles, following, 0.0)
        nexts = [one[0:1, :] for one in event[1:]] + [following]
        target = each(
            lambda one, after: jnp.where(
                row_id == part_rows - 1, after, pltpu.roll(one, part_rows - 1, 0)
            ),
            event,
            nexts,
        )
        negative = each(lambda one: dot_nt(one, negs_s[...]), final)
        positive = each(
            lambda one, aim: jnp.sum(one.astype(F32) * aim, axis=-1, keepdims=True), final, target
        )
        highest = each(
            lambda neg, pos: jnp.maximum(jnp.max(neg, axis=-1, keepdims=True), pos),
            negative,
            positive,
        )
        neg_exp = each(lambda neg, top: jnp.exp(neg - top), negative, highest)
        pos_exp = each(lambda pos, top: jnp.exp(pos - top), positive, highest)
        totals = each(
            lambda pos, neg: pos + jnp.sum(neg, axis=-1, keepdims=True), pos_exp, neg_exp
        )
        counted = each(lambda start: row_one + start < length - 1, starts)
        losses = each(
            lambda keep, top, total, pos: jnp.sum(
                jnp.where(keep, top + jnp.log(total) - pos, 0.0), axis=0, keepdims=True
            ),
            counted,
            highest,
            totals,
            positive,
        )
        misc_ref[3:4, :] += jnp.broadcast_to(sum(losses), (1, width))
        share = each(lambda keep, total: jnp.where(keep, 1.0 / total, 0.0), counted, totals)
        grad_neg = each(lambda one, scale: (one * scale).astype(BF), neg_exp, share)
        grad_pos = each(
            lambda keep, one, scale: jnp.where(keep, one * scale - 1.0, 0.0), counted, pos_exp, share
        )
        grad_final = each(
            lambda low, pos, aim: dot_nn(low, negs_s[...]) + pos * aim, grad_neg, grad_pos, target
        )
        gneg_ref[...] += dot_tn(jnp.concatenate(grad_neg, axis=0), jnp.concatenate(final, axis=0))
        pushed = each(lambda pos, one: pos * one.astype(F32), grad_pos, final)
        earlier = [carry_s[0:1, :]] + [one[part_rows - 1 : part_rows, :] for one in pushed[:-1]]
        grad_event = each(
            lambda one, before: jnp.where(row_id == 0, before, pltpu.roll(one, 1, 0)),
            pushed,
            earlier,
        )
        carry_s[0:1, :] = pushed[-1][part_rows - 1 : part_rows, :]
        gain_sums = each(
            lambda grad, one: jnp.sum(grad * one, axis=0, keepdims=True), grad_final, normed_out
        )
        misc_ref[2:3, :] += sum(gain_sums)
        grad_hidden = each(
            lambda one, scale, grad: row_back(one, scale, grad * gain_out),
            hidden,
            scale_out,
            grad_final,
        )
        branch = each(lambda one: one.astype(BF), grad_hidden)
        grad_mixed = each(lambda one: dot_nt(one, w_small), branch)
        for span, first, second in zip(spans, grad_event, grad_hidden):
            gatein_s[span, :] = first + second
        small_ref[...] += dot_tn(jnp.concatenate(mixed, axis=0), jnp.concatenate(branch, axis=0))
        gated = each(lambda grad, gate: grad * gate[0], grad_mixed, gates)
        gain_sums = each(
            lambda grad, one: jnp.sum(grad * one, axis=0, keepdims=True), gated, normed_mid
        )
        misc_ref[1:2, :] += sum(gain_sums)
        for span, grad, one, gate in zip(spans, grad_mixed, normed_mid, gates):
            ggate_s[span, :] = (grad * one * gain_mid * gate[1]).astype(BF)
        grad_out = each(
            lambda one, scale, grad: row_back(one, scale, grad * gain_mid).astype(BF) * BF(0.5),
            merged,
            scale_mid,
            gated,
        )
        for span, one in zip(spans, grad_out):
            for group in range(groups):
                part = one[:, group * 128 : (group + 1) * 128]
                gout_s[2 * group, span, :] = jnp.where(low_part, part, BF(0))
                gout_s[2 * group + 1, span, :] = jnp.where(low_part, BF(0), part)

    sweep(middle)

    def retreat(step, near_step, count, masked):
        span = place(step)
        near = rows_of(near_step, count)
        wide = WIDE

        def retreat_heads(base, _):
            for extra in range(wide):
                group = base * wide + extra
                keys = keys_s[group, near, :]
                total = None
                for half in range(2):
                    head = 2 * group + half
                    gout = gout_s[head, span, :]
                    query = query_s[head, span, :]
                    scores = dot_nt(keys, query)
                    grads = dot_nt(valuem_s[head, near, :], gout)
                    bent = 1.0 + jnp.tanh(scores)
                    weight = scores * bent
                    slope = bent * ((1.0 + (scores + scores)) - weight)
                    grads = grads * slope
                    if masked:
                        rows, columns = corner(count)
                        visible = rows <= columns + (count - 1) * TILE
                        weight = jnp.where(visible, weight, 0.0)
                        grads = jnp.where(visible, grads, 0.0)
                    grads = grads.astype(BF)
                    part = dot_nn(weight.astype(BF), gout)
                    total = part if total is None else total + part
                    dkeys_s[head, near, :] += dot_nn(
                        grads, jnp.concatenate([query[:, 0:128], hot_s[span, :]], axis=1)
                    )
                    dqueryt_s[head, :, span] += dot_nn(keyst_s[head, :, near], grads)
                out_s[group, near, :] += total
            return 0

        lax.fori_loop(0, groups // wide, retreat_heads, 0)

    def retreat_tile(step, _):
        odd = lax.bitwise_and(step, 1)

        @pl.when(odd == 0)
        def _():
            retreat(step, step, 1, True)

        @pl.when(odd == 1)
        def _():
            retreat(step, step - 1, 2, True)

        def before(index, _):
            retreat(step, 2 * index, 2, False)
            return 0

        lax.fori_loop(0, lax.div(step, 2), before, 0)
        return 0

    lax.fori_loop(0, tiles, retreat_tile, 0)

    def finish(step, count):
        span = rows_of(step, count)
        tall = count * TILE
        normed = normed_s[span, :]
        parts = [ggate_s[span, :]]
        grad = jnp.concatenate([out_s[group, span, :] for group in range(groups)], axis=1)
        parts.append((grad * (2.0 / seq) * slope_s[0, span, :].astype(F32)).astype(BF))
        grad = jnp.concatenate(
            [
                jnp.concatenate([dqueryt_s[2 * group, :, span], dqueryt_s[2 * group + 1, :, span]], axis=0).T
                for group in range(groups)
            ],
            axis=1,
        )
        parts.append((grad * 0.5 * slope_s[1, span, :].astype(F32)).astype(BF))
        grad = jnp.concatenate(
            [
                dkeys_s[2 * group, span, 0:128] + dkeys_s[2 * group + 1, span, 0:128]
                for group in range(groups)
            ],
            axis=1,
        )
        parts.append((grad * 2.0 * slope_s[2, span, :].astype(F32)).astype(BF))
        grad_normed = None
        for index in range(4):
            columns = slice(index * width, (index + 1) * width)
            big_ref[:, columns] += dot_tn(normed, parts[index])
            part = dot_nt(parts[index], dense_ref[:, columns])
            grad_normed = part if grad_normed is None else grad_normed + part
        hott = hott_s[:, span]
        for head in range(heads):
            wide = dkeys_s[head, span, 128:256]
            upper = wide.astype(BF)
            lower = (wide - upper.astype(F32)).astype(BF)
            pairs_s[head] += dot_nn(hott, upper) + dot_nn(hott, lower)
        event = event_s[span, :].astype(F32)
        scale = row_scale(event)
        misc_ref[0:1, :] += jnp.sum(grad_normed * event * scale, axis=0, keepdims=True)
        total = gatein_s[span, :] + row_back(event, scale, grad_normed * gain_in)
        column = orderc_s[...]
        hot = jnp.where(
            jnp.concatenate([column] * (tall // 128), axis=1)
            == lax.broadcasted_iota(jnp.int32, (seq, tall), 1) + step * TILE,
            1.0,
            0.0,
        ).astype(BF)
        moved = dot_nn(hot, total.astype(BF)).astype(BF)
        for block in range(blocks):
            for one in range(pieces):
                ge_ref[one, block] += moved[
                    block * per : (block + 1) * per, one * piece : (one + 1) * piece
                ]

    sweep(finish)

    lane_row = lax.broadcasted_iota(jnp.int32, (64, 128), 1)
    for head in range(heads):
        kept = jnp.where(lane_row < 64, pairs_s[head], 0.0)
        turned = pltpu.roll(kept, 0, 1, stride=1, stride_axis=0)
        misc_ref[8 + head : 9 + head, 0:128] += jnp.sum(turned, axis=0, keepdims=True)
    if last:
        kept = jnp.where(lax.broadcasted_iota(jnp.int32, (8, width), 0) < 3, misc_ref[0:8, :], 0.0)
        gain_rows = jnp.concatenate([kept, jnp.zeros((120, width), F32)], axis=0)
        gain_rows = gain_rows.T.astype(BF)

        def pack(out_ref, target, source, one, block):
            out_ref[target, 0 : 4 * width] = big_ref[source, :].astype(BF)
            out_ref[target, 4 * width : 5 * width] = small_ref[source, :].astype(BF)
            if blocked:
                for index in range(width // piece):
                    start = (block * (width // piece) + index) * own
                    out_ref[target, 5 * width + index * piece : 5 * width + (index + 1) * piece] = gneg_ref[
                        start : start + own, one * piece : (one + 1) * piece
                    ].astype(BF)
            else:
                out_ref[target, 5 * width : 6 * width] = gneg_ref[source, :].astype(BF)
            out_ref[target, 6 * width : 6 * width + 128] = gain_rows[source, :]

        if blocked:
            for core in range(2):

                @pl.when(spot_ref[2] == core)
                def _(core=core):
                    for device in range(devices):
                        one, block = device // blocks, device % blocks
                        source = slice(device * own, (device + 1) * own)
                        target = slice(device // 2 * own, (device // 2 + 1) * own)
                        pack(keep_ref if device % 2 == core else send_ref, target, source, one, block)

        else:
            half = width // 2
            pack(keep_ref, slice(0, half), slice(0, half), 0, 0)
            pack(send_ref, slice(0, half), slice(half, width), 0, 0)


def history_call(length, spot, recv, same, other, bias, before, blocked):
    last = before is not None
    pieces, blocks, tall, piece = recv.shape
    per = tall - 16
    seq = blocks * per
    width = pieces * piece
    heads = width // 64
    groups = heads // 2
    neg_total = width
    vmem = pl.BlockSpec(memory_space=pltpu.VMEM)
    smem = pl.BlockSpec(memory_space=pltpu.SMEM)
    anywhere = pl.BlockSpec(memory_space=pl.ANY)
    shapes = [
        jax.ShapeDtypeStruct((pieces, blocks, per, piece), BF),
        jax.ShapeDtypeStruct((16, width), F32),
    ]
    sums = [(width, 4 * width), (width, width), (neg_total, width)]
    operands = (length, spot, recv, same, other, bias)
    specs = [smem, smem, vmem, anywhere, anywhere, vmem]
    if last:
        operands += tuple(before)
        specs += [vmem, anywhere, anywhere, anywhere]
        shapes += [jax.ShapeDtypeStruct((width // 2, 6 * width + 128), BF)] * 2
        extra = [pltpu.VMEM(one, F32) for one in sums] + [pltpu.SemaphoreType.DMA((3,))]
    else:
        shapes += [jax.ShapeDtypeStruct(one, F32) for one in sums]
        extra = []
    return pl.pallas_call(
        functools.partial(history_kernel, last, blocked),
        out_shape=tuple(shapes),
        in_specs=specs,
        out_specs=(vmem,) * len(shapes),
        scratch_shapes=extra
        + [
            pltpu.VMEM((seq, width + 128), BF),
            pltpu.VMEM((seq + 16, width), BF),
            pltpu.VMEM((seq, width), BF),
            pltpu.VMEM((seq, width), F32),
            pltpu.VMEM((3, seq, width), BF),
            pltpu.VMEM((heads, seq, 128), BF),
            pltpu.VMEM((heads, seq, 256), BF),
            pltpu.VMEM((groups, seq, 256), BF),
            pltpu.VMEM((heads, 64, seq), BF),
            pltpu.VMEM((seq, 128), BF),
            pltpu.VMEM((64, seq), BF),
            pltpu.VMEM((seq, 128), jnp.int32),
            pltpu.VMEM((8, seq), jnp.int32),
            pltpu.VMEM((groups, seq, 128), F32),
            pltpu.VMEM((heads, seq, 128), BF),
            pltpu.VMEM((seq, width), BF),
            pltpu.VMEM((heads, seq, 256), F32),
            pltpu.VMEM((heads, 64, seq), F32),
            pltpu.VMEM((8, width), F32),
            pltpu.VMEM((heads, 64, 128), F32),
            pltpu.VMEM((8, width), F32),
            pltpu.VMEM((neg_total, width), BF),
            pltpu.VMEM((128, heads * 128), BF),
            pltpu.VMEM((width, same.shape[-1]), BF),
            pltpu.SemaphoreType.DMA((pieces * blocks,)),
        ],
        compiler_params=pltpu.CompilerParams(vmem_limit_bytes=60 * 1024 * 1024),
        cost_estimate=pl.CostEstimate(
            flops=40_000_000_000, bytes_accessed=20_000_000, transcendentals=10_000_000
        ),
        name="history_last" if last else "history_first",
    )(*operands)


def prepare_kernel(
    rows_dev,
    col_count,
    len_ref,
    negs_ref,
    spot_ref,
    items_ref,
    times_ref,
    table_ref,
    w_in_ref,
    w_out_ref,
    gains_ref,
    told_ref,
    payload_ref,
    stage_s,
):
    slots, _, seq = items_ref.shape
    own, width = w_out_ref.shape
    blocks = told_ref.shape[0] // col_count
    per = seq // blocks
    payload_ref[:, 0 : 4 * width] = w_in_ref[...].astype(BF)
    payload_ref[:, 4 * width : 5 * width] = w_out_ref[...].astype(BF)
    neg_own = negs_ref.shape[0] // blocks
    row_place = spot_ref[1] * 2 + spot_ref[2]
    for index in range(neg_own):
        number = negs_ref[row_place * neg_own + index] - row_place * rows_dev
        stage_s[index : index + 1, :] = table_ref[pl.ds(number, 1), :]
    for index in range(neg_own // own):
        payload_ref[:, 5 * width + index * 128 : 5 * width + (index + 1) * 128] = stage_s[
            index * own : (index + 1) * own, :
        ].astype(BF)
    square = jnp.zeros((128, 128), F32)
    stage_s[...] = jnp.zeros_like(stage_s)
    stage_s[0 : gains_ref.shape[0], 0:own] = gains_ref[...]
    square = stage_s[0:128, :].T
    payload_ref[:, 6 * width : 6 * width + 128] = square[0:own, :].astype(BF)
    before = jnp.where(
        lax.broadcasted_iota(jnp.int32, (128, 128), 0) < lax.broadcasted_iota(jnp.int32, (128, 128), 1),
        1.0,
        0.0,
    ).astype(BF)
    block_row = lax.broadcasted_iota(jnp.int32, (blocks, seq), 0)
    time = lax.broadcasted_iota(jnp.int32, (1, seq), 1)
    lane = lax.broadcasted_iota(jnp.int32, (1, 128), 1)
    lengths = jnp.zeros((1, 128), jnp.int32)
    for slot in range(slots):
        lengths = jnp.where(lane == slot, len_ref[slot : slot + 1, 0:1], lengths)
        item = items_ref[slot]
        block = jnp.zeros((1, seq), jnp.int32)
        for index in range(1, blocks):
            block = block + jnp.where(item >= index * rows_dev, 1, 0)
        place = item - block * rows_dev
        member = jnp.where(block_row == block, 1.0, 0.0)
        counts = []
        running = jnp.zeros((blocks, 1), F32)
        for part in range(seq // 128):
            piece = member[:, part * 128 : (part + 1) * 128]
            counts.append(dot_nn(piece.astype(BF), before) + running)
            running = running + jnp.sum(piece, axis=1, keepdims=True)
        rank = jnp.sum(member * jnp.concatenate(counts, axis=1), axis=0, keepdims=True)
        target = block * per + rank.astype(jnp.int32)
        upper = lax.shift_right_logical(place, 6)
        late = lax.shift_right_logical(time, 5)
        values = [upper, place - upper * 64, late, time - late * 32, times_ref[slot]]
        values = jnp.concatenate(values + [jnp.zeros((11, seq), jnp.int32)], axis=0)
        values = values.astype(F32).astype(BF)
        for index in range(seq // 256):
            span = slice(index * 256, (index + 1) * 256)
            hot = jnp.where(
                lax.broadcasted_iota(jnp.int32, (256, seq), 0) + index * 256 == target, 1.0, 0.0
            ).astype(BF)
            moved = dot_nt(values, hot).astype(jnp.int32)
            rows = [moved[0:1] * 64 + moved[1:2], moved[2:3] * 32 + moved[3:4], moved[4:5]]
            for inner in range(256 // per):
                cut = slice(inner * per, (inner + 1) * per)
                row = jnp.concatenate([one[:, cut] for one in rows], axis=0)
                if per < 128:
                    row = jnp.concatenate([row, jnp.zeros((3, 128 - per), jnp.int32)], axis=1)
                for one in range(col_count):
                    told_ref[one * blocks + index * (256 // per) + inner, 3 * slot : 3 * slot + 3, :] = row
    for index in range(told_ref.shape[0]):
        told_ref[index, 3 * slots : 3 * slots + 2, :] = jnp.broadcast_to(lengths, (2, 128))


def prepare_call(lengths, negs, spot, items, times, table, w_in, w_out, gains, devices, col_count):
    slots = items.shape[0]
    own, width = w_out.shape
    smem = pl.BlockSpec(memory_space=pltpu.SMEM)
    vmem = pl.BlockSpec(memory_space=pltpu.VMEM)
    return pl.pallas_call(
        functools.partial(prepare_kernel, table.shape[0], col_count),
        out_shape=(
            jax.ShapeDtypeStruct((devices, 3 * slots + 2, 128), jnp.int32),
            jax.ShapeDtypeStruct((own, 6 * width + 128), BF),
        ),
        in_specs=[vmem, smem, smem] + [vmem] * 6,
        out_specs=(vmem, vmem),
        scratch_shapes=[pltpu.VMEM((128, 128), F32)],
        compiler_params=pltpu.CompilerParams(vmem_limit_bytes=60 * 1024 * 1024),
        name="prepare",
    )(lengths, negs, spot, items, times, table, w_in, w_out, gains)


def lookup_kernel(slot, slots, hist_ref, ids_ref, about_ref, table_ref, found_ref, stage_s):
    count, tall, piece = found_ref.shape
    per = tall - 16

    def one(place, _):
        number = hist_ref[slot, place]
        source = lax.div(number, slots)
        line = source * (3 * slots + 2) + 3 * (number - source * slots)
        for index in range(per):
            stage_s[index : index + 1, :] = table_ref[pl.ds(ids_ref[number, index], 1), :]
        found_ref[place, 0:per, :] = stage_s[...].astype(BF)
        spot = about_ref[pl.ds(line + 1, 1), :]
        upper = lax.shift_right_logical(spot, 5)
        times = about_ref[pl.ds(line + 2, 1), :]
        rows = [upper, spot - upper * 32, times, jnp.zeros((13, piece), jnp.int32)]
        found_ref[place, per:tall, :] = jnp.concatenate(rows, axis=0).astype(F32).astype(BF)
        return 0

    lax.fori_loop(0, count, one, 0)


def lookup_call(slot, hist, ids, about, table, per):
    slots, count = hist.shape
    smem = pl.BlockSpec(memory_space=pltpu.SMEM)
    vmem = pl.BlockSpec(memory_space=pltpu.VMEM)
    return pl.pallas_call(
        functools.partial(lookup_kernel, slot, slots),
        out_shape=jax.ShapeDtypeStruct((count, per + 16, table.shape[1]), BF),
        in_specs=[smem, smem, vmem, vmem],
        out_specs=vmem,
        scratch_shapes=[pltpu.VMEM((per, table.shape[1]), F32)],
        compiler_params=pltpu.CompilerParams(vmem_limit_bytes=60 * 1024 * 1024),
        cost_estimate=pl.CostEstimate(
            flops=5_000_000_000, bytes_accessed=4_000_000, transcendentals=0
        ),
        name="lookup",
    )(hist, ids, about, table)


def add_rows(slot, hist_ref, ids_ref, grads_ref, stage_s, sums):
    count = hist_ref.shape[1]
    per = stage_s.shape[0]
    for held in sums:
        held[...] = jnp.zeros_like(held)

    def one(place, _):
        number = hist_ref[slot, place]
        stage_s[...] = grads_ref[pl.ds(pl.multiple_of(place * per, per), per), :].astype(F32)
        for index in range(per):
            held = sums[index % len(sums)]
            spot = pl.ds(ids_ref[number, index], 1)
            held[spot, :] = held[spot, :] + stage_s[index : index + 1, :]
        return 0

    lax.fori_loop(0, count, one, 0)


def scatter_kernel(slot, hist_ref, ids_ref, grads_ref, *refs):
    total_ref, stage_s = refs[-6:-4]
    add_rows(slot, hist_ref, ids_ref, grads_ref, stage_s, refs[-4:])
    total = refs[-4][...]
    for held in refs[-3:]:
        total = total + held[...]
    for init_ref in refs[:-6]:
        total = total + init_ref[...]
    total_ref[...] = total


def scatter_call(slot, hist, heard, grads, rows, per, *init):
    smem = pl.BlockSpec(memory_space=pltpu.SMEM)
    vmem = pl.BlockSpec(memory_space=pltpu.VMEM)
    piece = grads.shape[1]
    return pl.pallas_call(
        functools.partial(scatter_kernel, slot),
        out_shape=jax.ShapeDtypeStruct((rows, piece), F32),
        in_specs=[smem, smem, vmem] + [vmem] * len(init),
        out_specs=vmem,
        scratch_shapes=[pltpu.VMEM((per, piece), F32)] + [pltpu.VMEM((rows, piece), F32)] * 4,
        compiler_params=pltpu.CompilerParams(vmem_limit_bytes=60 * 1024 * 1024),
        cost_estimate=pl.CostEstimate(
            flops=6_000_000_000, bytes_accessed=4_000_000, transcendentals=0
        ),
        name="scatter",
    )(hist, heard, grads, *init)


def gather_up_kernel(width, blocks, negs_ref, spot_ref, table_ref, misc_ref, base_ref, *refs):
    total_ref, shard_ref, gain_ref, told_ref = refs[-4:]
    shard = base_ref[...]
    for got in refs[:-4]:
        shard = shard + got[...].astype(F32)
    shard_ref[...] = shard
    own = shard.shape[0]
    total_ref[...] = table_ref[...]
    neg_own = negs_ref.shape[0] // blocks
    row_place = spot_ref[1] * 2 + spot_ref[2]
    for index in range(neg_own):
        number = negs_ref[row_place * neg_own + index] - row_place * total_ref.shape[0]
        spot = pl.ds(number, 1)
        row = index % own
        start = 5 * width + index // own * 128
        total_ref[spot, :] = total_ref[spot, :] + shard_ref[row : row + 1, start : start + 128]
    total = total_ref[...]
    squares = jnp.sum(total * total, axis=0, keepdims=True)
    for index in range(5 * width // 128):
        part = shard_ref[:, index * 128 : (index + 1) * 128]
        squares = squares + jnp.sum(part * part, axis=0, keepdims=True)
    part = shard_ref[:, 6 * width : 6 * width + 128]
    squares = squares + jnp.sum(part * part, axis=0, keepdims=True)
    turned = jnp.concatenate([part, jnp.zeros((128 - own, 128), F32)], axis=0).T
    gain_ref[...] = turned[0:8, :]
    spread = misc_ref[8:16, 0:128]
    lane = lax.broadcasted_iota(jnp.int32, (8, 128), 1)
    low = jnp.sum(jnp.where(lane < 63, spread, 0.0), axis=1, keepdims=True)
    high = jnp.sum(jnp.where(lane >= 62 + NB, spread, 0.0), axis=1, keepdims=True)
    folded = jnp.where(lane < NB - 1, pltpu.roll(spread, 65, 1), 0.0)
    folded = folded + jnp.where(lane == 0, low, 0.0) + jnp.where(lane == NB - 1, high, 0.0)
    rows = []
    for half in range(2):
        row = folded[4 * half : 4 * half + 1, :]
        for index in range(1, 4):
            row = row + pltpu.roll(folded[4 * half + index : 4 * half + index + 1, :], NB * index, 1)
        rows.append(row)
    rows += [misc_ref[3:4, 0:128], squares]
    told_ref[...] = jnp.broadcast_to(jnp.concatenate(rows, axis=0)[None], told_ref.shape)


def gather_up_call(negs, spot, table_sum, misc, base, gots, devices, row_count):
    smem = pl.BlockSpec(memory_space=pltpu.SMEM)
    vmem = pl.BlockSpec(memory_space=pltpu.VMEM)
    return pl.pallas_call(
        functools.partial(gather_up_kernel, misc.shape[1], row_count),
        out_shape=(
            jax.ShapeDtypeStruct(table_sum.shape, F32),
            jax.ShapeDtypeStruct(base.shape, F32),
            jax.ShapeDtypeStruct((8, 128), F32),
            jax.ShapeDtypeStruct((devices, 4, 128), F32),
        ),
        in_specs=[smem, smem] + [vmem] * (3 + len(gots)),
        out_specs=(vmem,) * 4,
        compiler_params=pltpu.CompilerParams(vmem_limit_bytes=60 * 1024 * 1024),
        name="gather_up",
    )(negs, spot, table_sum, misc, base, *gots)


def fold_kernel(parts, place_ref, base_ref, *refs):
    gots = refs[: len(refs) - parts]
    own_ref = refs[len(refs) - parts]
    sends = refs[len(refs) - parts + 1 :]
    tall = own_ref.shape[0]
    for offset in range(parts):
        span = pl.ds(pl.multiple_of(lax.bitwise_xor(place_ref[0], offset) * tall, tall), tall)
        total = base_ref[span, :].astype(F32)
        for got in gots:
            total = total + got[span, :].astype(F32)
        if offset == 0:
            own_ref[...] = total
        else:
            sends[offset - 1][...] = total.astype(BF)


def fold_call(place, base, gots, parts):
    tall = base.shape[0] // parts
    vmem = pl.BlockSpec(memory_space=pltpu.VMEM)
    shapes = [jax.ShapeDtypeStruct((tall, base.shape[1]), F32)]
    shapes += [jax.ShapeDtypeStruct((tall, base.shape[1]), BF)] * (parts - 1)
    return pl.pallas_call(
        functools.partial(fold_kernel, parts),
        out_shape=tuple(shapes),
        in_specs=[pl.BlockSpec(memory_space=pltpu.SMEM)] + [vmem] * (1 + len(gots)),
        out_specs=(vmem,) * parts,
        compiler_params=pltpu.CompilerParams(vmem_limit_bytes=60 * 1024 * 1024),
        name="fold",
    )(place, base, *gots)


def update_kernel(
    width,
    count_ref,
    heard_ref,
    shard_ref,
    sum_ref,
    table_ref,
    table_m_ref,
    table_v_ref,
    w_in_ref,
    w_in_m_ref,
    w_in_v_ref,
    w_out_ref,
    w_out_m_ref,
    w_out_v_ref,
    gain_grad_ref,
    gains_ref,
    gains_m_ref,
    gains_v_ref,
    rab_ref,
    rab_m_ref,
    rab_v_ref,
    loss_ref,
    total_ref,
    norm_ref,
    table_new_ref,
    table_m_new_ref,
    table_v_new_ref,
    table_low_ref,
    w_in_new_ref,
    w_in_m_new_ref,
    w_in_v_new_ref,
    w_in_low_ref,
    w_out_new_ref,
    w_out_m_new_ref,
    w_out_v_new_ref,
    w_out_low_ref,
    gains_new_ref,
    gains_m_new_ref,
    gains_v_new_ref,
    rab_new_ref,
    rab_m_new_ref,
    rab_v_new_ref,
    factor_s,
    rab_s,
):
    def update(weight_ref, first_ref, second_ref, grad, rate, outs):
        weight, first, second = adamw_update(
            weight_ref[...], first_ref[...], second_ref[...], grad, rate
        )
        outs[0][...] = weight
        outs[1][...] = first
        outs[2][...] = second
        if len(outs) > 3:
            outs[3][...] = weight.astype(BF)

    @pl.when(pl.program_id(0) == 0)
    def _():
        heard = jnp.sum(heard_ref[...], axis=0)
        for head in range(rab_s.shape[0]):
            rab_s[head : head + 1, :] = heard[
                head // 4 : head // 4 + 1, head % 4 * NB : (head % 4 + 1) * NB
            ]
        count = jnp.full((1, 1), count_ref[0].astype(F32))
        squares = jnp.sum(heard[3:4, :], axis=1, keepdims=True)
        squares = squares + jnp.sum(jnp.sum(heard[0:2, :] * heard[0:2, :], axis=1, keepdims=True), axis=0, keepdims=True)
        norm = jnp.sqrt(squares) / count
        factor = jnp.minimum(1.0, CLIP_NORM / norm) / count
        factor_s[...] = jnp.broadcast_to(factor, factor_s.shape)
        loss_ref[0] = jnp.sum(heard[2:3, 0:1])
        total_ref[0] = count_ref[0].astype(F32)
        norm_ref[0] = jnp.sum(norm)
        update(
            w_in_ref,
            w_in_m_ref,
            w_in_v_ref,
            shard_ref[:, 0 : 4 * width] * factor,
            RATE_DENSE,
            (w_in_new_ref, w_in_m_new_ref, w_in_v_new_ref, w_in_low_ref),
        )
        update(
            w_out_ref,
            w_out_m_ref,
            w_out_v_ref,
            shard_ref[:, 4 * width : 5 * width] * factor,
            RATE_DENSE,
            (w_out_new_ref, w_out_m_new_ref, w_out_v_new_ref, w_out_low_ref),
        )
        update(
            gains_ref,
            gains_m_ref,
            gains_v_ref,
            gain_grad_ref[0:3, 0 : gains_ref.shape[1]] * factor,
            RATE_SMALL,
            (gains_new_ref, gains_m_new_ref, gains_v_new_ref),
        )
        update(
            rab_ref,
            rab_m_ref,
            rab_v_ref,
            rab_s[...] * factor,
            RATE_SMALL,
            (rab_new_ref, rab_m_new_ref, rab_v_new_ref),
        )

    update(
        table_ref,
        table_m_ref,
        table_v_ref,
        sum_ref[...] * factor_s[0:1, :],
        RATE_TABLE,
        (table_new_ref, table_m_new_ref, table_v_new_ref, table_low_ref),
    )


def update_call(count, heard, shard, table_sum, tables, w_ins, w_outs, gain_grad, gains, rabs):
    steps = 2
    rows, piece = table_sum.shape

    def whole(array):
        zeros = (0,) * len(array.shape)
        return pl.BlockSpec(array.shape, lambda step: zeros)

    def block(array):
        return pl.BlockSpec((rows // steps, piece), lambda step: (step, 0))

    operands = [heard, shard, table_sum, *tables, *w_ins, *w_outs, gain_grad, *gains, *rabs]
    specs = [pl.BlockSpec(memory_space=pltpu.SMEM)]
    specs += [block(one) if one.shape == (rows, piece) else whole(one) for one in operands]

    def like(array, kind=F32):
        return jax.ShapeDtypeStruct(array.shape, kind)

    shapes = [jax.ShapeDtypeStruct((1,), F32)] * 3
    for group in (tables, w_ins, w_outs, gains, rabs):
        shapes += [like(group[0])] * 3
        if group is tables or group is w_ins or group is w_outs:
            shapes.append(like(group[0], BF))
    return pl.pallas_call(
        functools.partial(update_kernel, shard.shape[1] // 6 // 128 * 128),
        out_shape=tuple(shapes),
        grid=(steps,),
        in_specs=specs,
        out_specs=(pl.BlockSpec(memory_space=pltpu.SMEM),) * 3
        + tuple(block(one) if one.shape == (rows, piece) else whole(one) for one in shapes[3:]),
        scratch_shapes=[pltpu.VMEM((8, 128), F32), pltpu.VMEM(rabs[0].shape, F32)],
        compiler_params=pltpu.CompilerParams(vmem_limit_bytes=60 * 1024 * 1024),
        name="update",
    )(count, *operands)


def bias_line(rab):
    first = jnp.broadcast_to(rab[:, :1], (rab.shape[0], 64))
    final = jnp.broadcast_to(rab[:, NB - 1 :], (rab.shape[0], 65 - NB))
    return 0.5 * jnp.concatenate([first, final, rab[:, NB - 1 : 0 : -1]], axis=1)


def adamw_update(weight, first, second, grad, rate):
    first = BETA_ONE * first + (1.0 - BETA_ONE) * grad
    second = BETA_TWO * second + (1.0 - BETA_TWO) * grad * grad
    fixed_first = first / (1.0 - BETA_ONE**STEP)
    fixed_second = second / (1.0 - BETA_TWO**STEP)
    weight = weight - rate * (
        fixed_first / (jnp.sqrt(fixed_second) + EPS_ADAM) + WEIGHT_DECAY * weight
    )
    return (weight, first, second)


def exchange(values, axes, groups=None):
    return lax.all_to_all(
        values, axes, split_axis=0, concat_axis=0, tiled=True, axis_index_groups=groups
    )


def swap_sum(values, axis, count, stride, parts):
    mine = (lax.axis_index(axis) // stride) % parts

    def part(index):
        return lax.dynamic_index_in_dim(values, index, axis=0, keepdims=False)

    total = part(mine).astype(F32)
    for offset in range(1, parts):
        pairs = []
        for place in range(count):
            spot = (place // stride) % parts
            pairs.append((place, place + ((spot ^ offset) - spot) * stride))
        got = lax.ppermute(part(mine ^ offset).astype(BF), axis, pairs)
        total = total + got.astype(F32)
    return total


def swap_parts(sends, axis, count, stride):
    gots = []
    for offset, send in enumerate(sends, 1):
        pairs = []
        for place in range(count):
            spot = place // stride
            pairs.append((place, place + ((spot ^ offset) - spot) * stride))
        gots.append(lax.ppermute(send, axis, pairs))
    return gots


def fold_dense(keep, send, col_count, row_count, blocked, between):
    columns = keep.shape[1]
    half = row_count // 2
    own = keep.shape[0] // (col_count * half)
    got = lax.ppermute(send, "row", [(place, place ^ 1) for place in range(row_count)])
    if blocked:
        total, *sends = fold_call(lax.axis_index("col").reshape(1), keep, [got], col_count)
        gots = swap_parts(sends, "col", col_count, 1)
        gots[0] = between(gots[0])
        total, *sends = fold_call((lax.axis_index("row") // 2).reshape(1), total, gots, half)
        return total, swap_parts(sends, "row", row_count, 2)
    total = (keep.astype(F32) + got.astype(F32)).reshape(col_count, half * own, columns)
    total = swap_sum(total, "col", col_count, 1, col_count)
    return swap_sum(total.reshape(half, own, columns), "row", row_count, 2, half), []


def local(
    lengths,
    items,
    negatives,
    time_buckets,
    table,
    table_m,
    table_v,
    w_in,
    w_in_m,
    w_in_v,
    w_out,
    w_out_m,
    w_out_v,
    gains,
    gains_m,
    gains_v,
    rab,
    rab_m,
    rab_v,
):
    col_count = lax.axis_size("col")
    row_count = lax.axis_size("row")
    devices = col_count * row_count
    row_place = lax.axis_index("row")
    me = lax.axis_index("col") * row_count + row_place
    rows_dev, piece = table.shape
    own, width = w_out.shape
    slots, _, seq = items.shape
    per = seq // row_count
    neg_total = negatives.shape[0]
    neg_own = neg_total // row_count
    blocked = own % 16 == 0
    spot = jnp.stack([lax.axis_index("col"), row_place // 2, row_place % 2])
    told, payload = prepare_call(
        lengths,
        negatives,
        spot,
        items,
        time_buckets,
        table,
        w_in,
        w_out,
        gains,
        devices,
        col_count,
    )
    bias = bias_line(rab)
    heard = exchange(told, BOTH)
    if blocked:
        half = row_count // 2
        same = jnp.stack([payload] + swap_parts([payload] * (half - 1), "row", row_count, 2))
        same = jnp.stack([same] + swap_parts([same] * (col_count - 1), "col", col_count, 1))
        same = same.reshape(devices // 2, own, -1)
        other = lax.ppermute(same, "row", [(place, place ^ 1) for place in range(row_count)])
    else:
        dense = lax.all_gather(payload, BOTH, axis=0, tiled=True)
        neg_rows = (
            dense[:, 5 * width : 6 * width]
            .reshape(col_count, row_count, own, neg_own // own, piece)
            .transpose(1, 3, 2, 0, 4)
            .reshape(neg_total, width)
        )
        same = jnp.concatenate([dense[:, : 5 * width], neg_rows, dense[:, 6 * width :]], axis=1)
        other = same
    heard = heard.reshape(-1, 128)
    ids = heard.reshape(devices, -1, 128)[:, : 3 * slots]
    ids = ids.reshape(devices * slots, 3, 128)[:, 0]
    every_length = heard.reshape(devices, -1, 128)[:, 3 * slots, :slots].reshape(-1)
    total = devices * slots
    number = jnp.arange(total)
    ahead = (every_length[None, :] > every_length[:, None]) | (
        (every_length[None, :] == every_length[:, None]) & (number[None, :] < number[:, None])
    )
    rank = jnp.sum(ahead.astype(jnp.int32), axis=1)
    wanted = jnp.stack(
        [
            slot * devices + (jnp.arange(devices) if slot % 2 == 0 else devices - 1 - jnp.arange(devices))
            for slot in range(slots)
        ]
    )
    hist = jnp.sum(
        jnp.where(rank[None, None, :] == wanted[:, :, None], number[None, None, :], 0), axis=2
    )
    my_length = jnp.sum(
        jnp.where(
            rank[None, :] == lax.dynamic_slice_in_dim(wanted, me, 1, axis=1),
            every_length[None, :],
            0,
        ),
        axis=1,
    )
    sent = []
    for slot in range(slots):
        found = lookup_call(slot, hist, ids, heard, table, per)
        sent.append(exchange(found, BOTH).reshape(col_count, row_count, per + 16, piece))
    core = (row_place % 2).reshape(1)
    first = history_call(my_length[0:1], spot, sent[0], same, other, bias, None, blocked)
    back = [exchange(first[0].reshape(devices, per, piece), BOTH)]
    final = history_call(my_length[1:2], spot, sent[1], same, other, bias, first[1:], blocked)
    final_rows, back[0] = lax.optimization_barrier((final[0], back[0]))
    back.append(exchange(final_rows.reshape(devices, per, piece), BOTH))
    grad_misc, keep, send = final[1:]
    if not blocked:
        packed = jnp.concatenate([keep, send], axis=0)
        neg_part = (
            packed[:, 5 * width : 6 * width]
            .reshape(row_count, neg_own // own, own, col_count, piece)
            .transpose(3, 0, 2, 1, 4)
            .reshape(width, width)
        )
        packed = jnp.concatenate(
            [packed[:, : 5 * width], neg_part, packed[:, 6 * width :]], axis=1
        ).reshape(devices // 2, 2, own, -1)
        keep = lax.dynamic_index_in_dim(packed, core[0], axis=1, keepdims=False)
        send = lax.dynamic_index_in_dim(packed, 1 - core[0], axis=1, keepdims=False)
        keep = keep.reshape(width // 2, -1)
        send = send.reshape(width // 2, -1)
    loss_count = jnp.sum(jnp.maximum(every_length - 1, 0)).reshape(1)
    table_part = scatter_call(
        0, hist, ids, back[0].reshape(devices * per, piece), rows_dev, per
    )
    base, gots = fold_dense(
        keep,
        send,
        col_count,
        row_count,
        blocked,
        lambda value: lax.optimization_barrier((value, table_part))[0],
    )
    table_sum = scatter_call(
        1, hist, ids, back[1].reshape(devices * per, piece), rows_dev, per, table_part
    )
    table_sum, shard, gain_grad, told = gather_up_call(
        negatives, spot, table_sum, grad_misc, base, gots, devices, row_count
    )
    heard = exchange(told, BOTH)
    loss, total_count, norm, *updated = update_call(
        loss_count,
        heard,
        shard,
        table_sum,
        (table, table_m, table_v),
        (w_in, w_in_m, w_in_v),
        (w_out, w_out_m, w_out_v),
        gain_grad,
        (gains, gains_m, gains_v),
        (rab, rab_m, rab_v),
    )
    return (loss.reshape(()), total_count.reshape(()), norm.reshape(()), *updated)


def solution(mesh):
    placed = (
        P(None, ("col", "row")),
        P(None, ("col", "row"), None),
        P(),
        P(None, ("col", "row"), None),
        P("row", "col"),
        P("row", "col"),
        P("row", "col"),
        P(("col", "row"), None),
        P(("col", "row"), None),
        P(("col", "row"), None),
        P(("col", "row"), None),
        P(("col", "row"), None),
        P(("col", "row"), None),
        P(None, ("col", "row")),
        P(None, ("col", "row")),
        P(None, ("col", "row")),
        P(),
        P(),
        P(),
    )
    return jax.shard_map(
        local,
        mesh=mesh,
        in_specs=placed,
        out_specs=(
            P(),
            P(),
            P(),
            P("row", "col"),
            P("row", "col"),
            P("row", "col"),
            P("row", "col"),
            P(("col", "row"), None),
            P(("col", "row"), None),
            P(("col", "row"), None),
            P(("col", "row"), None),
            P(("col", "row"), None),
            P(("col", "row"), None),
            P(("col", "row"), None),
            P(("col", "row"), None),
            P(None, ("col", "row")),
            P(None, ("col", "row")),
            P(None, ("col", "row")),
            P(),
            P(),
            P(),
        ),
        check_vma=False,
    )
```

```python
import functools
import jax
import jax.numpy as jnp
from jax import lax
from jax.experimental import pallas as pl
from jax.experimental.pallas import tpu as pltpu
from jax.sharding import PartitionSpec as P

NB = 32
STEP = 10
BETA_ONE = 0.9
BETA_TWO = 0.999
EPS_ADAM = 1e-08
EPS_NORM = 1e-06
WEIGHT_DECAY = 0.01
CLIP_NORM = 0.05
RATE_TABLE = 0.06
RATE_DENSE = 0.01
RATE_SMALL = 0.5
BOTH = ("col", "row")
TILE = 256
WIDE = 4
PARTS = 1
BF = jnp.bfloat16
F32 = jnp.float32


def dot_nn(left, right):
    return lax.dot_general(left, right, (((1,), (0,)), ((), ())), preferred_element_type=F32)


def dot_nt(left, right):
    return lax.dot_general(left, right, (((1,), (1,)), ((), ())), preferred_element_type=F32)


def dot_tn(left, right):
    return lax.dot_general(left, right, (((0,), (0,)), ((), ())), preferred_element_type=F32)


def row_scale(values):
    return lax.rsqrt(jnp.mean(values * values, axis=-1, keepdims=True) + EPS_NORM)


def row_back(values, scale, grad):
    cubed = scale * scale * scale
    return scale * grad - values * (cubed * jnp.mean(grad * values, axis=-1, keepdims=True))


def silu_slope(values):
    half = 0.5 * jnp.tanh(0.5 * values)
    sigmoid = 0.5 + half
    active = values * sigmoid
    return active, sigmoid + active * (0.5 - half)


def history_kernel(last, blocked, *refs):
    if last:
        (len_ref, spot_ref, recv_ref, same_ref, other_ref, bias_ref) = refs[:6]
        (misc0_ref, big0_ref, small0_ref, gneg0_ref) = refs[6:10]
        (ge_ref, misc_ref, keep_ref, send_ref) = refs[10:14]
        (big_ref, small_ref, gneg_ref, load_sem) = refs[14:18]
        scratch = refs[18:]
    else:
        (len_ref, spot_ref, recv_ref, same_ref, other_ref, bias_ref) = refs[:6]
        (ge_ref, misc_ref, big_ref, small_out_ref, gneg_out_ref) = refs[6:11]
        (small_ref, gneg_ref, store_sem) = refs[11:14]
        scratch = refs[14:]
    (
        rows_s,
        event_s,
        normed_s,
        gatein_s,
        slope_s,
        valuem_s,
        query_s,
        keys_s,
        keyst_s,
        hot_s,
        hott_s,
        orderc_s,
        order_s,
        out_s,
        gout_s,
        ggate_s,
        dkeys_s,
        dqueryt_s,
        carry_s,
        pairs_s,
        gains_s,
        negs_s,
        bias_s,
        dense_ref,
        dense_sem,
    ) = scratch
    pieces, blocks, tall, piece = recv_ref.shape
    per = tall - 8
    seq, width = normed_s.shape
    groups = width // 128
    heads = 2 * groups
    devices = pieces * blocks
    own = width // devices
    length = len_ref[0]
    tiles = lax.div(length + (TILE - 1), TILE)
    lane = lax.broadcasted_iota(jnp.int32, (TILE, 128), 1)
    low_lanes = lane < 64
    pulls = []
    if blocked:
        for index in range(devices // 2):
            far_col, far_z = index // (blocks // 2), index % (blocks // 2)
            base = lax.bitwise_xor(spot_ref[0], far_col) * blocks
            base = base + lax.bitwise_xor(spot_ref[1], far_z) * 2
            for which, source in enumerate((same_ref, other_ref)):
                core = spot_ref[2] if which == 0 else 1 - spot_ref[2]
                target = pl.ds(pl.multiple_of((base + core) * own, own), own)
                pulls.append(
                    pltpu.make_async_copy(
                        source.at[index], dense_ref.at[target, :], dense_sem.at[2 * index + which]
                    )
                )
    else:
        pulls.append(pltpu.make_async_copy(same_ref, dense_ref, dense_sem.at[0]))
    for one in pulls:
        one.start()
    if last:
        loads = [
            pltpu.make_async_copy(big0_ref, big_ref, load_sem.at[0]),
            pltpu.make_async_copy(small0_ref, small_ref, load_sem.at[1]),
            pltpu.make_async_copy(gneg0_ref, gneg_ref, load_sem.at[2]),
        ]
        for one in loads:
            one.start()
    else:
        big_ref[...] = jnp.zeros_like(big_ref)
        small_ref[...] = jnp.zeros_like(small_ref)
        gneg_ref[...] = jnp.zeros_like(gneg_ref)

    def rows_of(step, count):
        return pl.ds(pl.multiple_of(step * TILE, TILE), count * TILE)

    def sweep(function):
        def pair(index, _):
            function(2 * index, 2)
            return 0

        lax.fori_loop(0, lax.div(tiles, 2), pair, 0)

        @pl.when(lax.bitwise_and(tiles, 1) == 1)
        def _():
            function(tiles - 1, 1)

    def place(step):
        return pl.ds(pl.multiple_of(step * TILE, TILE), TILE)

    for block in range(blocks):
        span = slice(block * per, (block + 1) * per)
        for one in range(pieces):
            rows_s[span, one * piece : (one + 1) * piece] = recv_ref[one, block, 0:per, :]
        about = recv_ref[0, block, per : per + 8, :].astype(F32)
        spot = about[0:1, 0:per] * 32.0 + about[1:2, 0:per]
        order_s[0:1, span] = spot.astype(jnp.int32)
        orderc_s[span, :] = jnp.broadcast_to(about[0:1, :] * 32.0 + about[1:2, :], (128, 128)).T[0:per, :].astype(jnp.int32)
        rows_s[span, width : width + 128] = jnp.broadcast_to(about[2:3, :], (128, 128)).T[0:per, :].astype(BF)
    for one in pulls:
        one.wait()
    if blocked:
        for one in range(pieces):
            for block in range(blocks):
                source = slice((one * blocks + block) * own, (one * blocks + block + 1) * own)
                for index in range(width // piece):
                    start = (block * (width // piece) + index) * own
                    negs_s[start : start + own, one * piece : (one + 1) * piece] = dense_ref[
                        source, 5 * width + index * piece : 5 * width + (index + 1) * piece
                    ]
    else:
        negs_s[...] = dense_ref[:, 5 * width : 6 * width]
    gains_s[...] = dense_ref[:, 6 * width : 6 * width + 128].astype(F32).T[0:8, :]
    lane_half = lax.broadcasted_iota(jnp.int32, (64, 128), 1) < 64
    for head in range(heads):
        line = jnp.broadcast_to(bias_ref[head : head + 1, :], (64, 128))
        wide = pltpu.roll(line, 0, 1, stride=1, stride_axis=0)
        again = pltpu.roll(wide, 64, 1)
        whole = jnp.where(lane_half, wide, again)
        upper = whole.astype(BF)
        lower = (whole - upper.astype(F32)).astype(BF)
        bias_s[0:64, head * 128 : (head + 1) * 128] = jnp.where(lane_half, upper, lower)
    bias_s[64:128, :] = jnp.zeros((64, heads * 128), BF)
    misc_ref[...] = misc0_ref[...] if last else jnp.zeros_like(misc_ref)
    ge_ref[...] = jnp.zeros_like(ge_ref)
    carry_s[...] = jnp.zeros_like(carry_s)
    pairs_s[...] = jnp.zeros_like(pairs_s)
    gain_in = gains_s[0:1, :]
    gain_mid = gains_s[1:2, :]
    gain_out = gains_s[2:3, :]

    def project(step, count):
        span = rows_of(step, count)
        tall = count * TILE
        lane = lax.broadcasted_iota(jnp.int32, (tall, 128), 1)
        low_lanes = lane < 64
        hot = jnp.where(
            order_s[0:1, :] == lax.broadcasted_iota(jnp.int32, (tall, seq), 0) + step * TILE,
            1.0,
            0.0,
        ).astype(BF)
        wide = dot_nn(hot, rows_s[...])
        event = wide[:, 0:width]
        times = wide[:, width : width + 128].astype(jnp.int32)
        bucket = jnp.where(times == jnp.bitwise_and(lane, 63), 1.0, 0.0).astype(BF)
        hot_s[span, :] = bucket
        hott_s[:, span] = jnp.where(times == 63 - lane, 1.0, 0.0).T[0:64, :].astype(BF)
        event_s[span, :] = event.astype(BF)
        normed = (event * row_scale(event) * gain_in).astype(BF)
        normed_s[span, :] = normed
        gatein_s[span, :] = dot_nn(normed, dense_ref[:, 0:width])
        active, slope = silu_slope(dot_nn(normed, dense_ref[:, width : 2 * width]))
        slope_s[0, span, :] = slope.astype(BF)
        scaled = active.astype(BF) * BF(1.0 / seq)
        for group in range(groups):
            part = scaled[:, group * 128 : (group + 1) * 128]
            valuem_s[2 * group, span, :] = jnp.where(low_lanes, part, BF(0))
            valuem_s[2 * group + 1, span, :] = jnp.where(low_lanes, BF(0), part)
        active, slope = silu_slope(dot_nn(normed, dense_ref[:, 2 * width : 3 * width]))
        slope_s[1, span, :] = slope.astype(BF)
        scaled = active.astype(BF) * BF(0.25)
        bias = dot_nn(bucket, bias_s[...]).astype(BF)
        for group in range(groups):
            part = scaled[:, group * 128 : (group + 1) * 128]
            query_s[2 * group, span, 0:128] = jnp.where(low_lanes, part, BF(0))
            query_s[2 * group + 1, span, 0:128] = jnp.where(low_lanes, BF(0), part)
            query_s[2 * group, span, 128:256] = bias[:, group * 256 : group * 256 + 128]
            query_s[2 * group + 1, span, 128:256] = bias[:, group * 256 + 128 : group * 256 + 256]
        active, slope = silu_slope(dot_nn(normed, dense_ref[:, 3 * width : 4 * width]))
        slope_s[2, span, :] = slope.astype(BF)
        scaled = active.astype(BF)
        for group in range(groups):
            part = scaled[:, group * 128 : (group + 1) * 128]
            keys_s[group, span, 0:128] = part
            keys_s[group, span, 128:256] = bucket
            turned = part.T
            keyst_s[2 * group, :, span] = turned[0:64, :]
            keyst_s[2 * group + 1, :, span] = turned[64:128, :]
        for group in range(groups):
            out_s[group, span, :] = jnp.zeros((tall, 128), F32)
        for head in range(heads):
            dkeys_s[head, span, :] = jnp.zeros((tall, 256), F32)
            dqueryt_s[head, :, span] = jnp.zeros((64, tall), F32)

    sweep(project)

    def corner(count):
        rows = lax.broadcasted_iota(jnp.int32, (count * TILE, TILE), 0)
        return rows, lax.broadcasted_iota(jnp.int32, (count * TILE, TILE), 1)

    def attend(near_step, step, count, masked):
        near = place(near_step)
        span = rows_of(step, count)
        wide = WIDE

        def attend_heads(base, _):
            for extra in range(wide):
                group = base * wide + extra
                total = None
                for half in range(2):
                    head = 2 * group + half
                    scores = dot_nt(query_s[head, span, :], keys_s[group, near, :])
                    weight = scores + scores * jnp.tanh(scores)
                    if masked:
                        rows, columns = corner(count)
                        weight = jnp.where(columns <= rows, weight, 0.0)
                    part = dot_nn(weight.astype(BF), valuem_s[head, near, :])
                    total = part if total is None else total + part
                out_s[group, span, :] += total
            return 0

        lax.fori_loop(0, groups // wide, attend_heads, 0)

    def attend_tile(near_step, _):
        odd = lax.bitwise_and(tiles - near_step, 1)

        @pl.when(odd == 1)
        def _():
            attend(near_step, near_step, 1, True)

        @pl.when(odd == 0)
        def _():
            attend(near_step, near_step, 2, True)

        first = near_step + 2 - odd

        def beyond(index, _):
            attend(near_step, first + 2 * index, 2, False)
            return 0

        lax.fori_loop(0, lax.div(tiles - first, 2), beyond, 0)
        return 0

    lax.fori_loop(0, tiles, attend_tile, 0)

    if last:
        for one in loads:
            one.wait()

    def middle(step, count):
        part_rows = count * TILE // PARTS
        row_id = lax.broadcasted_iota(jnp.int32, (part_rows, width), 0)
        row_one = lax.broadcasted_iota(jnp.int32, (part_rows, 1), 0)
        low_part = lax.broadcasted_iota(jnp.int32, (part_rows, 128), 1) < 64
        w_small = dense_ref[:, 4 * width : 5 * width]
        starts = [step * TILE + part * part_rows for part in range(PARTS)]
        spans = [pl.ds(pl.multiple_of(start, part_rows), part_rows) for start in starts]

        def each(function, *lists):
            return [function(*values) for values in zip(*lists)]

        event = each(lambda span: event_s[span, :].astype(F32), spans)
        merged = each(
            lambda span: jnp.concatenate([out_s[group, span, :] for group in range(groups)], axis=1),
            spans,
        )
        for group in range(groups):
            out_s[group, rows_of(step, count), :] = jnp.zeros((count * TILE, 128), F32)
        scale_mid = each(row_scale, merged)
        normed_mid = each(lambda one, scale: one * scale, merged, scale_mid)
        gates = each(lambda span: silu_slope(gatein_s[span, :]), spans)
        mixed = each(
            lambda one, gate: (one * gain_mid * gate[0]).astype(BF), normed_mid, gates
        )
        hidden = each(lambda one, low: one + dot_nn(low, w_small), event, mixed)
        scale_out = each(row_scale, hidden)
        normed_out = each(lambda one, scale: one * scale, hidden, scale_out)
        final = each(lambda one: (one * gain_out).astype(BF), normed_out)
        following = event_s[pl.ds(pl.multiple_of((step + count) * TILE, TILE), 16), :][0:1, :].astype(F32)
        following = jnp.where(step + count < tiles, following, 0.0)
        nexts = [one[0:1, :] for one in event[1:]] + [following]
        target = each(
            lambda one, after: jnp.where(
                row_id == part_rows - 1, after, pltpu.roll(one, part_rows - 1, 0)
            ),
            event,
            nexts,
        )
        negative = each(lambda one: dot_nt(one, negs_s[...]), final)
        positive = each(
            lambda one, aim: jnp.sum(one.astype(F32) * aim, axis=-1, keepdims=True), final, target
        )
        highest = each(
            lambda neg, pos: jnp.maximum(jnp.max(neg, axis=-1, keepdims=True), pos),
            negative,
            positive,
        )
        neg_exp = each(lambda neg, top: jnp.exp(neg - top), negative, highest)
        pos_exp = each(lambda pos, top: jnp.exp(pos - top), positive, highest)
        totals = each(
            lambda pos, neg: pos + jnp.sum(neg, axis=-1, keepdims=True), pos_exp, neg_exp
        )
        counted = each(lambda start: row_one + start < length - 1, starts)
        losses = each(
            lambda keep, top, total, pos: jnp.sum(
                jnp.where(keep, top + jnp.log(total) - pos, 0.0), axis=0, keepdims=True
            ),
            counted,
            highest,
            totals,
            positive,
        )
        misc_ref[3:4, :] += jnp.broadcast_to(sum(losses), (1, width))
        share = each(lambda keep, total: jnp.where(keep, 1.0 / total, 0.0), counted, totals)
        grad_neg = each(lambda one, scale: (one * scale).astype(BF), neg_exp, share)
        grad_pos = each(
            lambda keep, one, scale: jnp.where(keep, one * scale - 1.0, 0.0), counted, pos_exp, share
        )
        grad_final = each(
            lambda low, pos, aim: dot_nn(low, negs_s[...]) + pos * aim, grad_neg, grad_pos, target
        )
        gneg_ref[...] += dot_tn(jnp.concatenate(grad_neg, axis=0), jnp.concatenate(final, axis=0))
        pushed = each(lambda pos, one: pos * one.astype(F32), grad_pos, final)
        earlier = [carry_s[0:1, :]] + [one[part_rows - 1 : part_rows, :] for one in pushed[:-1]]
        grad_event = each(
            lambda one, before: jnp.where(row_id == 0, before, pltpu.roll(one, 1, 0)),
            pushed,
            earlier,
        )
        carry_s[0:1, :] = pushed[-1][part_rows - 1 : part_rows, :]
        gain_sums = each(
            lambda grad, one: jnp.sum(grad * one, axis=0, keepdims=True), grad_final, normed_out
        )
        misc_ref[2:3, :] += sum(gain_sums)
        grad_hidden = each(
            lambda one, scale, grad: row_back(one, scale, grad * gain_out),
            hidden,
            scale_out,
            grad_final,
        )
        branch = each(lambda one: one.astype(BF), grad_hidden)
        grad_mixed = each(lambda one: dot_nt(one, w_small), branch)
        for span, first, second in zip(spans, grad_event, grad_hidden):
            gatein_s[span, :] = first + second
        small_ref[...] += dot_tn(jnp.concatenate(mixed, axis=0), jnp.concatenate(branch, axis=0))
        gated = each(lambda grad, gate: grad * gate[0], grad_mixed, gates)
        gain_sums = each(
            lambda grad, one: jnp.sum(grad * one, axis=0, keepdims=True), gated, normed_mid
        )
        misc_ref[1:2, :] += sum(gain_sums)
        for span, grad, one, gate in zip(spans, grad_mixed, normed_mid, gates):
            ggate_s[span, :] = (grad * one * gain_mid * gate[1]).astype(BF)
        grad_out = each(
            lambda one, scale, grad: row_back(one, scale, grad * gain_mid).astype(BF) * BF(0.5),
            merged,
            scale_mid,
            gated,
        )
        for span, one in zip(spans, grad_out):
            for group in range(groups):
                part = one[:, group * 128 : (group + 1) * 128]
                gout_s[2 * group, span, :] = jnp.where(low_part, part, BF(0))
                gout_s[2 * group + 1, span, :] = jnp.where(low_part, BF(0), part)

    sweep(middle)
    stores = []
    if not last:
        stores = [
            pltpu.make_async_copy(small_ref, small_out_ref, store_sem.at[0]),
            pltpu.make_async_copy(gneg_ref, gneg_out_ref, store_sem.at[1]),
        ]
    for one in stores:
        one.start()

    def retreat(step, near_step, count, masked):
        span = place(step)
        near = rows_of(near_step, count)
        wide = WIDE

        def retreat_heads(base, _):
            for extra in range(wide):
                group = base * wide + extra
                keys = keys_s[group, near, :]
                total = None
                for half in range(2):
                    head = 2 * group + half
                    gout = gout_s[head, span, :]
                    query = query_s[head, span, :]
                    scores = dot_nt(keys, query)
                    grads = dot_nt(valuem_s[head, near, :], gout)
                    bent = 1.0 + jnp.tanh(scores)
                    weight = scores * bent
                    slope = bent * ((1.0 + (scores + scores)) - weight)
                    grads = grads * slope
                    if masked:
                        rows, columns = corner(count)
                        visible = rows <= columns + (count - 1) * TILE
                        weight = jnp.where(visible, weight, 0.0)
                        grads = jnp.where(visible, grads, 0.0)
                    grads = grads.astype(BF)
                    part = dot_nn(weight.astype(BF), gout)
                    total = part if total is None else total + part
                    dkeys_s[head, near, :] += dot_nn(
                        grads, jnp.concatenate([query[:, 0:128], hot_s[span, :]], axis=1)
                    )
                    dqueryt_s[head, :, span] += dot_nn(keyst_s[head, :, near], grads)
                out_s[group, near, :] += total
            return 0

        lax.fori_loop(0, groups // wide, retreat_heads, 0)

    def retreat_tile(step, _):
        odd = lax.bitwise_and(step, 1)

        @pl.when(odd == 0)
        def _():
            retreat(step, step, 1, True)

        @pl.when(odd == 1)
        def _():
            retreat(step, step - 1, 2, True)

        def before(index, _):
            retreat(step, 2 * index, 2, False)
            return 0

        lax.fori_loop(0, lax.div(step, 2), before, 0)
        return 0

    lax.fori_loop(0, tiles, retreat_tile, 0)

    def finish(step, count):
        span = rows_of(step, count)
        tall = count * TILE
        normed = normed_s[span, :]
        parts = [ggate_s[span, :]]
        grad = jnp.concatenate([out_s[group, span, :] for group in range(groups)], axis=1)
        parts.append((grad * (2.0 / seq) * slope_s[0, span, :].astype(F32)).astype(BF))
        grad = jnp.concatenate(
            [
                jnp.concatenate([dqueryt_s[2 * group, :, span], dqueryt_s[2 * group + 1, :, span]], axis=0).T
                for group in range(groups)
            ],
            axis=1,
        )
        parts.append((grad * 0.5 * slope_s[1, span, :].astype(F32)).astype(BF))
        grad = jnp.concatenate(
            [
                dkeys_s[2 * group, span, 0:128] + dkeys_s[2 * group + 1, span, 0:128]
                for group in range(groups)
            ],
            axis=1,
        )
        parts.append((grad * 2.0 * slope_s[2, span, :].astype(F32)).astype(BF))
        grad_normed = None
        for index in range(4):
            columns = slice(index * width, (index + 1) * width)
            big_ref[:, columns] += dot_tn(normed, parts[index])
            part = dot_nt(parts[index], dense_ref[:, columns])
            grad_normed = part if grad_normed is None else grad_normed + part
        hott = hott_s[:, span]
        for head in range(heads):
            wide = dkeys_s[head, span, 128:256]
            upper = wide.astype(BF)
            lower = (wide - upper.astype(F32)).astype(BF)
            pairs_s[head] += dot_nn(hott, upper) + dot_nn(hott, lower)
        event = event_s[span, :].astype(F32)
        scale = row_scale(event)
        misc_ref[0:1, :] += jnp.sum(grad_normed * event * scale, axis=0, keepdims=True)
        total = gatein_s[span, :] + row_back(event, scale, grad_normed * gain_in)
        column = orderc_s[...]
        hot = jnp.where(
            jnp.concatenate([column] * (tall // 128), axis=1)
            == lax.broadcasted_iota(jnp.int32, (seq, tall), 1) + step * TILE,
            1.0,
            0.0,
        ).astype(BF)
        moved = dot_nn(hot, total.astype(BF)).astype(BF)
        for block in range(blocks):
            for one in range(pieces):
                ge_ref[one, block] += moved[
                    block * per : (block + 1) * per, one * piece : (one + 1) * piece
                ]

    sweep(finish)
    for one in stores:
        one.wait()

    lane_row = lax.broadcasted_iota(jnp.int32, (64, 128), 1)
    for head in range(heads):
        kept = jnp.where(lane_row < 64, pairs_s[head], 0.0)
        turned = pltpu.roll(kept, 0, 1, stride=1, stride_axis=0)
        misc_ref[8 + head : 9 + head, 0:128] += jnp.sum(turned, axis=0, keepdims=True)
    if last:
        kept = jnp.where(lax.broadcasted_iota(jnp.int32, (8, width), 0) < 3, misc_ref[0:8, :], 0.0)
        gain_rows = jnp.concatenate([kept, jnp.zeros((120, width), F32)], axis=0)
        gain_rows = gain_rows.T.astype(BF)

        def pack(out_ref, target, source, one, block):
            out_ref[target, 0 : 4 * width] = big_ref[source, :].astype(BF)
            out_ref[target, 4 * width : 5 * width] = small_ref[source, :].astype(BF)
            if blocked:
                for index in range(width // piece):
                    start = (block * (width // piece) + index) * own
                    out_ref[target, 5 * width + index * piece : 5 * width + (index + 1) * piece] = gneg_ref[
                        start : start + own, one * piece : (one + 1) * piece
                    ].astype(BF)
            else:
                out_ref[target, 5 * width : 6 * width] = gneg_ref[source, :].astype(BF)
            out_ref[target, 6 * width : 6 * width + 128] = gain_rows[source, :]

        if blocked:
            for core in range(2):

                @pl.when(spot_ref[2] == core)
                def _(core=core):
                    for device in range(devices):
                        one, block = device // blocks, device % blocks
                        source = slice(device * own, (device + 1) * own)
                        target = slice(device // 2 * own, (device // 2 + 1) * own)
                        pack(keep_ref if device % 2 == core else send_ref, target, source, one, block)

        else:
            half = width // 2
            pack(keep_ref, slice(0, half), slice(0, half), 0, 0)
            pack(send_ref, slice(0, half), slice(half, width), 0, 0)


def history_call(length, spot, recv, same, other, bias, before, blocked):
    last = before is not None
    pieces, blocks, tall, piece = recv.shape
    per = tall - 8
    seq = blocks * per
    width = pieces * piece
    heads = width // 64
    groups = heads // 2
    neg_total = width
    vmem = pl.BlockSpec(memory_space=pltpu.VMEM)
    smem = pl.BlockSpec(memory_space=pltpu.SMEM)
    anywhere = pl.BlockSpec(memory_space=pl.ANY)
    shapes = [
        jax.ShapeDtypeStruct((pieces, blocks, per, piece), BF),
        jax.ShapeDtypeStruct((16, width), F32),
    ]
    sums = [(width, 4 * width), (width, width), (neg_total, width)]
    operands = (length, spot, recv, same, other, bias)
    specs = [smem, smem, vmem, anywhere, anywhere, vmem]
    if last:
        operands += tuple(before)
        specs += [vmem, anywhere, anywhere, anywhere]
        shapes += [jax.ShapeDtypeStruct((width // 2, 6 * width + 128), BF)] * 2
        extra = [pltpu.VMEM(one, F32) for one in sums] + [pltpu.SemaphoreType.DMA((3,))]
    else:
        shapes += [jax.ShapeDtypeStruct(one, F32) for one in sums]
        extra = [pltpu.VMEM(one, F32) for one in sums[1:]] + [pltpu.SemaphoreType.DMA((2,))]
    return pl.pallas_call(
        functools.partial(history_kernel, last, blocked),
        out_shape=tuple(shapes),
        in_specs=specs,
        out_specs=(vmem,) * 4 if last else (vmem,) * 3 + (anywhere,) * 2,
        scratch_shapes=extra
        + [
            pltpu.VMEM((seq, width + 128), BF),
            pltpu.VMEM((seq + 16, width), BF),
            pltpu.VMEM((seq, width), BF),
            pltpu.VMEM((seq, width), F32),
            pltpu.VMEM((3, seq, width), BF),
            pltpu.VMEM((heads, seq, 128), BF),
            pltpu.VMEM((heads, seq, 256), BF),
            pltpu.VMEM((groups, seq, 256), BF),
            pltpu.VMEM((heads, 64, seq), BF),
            pltpu.VMEM((seq, 128), BF),
            pltpu.VMEM((64, seq), BF),
            pltpu.VMEM((seq, 128), jnp.int32),
            pltpu.VMEM((8, seq), jnp.int32),
            pltpu.VMEM((groups, seq, 128), F32),
            pltpu.VMEM((heads, seq, 128), BF),
            pltpu.VMEM((seq, width), BF),
            pltpu.VMEM((heads, seq, 256), F32),
            pltpu.VMEM((heads, 64, seq), F32),
            pltpu.VMEM((8, width), F32),
            pltpu.VMEM((heads, 64, 128), F32),
            pltpu.VMEM((8, width), F32),
            pltpu.VMEM((neg_total, width), BF),
            pltpu.VMEM((128, heads * 128), BF),
            pltpu.VMEM((width, same.shape[-1]), BF),
            pltpu.SemaphoreType.DMA((pieces * blocks,)),
        ],
        compiler_params=pltpu.CompilerParams(vmem_limit_bytes=60 * 1024 * 1024),
        cost_estimate=pl.CostEstimate(
            flops=40_000_000_000, bytes_accessed=20_000_000, transcendentals=10_000_000
        ),
        name="history_last" if last else "history_first",
    )(*operands)


def prepare_kernel(
    rows_dev,
    col_count,
    len_ref,
    negs_ref,
    spot_ref,
    items_ref,
    times_ref,
    table_ref,
    w_in_ref,
    w_out_ref,
    gains_ref,
    told_ref,
    payload_ref,
    stage_s,
):
    slots, _, seq = items_ref.shape
    own, width = w_out_ref.shape
    blocks = told_ref.shape[0] // col_count
    per = seq // blocks
    payload_ref[:, 0 : 4 * width] = w_in_ref[...].astype(BF)
    payload_ref[:, 4 * width : 5 * width] = w_out_ref[...].astype(BF)
    neg_own = negs_ref.shape[0] // blocks
    row_place = spot_ref[1] * 2 + spot_ref[2]
    for index in range(neg_own):
        number = negs_ref[row_place * neg_own + index] - row_place * rows_dev
        stage_s[index : index + 1, :] = table_ref[pl.ds(number, 1), :]
    for index in range(neg_own // own):
        payload_ref[:, 5 * width + index * 128 : 5 * width + (index + 1) * 128] = stage_s[
            index * own : (index + 1) * own, :
        ].astype(BF)
    square = jnp.zeros((128, 128), F32)
    stage_s[...] = jnp.zeros_like(stage_s)
    stage_s[0 : gains_ref.shape[0], 0:own] = gains_ref[...]
    square = stage_s[0:128, :].T
    payload_ref[:, 6 * width : 6 * width + 128] = square[0:own, :].astype(BF)
    before = jnp.where(
        lax.broadcasted_iota(jnp.int32, (128, 128), 0) < lax.broadcasted_iota(jnp.int32, (128, 128), 1),
        1.0,
        0.0,
    ).astype(BF)
    block_row = lax.broadcasted_iota(jnp.int32, (blocks, seq), 0)
    time = lax.broadcasted_iota(jnp.int32, (1, seq), 1)
    lane = lax.broadcasted_iota(jnp.int32, (1, 128), 1)
    lengths = jnp.zeros((1, 128), jnp.int32)
    for slot in range(slots):
        lengths = jnp.where(lane == slot, len_ref[0, slot], lengths)
        item = items_ref[slot]
        block = jnp.zeros((1, seq), jnp.int32)
        for index in range(1, blocks):
            block = block + jnp.where(item >= index * rows_dev, 1, 0)
        place = item - block * rows_dev
        member = jnp.where(block_row == block, 1.0, 0.0)
        counts = []
        running = jnp.zeros((blocks, 1), F32)
        for part in range(seq // 128):
            piece = member[:, part * 128 : (part + 1) * 128]
            counts.append(dot_nn(piece.astype(BF), before) + running)
            running = running + jnp.sum(piece, axis=1, keepdims=True)
        rank = jnp.sum(member * jnp.concatenate(counts, axis=1), axis=0, keepdims=True)
        target = block * per + rank.astype(jnp.int32)
        upper = lax.shift_right_logical(place, 6)
        late = lax.shift_right_logical(time, 5)
        values = [upper, place - upper * 64, late, time - late * 32, times_ref[slot]]
        values = jnp.concatenate(values + [jnp.zeros((11, seq), jnp.int32)], axis=0)
        values = values.astype(F32).astype(BF)
        for index in range(seq // 256):
            span = slice(index * 256, (index + 1) * 256)
            hot = jnp.where(
                lax.broadcasted_iota(jnp.int32, (256, seq), 0) + index * 256 == target, 1.0, 0.0
            ).astype(BF)
            moved = dot_nt(values, hot).astype(jnp.int32)
            rows = [moved[0:1] * 64 + moved[1:2], moved[2:3] * 32 + moved[3:4], moved[4:5]]
            for inner in range(256 // per):
                cut = slice(inner * per, (inner + 1) * per)
                row = jnp.concatenate([one[:, cut] for one in rows], axis=0)
                if per < 128:
                    row = jnp.concatenate([row, jnp.zeros((3, 128 - per), jnp.int32)], axis=1)
                for one in range(col_count):
                    told_ref[one * blocks + index * (256 // per) + inner, 3 * slot : 3 * slot + 3, :] = row
    for index in range(told_ref.shape[0]):
        told_ref[index, 3 * slots : 3 * slots + 2, :] = jnp.broadcast_to(lengths, (2, 128))


def prepare_call(lengths, negs, spot, items, times, table, w_in, w_out, gains, devices, col_count):
    slots = items.shape[0]
    own, width = w_out.shape
    smem = pl.BlockSpec(memory_space=pltpu.SMEM)
    vmem = pl.BlockSpec(memory_space=pltpu.VMEM)
    return pl.pallas_call(
        functools.partial(prepare_kernel, table.shape[0], col_count),
        out_shape=(
            jax.ShapeDtypeStruct((devices, 3 * slots + 2, 128), jnp.int32),
            jax.ShapeDtypeStruct((own, 6 * width + 128), BF),
        ),
        in_specs=[smem, smem, smem] + [vmem] * 6,
        out_specs=(vmem, vmem),
        scratch_shapes=[pltpu.VMEM((128, 128), F32)],
        compiler_params=pltpu.CompilerParams(vmem_limit_bytes=60 * 1024 * 1024),
        name="prepare",
    )(lengths, negs, spot, items, times, table, w_in, w_out, gains)


def lookup_kernel(slot, slots, hist_ref, ids_ref, about_ref, table_ref, found_ref, stage_s):
    count, tall, piece = found_ref.shape
    per = tall - 8

    def one(place, _):
        number = hist_ref[slot, place]
        source = lax.div(number, slots)
        line = source * (3 * slots + 2) + 3 * (number - source * slots)
        for index in range(per):
            stage_s[index : index + 1, :] = table_ref[pl.ds(ids_ref[number, index], 1), :]
        found_ref[place, 0:per, :] = stage_s[...].astype(BF)
        spot = about_ref[pl.ds(line + 1, 1), :]
        upper = lax.shift_right_logical(spot, 5)
        times = about_ref[pl.ds(line + 2, 1), :]
        rows = [upper, spot - upper * 32, times, jnp.zeros((5, piece), jnp.int32)]
        found_ref[place, per:tall, :] = jnp.concatenate(rows, axis=0).astype(F32).astype(BF)
        return 0

    lax.fori_loop(0, count, one, 0)


def lookup_call(slot, hist, ids, about, table, per):
    slots, count = hist.shape
    smem = pl.BlockSpec(memory_space=pltpu.SMEM)
    vmem = pl.BlockSpec(memory_space=pltpu.VMEM)
    return pl.pallas_call(
        functools.partial(lookup_kernel, slot, slots),
        out_shape=jax.ShapeDtypeStruct((count, per + 8, table.shape[1]), BF),
        in_specs=[smem, smem, vmem, vmem],
        out_specs=vmem,
        scratch_shapes=[pltpu.VMEM((per, table.shape[1]), F32)],
        compiler_params=pltpu.CompilerParams(vmem_limit_bytes=63 * 1024 * 1024),
        cost_estimate=pl.CostEstimate(
            flops=5_000_000_000, bytes_accessed=4_000_000, transcendentals=0
        ),
        name="lookup",
    )(hist, ids, about, table)


def add_rows(slot, hist_ref, ids_ref, grads_ref, stage_s, sums):
    count = hist_ref.shape[1]
    per = stage_s.shape[0]
    for held in sums:
        held[...] = jnp.zeros_like(held)

    def one(place, _):
        number = hist_ref[slot, place]
        stage_s[...] = grads_ref[pl.ds(pl.multiple_of(place * per, per), per), :].astype(F32)
        for index in range(per):
            held = sums[index % len(sums)]
            spot = pl.ds(ids_ref[number, index], 1)
            held[spot, :] = held[spot, :] + stage_s[index : index + 1, :]
        return 0

    lax.fori_loop(0, count, one, 0)


def scatter_kernel(slot, hist_ref, ids_ref, grads_ref, *refs):
    total_ref, stage_s = refs[-6:-4]
    add_rows(slot, hist_ref, ids_ref, grads_ref, stage_s, refs[-4:])
    total = refs[-4][...]
    for held in refs[-3:]:
        total = total + held[...]
    for init_ref in refs[:-6]:
        total = total + init_ref[...]
    total_ref[...] = total


def scatter_call(slot, hist, heard, grads, rows, per, *init):
    smem = pl.BlockSpec(memory_space=pltpu.SMEM)
    vmem = pl.BlockSpec(memory_space=pltpu.VMEM)
    piece = grads.shape[1]
    return pl.pallas_call(
        functools.partial(scatter_kernel, slot),
        out_shape=jax.ShapeDtypeStruct((rows, piece), F32),
        in_specs=[smem, smem, vmem] + [vmem] * len(init),
        out_specs=vmem,
        scratch_shapes=[pltpu.VMEM((per, piece), F32)] + [pltpu.VMEM((rows, piece), F32)] * 4,
        compiler_params=pltpu.CompilerParams(vmem_limit_bytes=63 * 1024 * 1024),
        cost_estimate=pl.CostEstimate(
            flops=6_000_000_000, bytes_accessed=4_000_000, transcendentals=0
        ),
        name="scatter",
    )(hist, heard, grads, *init)


def gather_up_kernel(width, blocks, negs_ref, spot_ref, table_ref, misc_ref, base_ref, *refs):
    total_ref, shard_ref, gain_ref, told_ref = refs[-4:]
    shard = base_ref[...]
    for got in refs[:-4]:
        shard = shard + got[...].astype(F32)
    shard_ref[...] = shard
    own = shard.shape[0]
    total_ref[...] = table_ref[...]
    neg_own = negs_ref.shape[0] // blocks
    row_place = spot_ref[1] * 2 + spot_ref[2]
    for index in range(neg_own):
        number = negs_ref[row_place * neg_own + index] - row_place * total_ref.shape[0]
        spot = pl.ds(number, 1)
        row = index % own
        start = 5 * width + index // own * 128
        total_ref[spot, :] = total_ref[spot, :] + shard_ref[row : row + 1, start : start + 128]
    total = total_ref[...]
    squares = jnp.sum(total * total, axis=0, keepdims=True)
    for index in range(5 * width // 128):
        part = shard_ref[:, index * 128 : (index + 1) * 128]
        squares = squares + jnp.sum(part * part, axis=0, keepdims=True)
    part = shard_ref[:, 6 * width : 6 * width + 128]
    squares = squares + jnp.sum(part * part, axis=0, keepdims=True)
    turned = jnp.concatenate([part, jnp.zeros((128 - own, 128), F32)], axis=0).T
    gain_ref[...] = turned[0:8, :]
    spread = misc_ref[8:16, 0:128]
    lane = lax.broadcasted_iota(jnp.int32, (8, 128), 1)
    low = jnp.sum(jnp.where(lane < 63, spread, 0.0), axis=1, keepdims=True)
    high = jnp.sum(jnp.where(lane >= 62 + NB, spread, 0.0), axis=1, keepdims=True)
    folded = jnp.where(lane < NB - 1, pltpu.roll(spread, 65, 1), 0.0)
    folded = folded + jnp.where(lane == 0, low, 0.0) + jnp.where(lane == NB - 1, high, 0.0)
    rows = []
    for half in range(2):
        row = folded[4 * half : 4 * half + 1, :]
        for index in range(1, 4):
            row = row + pltpu.roll(folded[4 * half + index : 4 * half + index + 1, :], NB * index, 1)
        rows.append(row)
    rows += [misc_ref[3:4, 0:128], squares]
    told_ref[...] = jnp.broadcast_to(jnp.concatenate(rows, axis=0)[None], told_ref.shape)


def gather_up_call(negs, spot, table_sum, misc, base, gots, devices, row_count):
    smem = pl.BlockSpec(memory_space=pltpu.SMEM)
    vmem = pl.BlockSpec(memory_space=pltpu.VMEM)
    return pl.pallas_call(
        functools.partial(gather_up_kernel, misc.shape[1], row_count),
        out_shape=(
            jax.ShapeDtypeStruct(table_sum.shape, F32),
            jax.ShapeDtypeStruct(base.shape, F32),
            jax.ShapeDtypeStruct((8, 128), F32),
            jax.ShapeDtypeStruct((devices, 4, 128), F32),
        ),
        in_specs=[smem, smem] + [vmem] * (3 + len(gots)),
        out_specs=(vmem,) * 4,
        compiler_params=pltpu.CompilerParams(vmem_limit_bytes=63 * 1024 * 1024),
        name="gather_up",
    )(negs, spot, table_sum, misc, base, *gots)


def fold_kernel(parts, place_ref, base_ref, *refs):
    gots = refs[: len(refs) - parts]
    own_ref = refs[len(refs) - parts]
    sends = refs[len(refs) - parts + 1 :]
    tall = own_ref.shape[0]
    for offset in range(parts):
        span = pl.ds(pl.multiple_of(lax.bitwise_xor(place_ref[0], offset) * tall, tall), tall)
        total = base_ref[span, :].astype(F32)
        for got in gots:
            total = total + got[span, :].astype(F32)
        if offset == 0:
            own_ref[...] = total
        else:
            sends[offset - 1][...] = total.astype(BF)


def fold_call(place, base, gots, parts):
    tall = base.shape[0] // parts
    vmem = pl.BlockSpec(memory_space=pltpu.VMEM)
    shapes = [jax.ShapeDtypeStruct((tall, base.shape[1]), F32)]
    shapes += [jax.ShapeDtypeStruct((tall, base.shape[1]), BF)] * (parts - 1)
    return pl.pallas_call(
        functools.partial(fold_kernel, parts),
        out_shape=tuple(shapes),
        in_specs=[pl.BlockSpec(memory_space=pltpu.SMEM)] + [vmem] * (1 + len(gots)),
        out_specs=(vmem,) * parts,
        compiler_params=pltpu.CompilerParams(vmem_limit_bytes=63 * 1024 * 1024),
        name="fold",
    )(place, base, *gots)


def update_kernel(
    width,
    count_ref,
    heard_ref,
    shard_ref,
    sum_ref,
    table_ref,
    table_m_ref,
    table_v_ref,
    w_in_ref,
    w_in_m_ref,
    w_in_v_ref,
    w_out_ref,
    w_out_m_ref,
    w_out_v_ref,
    gain_grad_ref,
    gains_ref,
    gains_m_ref,
    gains_v_ref,
    rab_ref,
    rab_m_ref,
    rab_v_ref,
    loss_ref,
    total_ref,
    norm_ref,
    table_new_ref,
    table_m_new_ref,
    table_v_new_ref,
    table_low_ref,
    w_in_new_ref,
    w_in_m_new_ref,
    w_in_v_new_ref,
    w_in_low_ref,
    w_out_new_ref,
    w_out_m_new_ref,
    w_out_v_new_ref,
    w_out_low_ref,
    gains_new_ref,
    gains_m_new_ref,
    gains_v_new_ref,
    rab_new_ref,
    rab_m_new_ref,
    rab_v_new_ref,
    factor_s,
    rab_s,
):
    def update(weight_ref, first_ref, second_ref, grad, rate, outs):
        weight, first, second = adamw_update(
            weight_ref[...], first_ref[...], second_ref[...], grad, rate
        )
        outs[0][...] = weight
        outs[1][...] = first
        outs[2][...] = second
        if len(outs) > 3:
            outs[3][...] = weight.astype(BF)

    @pl.when(pl.program_id(0) == 0)
    def _():
        heard = jnp.sum(heard_ref[...], axis=0)
        for head in range(rab_s.shape[0]):
            rab_s[head : head + 1, :] = heard[
                head // 4 : head // 4 + 1, head % 4 * NB : (head % 4 + 1) * NB
            ]
        count = jnp.full((1, 1), count_ref[0].astype(F32))
        squares = jnp.sum(heard[3:4, :], axis=1, keepdims=True)
        squares = squares + jnp.sum(jnp.sum(heard[0:2, :] * heard[0:2, :], axis=1, keepdims=True), axis=0, keepdims=True)
        norm = jnp.sqrt(squares) / count
        factor = jnp.minimum(1.0, CLIP_NORM / norm) / count
        factor_s[...] = jnp.broadcast_to(factor, factor_s.shape)
        loss_ref[...] = heard[2:3, 0:1]
        total_ref[...] = count
        norm_ref[...] = norm
        update(
            w_in_ref,
            w_in_m_ref,
            w_in_v_ref,
            shard_ref[:, 0 : 4 * width] * factor,
            RATE_DENSE,
            (w_in_new_ref, w_in_m_new_ref, w_in_v_new_ref, w_in_low_ref),
        )
        update(
            w_out_ref,
            w_out_m_ref,
            w_out_v_ref,
            shard_ref[:, 4 * width : 5 * width] * factor,
            RATE_DENSE,
            (w_out_new_ref, w_out_m_new_ref, w_out_v_new_ref, w_out_low_ref),
        )
        update(
            gains_ref,
            gains_m_ref,
            gains_v_ref,
            gain_grad_ref[0:3, 0 : gains_ref.shape[1]] * factor,
            RATE_SMALL,
            (gains_new_ref, gains_m_new_ref, gains_v_new_ref),
        )
        update(
            rab_ref,
            rab_m_ref,
            rab_v_ref,
            rab_s[...] * factor,
            RATE_SMALL,
            (rab_new_ref, rab_m_new_ref, rab_v_new_ref),
        )

    update(
        table_ref,
        table_m_ref,
        table_v_ref,
        sum_ref[...] * factor_s[0:1, :],
        RATE_TABLE,
        (table_new_ref, table_m_new_ref, table_v_new_ref, table_low_ref),
    )


def update_call(count, heard, shard, table_sum, tables, w_ins, w_outs, gain_grad, gains, rabs):
    steps = 2
    rows, piece = table_sum.shape

    def whole(array):
        zeros = (0,) * len(array.shape)
        return pl.BlockSpec(array.shape, lambda step: zeros)

    def block(array):
        return pl.BlockSpec((rows // steps, piece), lambda step: (step, 0))

    operands = [heard, shard, table_sum, *tables, *w_ins, *w_outs, gain_grad, *gains, *rabs]
    specs = [pl.BlockSpec(memory_space=pltpu.SMEM)]
    specs += [block(one) if one.shape == (rows, piece) else whole(one) for one in operands]

    def like(array, kind=F32):
        return jax.ShapeDtypeStruct(array.shape, kind)

    shapes = [jax.ShapeDtypeStruct((1, 1), F32)] * 3
    for group in (tables, w_ins, w_outs, gains, rabs):
        shapes += [like(group[0])] * 3
        if group is tables or group is w_ins or group is w_outs:
            shapes.append(like(group[0], BF))
    return pl.pallas_call(
        functools.partial(update_kernel, shard.shape[1] // 6 // 128 * 128),
        out_shape=tuple(shapes),
        grid=(steps,),
        in_specs=specs,
        out_specs=tuple(block(one) if one.shape == (rows, piece) else whole(one) for one in shapes),
        scratch_shapes=[pltpu.VMEM((8, 128), F32), pltpu.VMEM(rabs[0].shape, F32)],
        compiler_params=pltpu.CompilerParams(vmem_limit_bytes=63 * 1024 * 1024),
        name="update",
    )(count, *operands)


def bias_line(rab):
    first = jnp.broadcast_to(rab[:, :1], (rab.shape[0], 64))
    final = jnp.broadcast_to(rab[:, NB - 1 :], (rab.shape[0], 65 - NB))
    return 0.5 * jnp.concatenate([first, final, rab[:, NB - 1 : 0 : -1]], axis=1)


def adamw_update(weight, first, second, grad, rate):
    first = BETA_ONE * first + (1.0 - BETA_ONE) * grad
    second = BETA_TWO * second + (1.0 - BETA_TWO) * grad * grad
    fixed_first = first / (1.0 - BETA_ONE**STEP)
    fixed_second = second / (1.0 - BETA_TWO**STEP)
    weight = weight - rate * (
        fixed_first / (jnp.sqrt(fixed_second) + EPS_ADAM) + WEIGHT_DECAY * weight
    )
    return (weight, first, second)


def exchange(values, axes, groups=None):
    return lax.all_to_all(
        values, axes, split_axis=0, concat_axis=0, tiled=True, axis_index_groups=groups
    )


def swap_sum(values, axis, count, stride, parts):
    mine = (lax.axis_index(axis) // stride) % parts

    def part(index):
        return lax.dynamic_index_in_dim(values, index, axis=0, keepdims=False)

    total = part(mine).astype(F32)
    for offset in range(1, parts):
        pairs = []
        for place in range(count):
            spot = (place // stride) % parts
            pairs.append((place, place + ((spot ^ offset) - spot) * stride))
        got = lax.ppermute(part(mine ^ offset).astype(BF), axis, pairs)
        total = total + got.astype(F32)
    return total


def swap_parts(sends, axis, count, stride):
    gots = []
    for offset, send in enumerate(sends, 1):
        pairs = []
        for place in range(count):
            spot = place // stride
            pairs.append((place, place + ((spot ^ offset) - spot) * stride))
        gots.append(lax.ppermute(send, axis, pairs))
    return gots


def local(
    lengths,
    items,
    negatives,
    time_buckets,
    table,
    table_m,
    table_v,
    w_in,
    w_in_m,
    w_in_v,
    w_out,
    w_out_m,
    w_out_v,
    gains,
    gains_m,
    gains_v,
    rab,
    rab_m,
    rab_v,
):
    col_count = lax.axis_size("col")
    row_count = lax.axis_size("row")
    devices = col_count * row_count
    row_place = lax.axis_index("row")
    me = lax.axis_index("col") * row_count + row_place
    rows_dev, piece = table.shape
    own, width = w_out.shape
    slots, _, seq = items.shape
    per = seq // row_count
    neg_total = negatives.shape[0]
    neg_own = neg_total // row_count
    blocked = own % 16 == 0
    spot = jnp.stack([lax.axis_index("col"), row_place // 2, row_place % 2])
    told, payload = prepare_call(
        lengths.T,
        negatives,
        spot,
        items,
        time_buckets,
        table,
        w_in,
        w_out,
        gains,
        devices,
        col_count,
    )
    bias = bias_line(rab)
    heard = exchange(told, BOTH)
    if blocked:
        half = row_count // 2
        same = jnp.stack([payload] + swap_parts([payload] * (half - 1), "row", row_count, 2))
        same = jnp.stack([same] + swap_parts([same] * (col_count - 1), "col", col_count, 1))
        same = same.reshape(devices // 2, own, -1)
        other = lax.ppermute(same, "row", [(place, place ^ 1) for place in range(row_count)])
    else:
        dense = lax.all_gather(payload, BOTH, axis=0, tiled=True)
        neg_rows = (
            dense[:, 5 * width : 6 * width]
            .reshape(col_count, row_count, own, neg_own // own, piece)
            .transpose(1, 3, 2, 0, 4)
            .reshape(neg_total, width)
        )
        same = jnp.concatenate([dense[:, : 5 * width], neg_rows, dense[:, 6 * width :]], axis=1)
        other = same
    heard = heard.reshape(-1, 128)
    ids = heard.reshape(devices, -1, 128)[:, : 3 * slots]
    ids = ids.reshape(devices * slots, 3, 128)[:, 0]
    every_length = heard.reshape(devices, -1, 128)[:, 3 * slots, :slots].reshape(-1)
    total = devices * slots
    number = jnp.arange(total)
    ahead = (every_length[None, :] > every_length[:, None]) | (
        (every_length[None, :] == every_length[:, None]) & (number[None, :] < number[:, None])
    )
    rank = jnp.sum(ahead.astype(jnp.int32), axis=1)
    wanted = jnp.stack(
        [
            slot * devices + (jnp.arange(devices) if slot % 2 == 0 else devices - 1 - jnp.arange(devices))
            for slot in range(slots)
        ]
    )
    hist = jnp.sum(
        jnp.where(rank[None, None, :] == wanted[:, :, None], number[None, None, :], 0), axis=2
    )
    my_length = jnp.sum(
        jnp.where(
            rank[None, :] == lax.dynamic_slice_in_dim(wanted, me, 1, axis=1),
            every_length[None, :],
            0,
        ),
        axis=1,
    )
    sent = []
    for slot in range(slots):
        found = lookup_call(slot, hist, ids, heard, table, per)
        sent.append(exchange(found, BOTH).reshape(col_count, row_count, per + 8, piece))
    core = (row_place % 2).reshape(1)
    first = history_call(my_length[0:1], spot, sent[0], same, other, bias, None, blocked)
    back = [exchange(first[0].reshape(devices, per, piece), BOTH)]
    final = history_call(my_length[1:2], spot, sent[1], same, other, bias, first[1:], blocked)
    grad_misc, keep, send = final[1:]
    if not blocked:
        packed = jnp.concatenate([keep, send], axis=0)
        neg_part = (
            packed[:, 5 * width : 6 * width]
            .reshape(row_count, neg_own // own, own, col_count, piece)
            .transpose(3, 0, 2, 1, 4)
            .reshape(width, width)
        )
        packed = jnp.concatenate(
            [packed[:, : 5 * width], neg_part, packed[:, 6 * width :]], axis=1
        ).reshape(devices // 2, 2, own, -1)
        keep = lax.dynamic_index_in_dim(packed, core[0], axis=1, keepdims=False)
        send = lax.dynamic_index_in_dim(packed, 1 - core[0], axis=1, keepdims=False)
        keep = keep.reshape(width // 2, -1)
        send = send.reshape(width // 2, -1)
    loss_count = jnp.sum(jnp.maximum(every_length - 1, 0)).reshape(1)
    half = row_count // 2
    got = lax.ppermute(send, "row", [(place, place ^ 1) for place in range(row_count)])
    if blocked:
        base, *sends = fold_call(spot[0:1], keep, [got], col_count)
    else:
        sends = [got]
    final_rows, back[0] = lax.optimization_barrier((final[0], back[0]))
    back.append(exchange(final_rows.reshape(devices, per, piece), BOTH))
    table_part = scatter_call(
        0, hist, ids, back[0].reshape(devices * per, piece), rows_dev, per
    )
    if blocked:
        gots = swap_parts(sends, "col", col_count, 1)
        gots[0] = lax.optimization_barrier((gots[0], table_part))[0]
        base, *sends = fold_call(spot[1:2], base, gots, half)
        gots = swap_parts(sends, "row", row_count, 2)
    else:
        base = (keep.astype(F32) + sends[0].astype(F32)).reshape(col_count, half * own, -1)
        base = swap_sum(base, "col", col_count, 1, col_count)
        base = swap_sum(base.reshape(half, own, -1), "row", row_count, 2, half)
        gots = []
    table_sum = scatter_call(
        1, hist, ids, back[1].reshape(devices * per, piece), rows_dev, per, table_part
    )
    table_sum, shard, gain_grad, told = gather_up_call(
        negatives, spot, table_sum, grad_misc, base, gots, devices, row_count
    )
    heard = exchange(told, BOTH)
    loss, total_count, norm, *updated = update_call(
        loss_count,
        heard,
        shard,
        table_sum,
        (table, table_m, table_v),
        (w_in, w_in_m, w_in_v),
        (w_out, w_out_m, w_out_v),
        gain_grad,
        (gains, gains_m, gains_v),
        (rab, rab_m, rab_v),
    )
    return (loss.reshape(()), total_count.reshape(()), norm.reshape(()), *updated)


def solution(mesh):
    placed = (
        P(None, ("col", "row")),
        P(None, ("col", "row"), None),
        P(),
        P(None, ("col", "row"), None),
        P("row", "col"),
        P("row", "col"),
        P("row", "col"),
        P(("col", "row"), None),
        P(("col", "row"), None),
        P(("col", "row"), None),
        P(("col", "row"), None),
        P(("col", "row"), None),
        P(("col", "row"), None),
        P(None, ("col", "row")),
        P(None, ("col", "row")),
        P(None, ("col", "row")),
        P(),
        P(),
        P(),
    )
    return jax.shard_map(
        local,
        mesh=mesh,
        in_specs=placed,
        out_specs=(
            P(),
            P(),
            P(),
            P("row", "col"),
            P("row", "col"),
            P("row", "col"),
            P("row", "col"),
            P(("col", "row"), None),
            P(("col", "row"), None),
            P(("col", "row"), None),
            P(("col", "row"), None),
            P(("col", "row"), None),
            P(("col", "row"), None),
            P(("col", "row"), None),
            P(("col", "row"), None),
            P(None, ("col", "row")),
            P(None, ("col", "row")),
            P(None, ("col", "row")),
            P(),
            P(),
            P(),
        ),
        check_vma=False,
    )
```

```python
import functools
import jax
import jax.numpy as jnp
from jax import lax
from jax.experimental import pallas as pl
from jax.experimental.pallas import tpu as pltpu
from jax.sharding import PartitionSpec as P

NB = 32
STEP = 10
BETA_ONE = 0.9
BETA_TWO = 0.999
EPS_ADAM = 1e-08
EPS_NORM = 1e-06
WEIGHT_DECAY = 0.01
CLIP_NORM = 0.05
RATE_TABLE = 0.06
RATE_DENSE = 0.01
RATE_SMALL = 0.5
BOTH = ("col", "row")
TILE = 256
WIDE = 4
PARTS = 1
BF = jnp.bfloat16
F32 = jnp.float32


def dot_nn(left, right):
    return lax.dot_general(left, right, (((1,), (0,)), ((), ())), preferred_element_type=F32)


def dot_nt(left, right):
    return lax.dot_general(left, right, (((1,), (1,)), ((), ())), preferred_element_type=F32)


def dot_tn(left, right):
    return lax.dot_general(left, right, (((0,), (0,)), ((), ())), preferred_element_type=F32)


def row_scale(values):
    return lax.rsqrt(jnp.mean(values * values, axis=-1, keepdims=True) + EPS_NORM)


def row_back(values, scale, grad):
    cubed = scale * scale * scale
    return scale * grad - values * (cubed * jnp.mean(grad * values, axis=-1, keepdims=True))


def silu_slope(values):
    half = 0.5 * jnp.tanh(0.5 * values)
    sigmoid = 0.5 + half
    active = values * sigmoid
    return active, sigmoid + active * (0.5 - half)


def history_kernel(last, blocked, *refs):
    if last:
        (len_ref, spot_ref, recv_ref, same_ref, other_ref, bias_ref) = refs[:6]
        (misc0_ref, big0_ref, small0_ref, gneg0_ref) = refs[6:10]
        (ge_ref, misc_ref, keep_ref, send_ref) = refs[10:14]
        (big_ref, small_ref, gneg_ref, load_sem) = refs[14:18]
        scratch = refs[18:]
    else:
        (len_ref, spot_ref, recv_ref, same_ref, other_ref, bias_ref) = refs[:6]
        (ge_ref, misc_ref, big_ref, small_out_ref, gneg_out_ref) = refs[6:11]
        (small_ref, gneg_ref, store_sem) = refs[11:14]
        scratch = refs[14:]
    (
        rows_s,
        event_s,
        normed_s,
        gatein_s,
        slope_s,
        valuem_s,
        query_s,
        keys_s,
        keyst_s,
        hot_s,
        hott_s,
        orderc_s,
        order_s,
        out_s,
        gout_s,
        ggate_s,
        dkeys_s,
        dqueryt_s,
        carry_s,
        pairs_s,
        gains_s,
        negs_s,
        bias_s,
        dense_ref,
        dense_sem,
    ) = scratch
    pieces, blocks, tall, piece = recv_ref.shape
    per = tall - 8
    seq, width = normed_s.shape
    groups = width // 128
    heads = 2 * groups
    devices = pieces * blocks
    own = width // devices
    length = len_ref[0]
    tiles = lax.div(length + (TILE - 1), TILE)
    lane = lax.broadcasted_iota(jnp.int32, (TILE, 128), 1)
    low_lanes = lane < 64
    pulls = []
    if blocked:
        for index in range(devices // 2):
            far_col, far_z = index // (blocks // 2), index % (blocks // 2)
            base = lax.bitwise_xor(spot_ref[0], far_col) * blocks
            base = base + lax.bitwise_xor(spot_ref[1], far_z) * 2
            for which, source in enumerate((same_ref, other_ref)):
                core = spot_ref[2] if which == 0 else 1 - spot_ref[2]
                target = pl.ds(pl.multiple_of((base + core) * own, own), own)
                pulls.append(
                    pltpu.make_async_copy(
                        source.at[index], dense_ref.at[target, :], dense_sem.at[2 * index + which]
                    )
                )
    else:
        pulls.append(pltpu.make_async_copy(same_ref, dense_ref, dense_sem.at[0]))
    for one in pulls:
        one.start()
    if last:
        loads = [
            pltpu.make_async_copy(big0_ref, big_ref, load_sem.at[0]),
            pltpu.make_async_copy(small0_ref, small_ref, load_sem.at[1]),
            pltpu.make_async_copy(gneg0_ref, gneg_ref, load_sem.at[2]),
        ]
        for one in loads:
            one.start()
    else:
        big_ref[...] = jnp.zeros_like(big_ref)
        small_ref[...] = jnp.zeros_like(small_ref)
        gneg_ref[...] = jnp.zeros_like(gneg_ref)

    def rows_of(step, count):
        return pl.ds(pl.multiple_of(step * TILE, TILE), count * TILE)

    def sweep(function):
        def pair(index, _):
            function(2 * index, 2)
            return 0

        lax.fori_loop(0, lax.div(tiles, 2), pair, 0)

        @pl.when(lax.bitwise_and(tiles, 1) == 1)
        def _():
            function(tiles - 1, 1)

    def place(step):
        return pl.ds(pl.multiple_of(step * TILE, TILE), TILE)

    for block in range(blocks):
        span = slice(block * per, (block + 1) * per)
        for one in range(pieces):
            rows_s[span, one * piece : (one + 1) * piece] = recv_ref[one, block, 0:per, :]
        about = recv_ref[0, block, per : per + 8, :].astype(F32)
        spot = about[0:1, 0:per] * 32.0 + about[1:2, 0:per]
        order_s[0:1, span] = spot.astype(jnp.int32)
        orderc_s[span, :] = jnp.broadcast_to(about[0:1, :] * 32.0 + about[1:2, :], (128, 128)).T[0:per, :].astype(jnp.int32)
        rows_s[span, width : width + 128] = jnp.broadcast_to(about[2:3, :], (128, 128)).T[0:per, :].astype(BF)
    for one in pulls:
        one.wait()
    if blocked:
        for one in range(pieces):
            for block in range(blocks):
                source = slice((one * blocks + block) * own, (one * blocks + block + 1) * own)
                for index in range(width // piece):
                    start = (block * (width // piece) + index) * own
                    negs_s[start : start + own, one * piece : (one + 1) * piece] = dense_ref[
                        source, 5 * width + index * piece : 5 * width + (index + 1) * piece
                    ]
    else:
        negs_s[...] = dense_ref[:, 5 * width : 6 * width]
    gains_s[...] = dense_ref[:, 6 * width : 6 * width + 128].astype(F32).T[0:8, :]
    lane_half = lax.broadcasted_iota(jnp.int32, (64, 128), 1) < 64
    for head in range(heads):
        line = jnp.broadcast_to(bias_ref[head : head + 1, :], (64, 128))
        wide = pltpu.roll(line, 0, 1, stride=1, stride_axis=0)
        again = pltpu.roll(wide, 64, 1)
        whole = jnp.where(lane_half, wide, again)
        upper = whole.astype(BF)
        lower = (whole - upper.astype(F32)).astype(BF)
        bias_s[0:64, head * 128 : (head + 1) * 128] = jnp.where(lane_half, upper, lower)
    bias_s[64:128, :] = jnp.zeros((64, heads * 128), BF)
    misc_ref[...] = misc0_ref[...] if last else jnp.zeros_like(misc_ref)
    ge_ref[...] = jnp.zeros_like(ge_ref)
    carry_s[...] = jnp.zeros_like(carry_s)
    pairs_s[...] = jnp.zeros_like(pairs_s)
    gain_in = gains_s[0:1, :]
    gain_mid = gains_s[1:2, :]
    gain_out = gains_s[2:3, :]

    def project(step, count):
        span = rows_of(step, count)
        tall = count * TILE
        lane = lax.broadcasted_iota(jnp.int32, (tall, 128), 1)
        low_lanes = lane < 64
        hot = jnp.where(
            order_s[0:1, :] == lax.broadcasted_iota(jnp.int32, (tall, seq), 0) + step * TILE,
            1.0,
            0.0,
        ).astype(BF)
        wide = dot_nn(hot, rows_s[...])
        event = wide[:, 0:width]
        times = wide[:, width : width + 128].astype(jnp.int32)
        bucket = jnp.where(times == jnp.bitwise_and(lane, 63), 1.0, 0.0).astype(BF)
        hot_s[span, :] = bucket
        hott_s[:, span] = jnp.where(times == 63 - lane, 1.0, 0.0).T[0:64, :].astype(BF)
        event_s[span, :] = event.astype(BF)
        normed = (event * row_scale(event) * gain_in).astype(BF)
        normed_s[span, :] = normed
        gatein_s[span, :] = dot_nn(normed, dense_ref[:, 0:width])
        active, slope = silu_slope(dot_nn(normed, dense_ref[:, width : 2 * width]))
        slope_s[0, span, :] = slope.astype(BF)
        scaled = active.astype(BF) * BF(1.0 / seq)
        for group in range(groups):
            part = scaled[:, group * 128 : (group + 1) * 128]
            valuem_s[2 * group, span, :] = jnp.where(low_lanes, part, BF(0))
            valuem_s[2 * group + 1, span, :] = jnp.where(low_lanes, BF(0), part)
        active, slope = silu_slope(dot_nn(normed, dense_ref[:, 2 * width : 3 * width]))
        slope_s[1, span, :] = slope.astype(BF)
        scaled = active.astype(BF) * BF(0.25)
        bias = dot_nn(bucket, bias_s[...]).astype(BF)
        for group in range(groups):
            part = scaled[:, group * 128 : (group + 1) * 128]
            query_s[2 * group, span, 0:128] = jnp.where(low_lanes, part, BF(0))
            query_s[2 * group + 1, span, 0:128] = jnp.where(low_lanes, BF(0), part)
            query_s[2 * group, span, 128:256] = bias[:, group * 256 : group * 256 + 128]
            query_s[2 * group + 1, span, 128:256] = bias[:, group * 256 + 128 : group * 256 + 256]
        active, slope = silu_slope(dot_nn(normed, dense_ref[:, 3 * width : 4 * width]))
        slope_s[2, span, :] = slope.astype(BF)
        scaled = active.astype(BF)
        for group in range(groups):
            part = scaled[:, group * 128 : (group + 1) * 128]
            keys_s[group, span, 0:128] = part
            keys_s[group, span, 128:256] = bucket
            turned = part.T
            keyst_s[2 * group, :, span] = turned[0:64, :]
            keyst_s[2 * group + 1, :, span] = turned[64:128, :]
        for group in range(groups):
            out_s[group, span, :] = jnp.zeros((tall, 128), F32)
        for head in range(heads):
            dkeys_s[head, span, :] = jnp.zeros((tall, 256), F32)
            dqueryt_s[head, :, span] = jnp.zeros((64, tall), F32)

    sweep(project)

    def corner(count):
        rows = lax.broadcasted_iota(jnp.int32, (count * TILE, TILE), 0)
        return rows, lax.broadcasted_iota(jnp.int32, (count * TILE, TILE), 1)

    def attend(near_step, step, count, masked):
        near = place(near_step)
        span = rows_of(step, count)
        wide = WIDE

        def attend_heads(base, _):
            for extra in range(wide):
                group = base * wide + extra
                total = None
                for half in range(2):
                    head = 2 * group + half
                    scores = dot_nt(query_s[head, span, :], keys_s[group, near, :])
                    weight = scores + scores * jnp.tanh(scores)
                    if masked:
                        rows, columns = corner(count)
                        weight = jnp.where(columns <= rows, weight, 0.0)
                    part = dot_nn(weight.astype(BF), valuem_s[head, near, :])
                    total = part if total is None else total + part
                out_s[group, span, :] += total
            return 0

        lax.fori_loop(0, groups // wide, attend_heads, 0)

    def attend_tile(near_step, _):
        odd = lax.bitwise_and(tiles - near_step, 1)

        @pl.when(odd == 1)
        def _():
            attend(near_step, near_step, 1, True)

        @pl.when(odd == 0)
        def _():
            attend(near_step, near_step, 2, True)

        first = near_step + 2 - odd

        def beyond(index, _):
            attend(near_step, first + 2 * index, 2, False)
            return 0

        lax.fori_loop(0, lax.div(tiles - first, 2), beyond, 0)
        return 0

    lax.fori_loop(0, tiles, attend_tile, 0)

    if last:
        for one in loads:
            one.wait()

    def middle(step, count):
        part_rows = count * TILE // PARTS
        row_id = lax.broadcasted_iota(jnp.int32, (part_rows, width), 0)
        row_one = lax.broadcasted_iota(jnp.int32, (part_rows, 1), 0)
        low_part = lax.broadcasted_iota(jnp.int32, (part_rows, 128), 1) < 64
        w_small = dense_ref[:, 4 * width : 5 * width]
        starts = [step * TILE + part * part_rows for part in range(PARTS)]
        spans = [pl.ds(pl.multiple_of(start, part_rows), part_rows) for start in starts]

        def each(function, *lists):
            return [function(*values) for values in zip(*lists)]

        event = each(lambda span: event_s[span, :].astype(F32), spans)
        merged = each(
            lambda span: jnp.concatenate([out_s[group, span, :] for group in range(groups)], axis=1),
            spans,
        )
        for group in range(groups):
            out_s[group, rows_of(step, count), :] = jnp.zeros((count * TILE, 128), F32)
        scale_mid = each(row_scale, merged)
        normed_mid = each(lambda one, scale: one * scale, merged, scale_mid)
        gates = each(lambda span: silu_slope(gatein_s[span, :]), spans)
        mixed = each(
            lambda one, gate: (one * gain_mid * gate[0]).astype(BF), normed_mid, gates
        )
        hidden = each(lambda one, low: one + dot_nn(low, w_small), event, mixed)
        scale_out = each(row_scale, hidden)
        normed_out = each(lambda one, scale: one * scale, hidden, scale_out)
        final = each(lambda one: (one * gain_out).astype(BF), normed_out)
        following = event_s[pl.ds(pl.multiple_of((step + count) * TILE, TILE), 16), :][0:1, :].astype(F32)
        following = jnp.where(step + count < tiles, following, 0.0)
        nexts = [one[0:1, :] for one in event[1:]] + [following]
        target = each(
            lambda one, after: jnp.where(
                row_id == part_rows - 1, after, pltpu.roll(one, part_rows - 1, 0)
            ),
            event,
            nexts,
        )
        negative = each(lambda one: dot_nt(one, negs_s[...]), final)
        positive = each(
            lambda one, aim: jnp.sum(one.astype(F32) * aim, axis=-1, keepdims=True), final, target
        )
        highest = each(
            lambda neg, pos: jnp.maximum(jnp.max(neg, axis=-1, keepdims=True), pos),
            negative,
            positive,
        )
        neg_exp = each(lambda neg, top: jnp.exp(neg - top), negative, highest)
        pos_exp = each(lambda pos, top: jnp.exp(pos - top), positive, highest)
        totals = each(
            lambda pos, neg: pos + jnp.sum(neg, axis=-1, keepdims=True), pos_exp, neg_exp
        )
        counted = each(lambda start: row_one + start < length - 1, starts)
        losses = each(
            lambda keep, top, total, pos: jnp.sum(
                jnp.where(keep, top + jnp.log(total) - pos, 0.0), axis=0, keepdims=True
            ),
            counted,
            highest,
            totals,
            positive,
        )
        misc_ref[3:4, :] += jnp.broadcast_to(sum(losses), (1, width))
        share = each(lambda keep, total: jnp.where(keep, 1.0 / total, 0.0), counted, totals)
        grad_neg = each(lambda one, scale: (one * scale).astype(BF), neg_exp, share)
        grad_pos = each(
            lambda keep, one, scale: jnp.where(keep, one * scale - 1.0, 0.0), counted, pos_exp, share
        )
        grad_final = each(
            lambda low, pos, aim: dot_nn(low, negs_s[...]) + pos * aim, grad_neg, grad_pos, target
        )
        gneg_ref[...] += dot_tn(jnp.concatenate(grad_neg, axis=0), jnp.concatenate(final, axis=0))
        pushed = each(lambda pos, one: pos * one.astype(F32), grad_pos, final)
        earlier = [carry_s[0:1, :]] + [one[part_rows - 1 : part_rows, :] for one in pushed[:-1]]
        grad_event = each(
            lambda one, before: jnp.where(row_id == 0, before, pltpu.roll(one, 1, 0)),
            pushed,
            earlier,
        )
        carry_s[0:1, :] = pushed[-1][part_rows - 1 : part_rows, :]
        gain_sums = each(
            lambda grad, one: jnp.sum(grad * one, axis=0, keepdims=True), grad_final, normed_out
        )
        misc_ref[2:3, :] += sum(gain_sums)
        grad_hidden = each(
            lambda one, scale, grad: row_back(one, scale, grad * gain_out),
            hidden,
            scale_out,
            grad_final,
        )
        branch = each(lambda one: one.astype(BF), grad_hidden)
        grad_mixed = each(lambda one: dot_nt(one, w_small), branch)
        for span, first, second in zip(spans, grad_event, grad_hidden):
            gatein_s[span, :] = first + second
        small_ref[...] += dot_tn(jnp.concatenate(mixed, axis=0), jnp.concatenate(branch, axis=0))
        gated = each(lambda grad, gate: grad * gate[0], grad_mixed, gates)
        gain_sums = each(
            lambda grad, one: jnp.sum(grad * one, axis=0, keepdims=True), gated, normed_mid
        )
        misc_ref[1:2, :] += sum(gain_sums)
        for span, grad, one, gate in zip(spans, grad_mixed, normed_mid, gates):
            ggate_s[span, :] = (grad * one * gain_mid * gate[1]).astype(BF)
        grad_out = each(
            lambda one, scale, grad: row_back(one, scale, grad * gain_mid).astype(BF) * BF(0.5),
            merged,
            scale_mid,
            gated,
        )
        for span, one in zip(spans, grad_out):
            for group in range(groups):
                part = one[:, group * 128 : (group + 1) * 128]
                gout_s[2 * group, span, :] = jnp.where(low_part, part, BF(0))
                gout_s[2 * group + 1, span, :] = jnp.where(low_part, BF(0), part)

    sweep(middle)
    stores = []
    if not last:
        stores = [
            pltpu.make_async_copy(small_ref, small_out_ref, store_sem.at[0]),
            pltpu.make_async_copy(gneg_ref, gneg_out_ref, store_sem.at[1]),
        ]
    for one in stores:
        one.start()

    def retreat(step, near_step, count, masked):
        span = place(step)
        near = rows_of(near_step, count)
        wide = WIDE

        def retreat_heads(base, _):
            for extra in range(wide):
                group = base * wide + extra
                keys = keys_s[group, near, :]
                total = None
                for half in range(2):
                    head = 2 * group + half
                    gout = gout_s[head, span, :]
                    query = query_s[head, span, :]
                    scores = dot_nt(keys, query)
                    grads = dot_nt(valuem_s[head, near, :], gout)
                    bent = 1.0 + jnp.tanh(scores)
                    weight = scores * bent
                    slope = bent * ((1.0 + (scores + scores)) - weight)
                    grads = grads * slope
                    if masked:
                        rows, columns = corner(count)
                        visible = rows <= columns + (count - 1) * TILE
                        weight = jnp.where(visible, weight, 0.0)
                        grads = jnp.where(visible, grads, 0.0)
                    grads = grads.astype(BF)
                    part = dot_nn(weight.astype(BF), gout)
                    total = part if total is None else total + part
                    dkeys_s[head, near, :] += dot_nn(
                        grads, jnp.concatenate([query[:, 0:128], hot_s[span, :]], axis=1)
                    )
                    dqueryt_s[head, :, span] += dot_nn(keyst_s[head, :, near], grads)
                out_s[group, near, :] += total
            return 0

        lax.fori_loop(0, groups // wide, retreat_heads, 0)

    def retreat_tile(step, _):
        odd = lax.bitwise_and(step, 1)

        @pl.when(odd == 0)
        def _():
            retreat(step, step, 1, True)

        @pl.when(odd == 1)
        def _():
            retreat(step, step - 1, 2, True)

        def before(index, _):
            retreat(step, 2 * index, 2, False)
            return 0

        lax.fori_loop(0, lax.div(step, 2), before, 0)
        return 0

    lax.fori_loop(0, tiles, retreat_tile, 0)

    def finish(step, count):
        span = rows_of(step, count)
        tall = count * TILE
        normed = normed_s[span, :]
        parts = [ggate_s[span, :]]
        grad = jnp.concatenate([out_s[group, span, :] for group in range(groups)], axis=1)
        parts.append((grad * (2.0 / seq) * slope_s[0, span, :].astype(F32)).astype(BF))
        grad = jnp.concatenate(
            [
                jnp.concatenate([dqueryt_s[2 * group, :, span], dqueryt_s[2 * group + 1, :, span]], axis=0).T
                for group in range(groups)
            ],
            axis=1,
        )
        parts.append((grad * 0.5 * slope_s[1, span, :].astype(F32)).astype(BF))
        grad = jnp.concatenate(
            [
                dkeys_s[2 * group, span, 0:128] + dkeys_s[2 * group + 1, span, 0:128]
                for group in range(groups)
            ],
            axis=1,
        )
        parts.append((grad * 2.0 * slope_s[2, span, :].astype(F32)).astype(BF))
        grad_normed = None
        for index in range(4):
            columns = slice(index * width, (index + 1) * width)
            big_ref[:, columns] += dot_tn(normed, parts[index])
            part = dot_nt(parts[index], dense_ref[:, columns])
            grad_normed = part if grad_normed is None else grad_normed + part
        hott = hott_s[:, span]
        for head in range(heads):
            wide = dkeys_s[head, span, 128:256]
            upper = wide.astype(BF)
            lower = (wide - upper.astype(F32)).astype(BF)
            pairs_s[head] += dot_nn(hott, upper) + dot_nn(hott, lower)
        event = event_s[span, :].astype(F32)
        scale = row_scale(event)
        misc_ref[0:1, :] += jnp.sum(grad_normed * event * scale, axis=0, keepdims=True)
        total = gatein_s[span, :] + row_back(event, scale, grad_normed * gain_in)
        column = orderc_s[...]
        hot = jnp.where(
            jnp.concatenate([column] * (tall // 128), axis=1)
            == lax.broadcasted_iota(jnp.int32, (seq, tall), 1) + step * TILE,
            1.0,
            0.0,
        ).astype(BF)
        moved = dot_nn(hot, total.astype(BF)).astype(BF)
        for block in range(blocks):
            for one in range(pieces):
                ge_ref[one, block] += moved[
                    block * per : (block + 1) * per, one * piece : (one + 1) * piece
                ]

    sweep(finish)
    for one in stores:
        one.wait()

    lane_row = lax.broadcasted_iota(jnp.int32, (64, 128), 1)
    for head in range(heads):
        kept = jnp.where(lane_row < 64, pairs_s[head], 0.0)
        turned = pltpu.roll(kept, 0, 1, stride=1, stride_axis=0)
        misc_ref[8 + head : 9 + head, 0:128] += jnp.sum(turned, axis=0, keepdims=True)
    if last:
        kept = jnp.where(lax.broadcasted_iota(jnp.int32, (8, width), 0) < 3, misc_ref[0:8, :], 0.0)
        gain_rows = jnp.concatenate([kept, jnp.zeros((120, width), F32)], axis=0)
        gain_rows = gain_rows.T.astype(BF)

        def pack(out_ref, target, source, one, block):
            out_ref[target, 0 : 4 * width] = big_ref[source, :].astype(BF)
            out_ref[target, 4 * width : 5 * width] = small_ref[source, :].astype(BF)
            if blocked:
                for index in range(width // piece):
                    start = (block * (width // piece) + index) * own
                    out_ref[target, 5 * width + index * piece : 5 * width + (index + 1) * piece] = gneg_ref[
                        start : start + own, one * piece : (one + 1) * piece
                    ].astype(BF)
            else:
                out_ref[target, 5 * width : 6 * width] = gneg_ref[source, :].astype(BF)
            out_ref[target, 6 * width : 6 * width + 128] = gain_rows[source, :]

        if blocked:
            for core in range(2):

                @pl.when(spot_ref[2] == core)
                def _(core=core):
                    for device in range(devices):
                        one, block = device // blocks, device % blocks
                        source = slice(device * own, (device + 1) * own)
                        target = slice(device // 2 * own, (device // 2 + 1) * own)
                        pack(keep_ref if device % 2 == core else send_ref, target, source, one, block)

        else:
            half = width // 2
            pack(keep_ref, slice(0, half), slice(0, half), 0, 0)
            pack(send_ref, slice(0, half), slice(half, width), 0, 0)


def history_call(length, spot, recv, same, other, bias, before, blocked):
    last = before is not None
    pieces, blocks, tall, piece = recv.shape
    per = tall - 8
    seq = blocks * per
    width = pieces * piece
    heads = width // 64
    groups = heads // 2
    neg_total = width
    vmem = pl.BlockSpec(memory_space=pltpu.VMEM)
    smem = pl.BlockSpec(memory_space=pltpu.SMEM)
    anywhere = pl.BlockSpec(memory_space=pl.ANY)
    shapes = [
        jax.ShapeDtypeStruct((pieces, blocks, per, piece), BF),
        jax.ShapeDtypeStruct((16, width), F32),
    ]
    sums = [(width, 4 * width), (width, width), (neg_total, width)]
    operands = (length, spot, recv, same, other, bias)
    specs = [smem, smem, vmem, anywhere, anywhere, vmem]
    if last:
        operands += tuple(before)
        specs += [vmem, anywhere, anywhere, anywhere]
        shapes += [jax.ShapeDtypeStruct((width // 2, 6 * width + 128), BF)] * 2
        extra = [pltpu.VMEM(one, F32) for one in sums] + [pltpu.SemaphoreType.DMA((3,))]
    else:
        shapes += [jax.ShapeDtypeStruct(one, F32) for one in sums]
        extra = [pltpu.VMEM(one, F32) for one in sums[1:]] + [pltpu.SemaphoreType.DMA((2,))]
    return pl.pallas_call(
        functools.partial(history_kernel, last, blocked),
        out_shape=tuple(shapes),
        in_specs=specs,
        out_specs=(vmem,) * 4 if last else (vmem,) * 3 + (anywhere,) * 2,
        scratch_shapes=extra
        + [
            pltpu.VMEM((seq, width + 128), BF),
            pltpu.VMEM((seq + 16, width), BF),
            pltpu.VMEM((seq, width), BF),
            pltpu.VMEM((seq, width), F32),
            pltpu.VMEM((3, seq, width), BF),
            pltpu.VMEM((heads, seq, 128), BF),
            pltpu.VMEM((heads, seq, 256), BF),
            pltpu.VMEM((groups, seq, 256), BF),
            pltpu.VMEM((heads, 64, seq), BF),
            pltpu.VMEM((seq, 128), BF),
            pltpu.VMEM((64, seq), BF),
            pltpu.VMEM((seq, 128), jnp.int32),
            pltpu.VMEM((8, seq), jnp.int32),
            pltpu.VMEM((groups, seq, 128), F32),
            pltpu.VMEM((heads, seq, 128), BF),
            pltpu.VMEM((seq, width), BF),
            pltpu.VMEM((heads, seq, 256), F32),
            pltpu.VMEM((heads, 64, seq), F32),
            pltpu.VMEM((8, width), F32),
            pltpu.VMEM((heads, 64, 128), F32),
            pltpu.VMEM((8, width), F32),
            pltpu.VMEM((neg_total, width), BF),
            pltpu.VMEM((128, heads * 128), BF),
            pltpu.VMEM((width, same.shape[-1]), BF),
            pltpu.SemaphoreType.DMA((pieces * blocks,)),
        ],
        compiler_params=pltpu.CompilerParams(vmem_limit_bytes=60 * 1024 * 1024),
        cost_estimate=pl.CostEstimate(
            flops=40_000_000_000, bytes_accessed=20_000_000, transcendentals=10_000_000
        ),
        name="history_last" if last else "history_first",
    )(*operands)


def prepare_kernel(
    rows_dev,
    col_count,
    len_ref,
    negs_ref,
    spot_ref,
    items_ref,
    times_ref,
    table_ref,
    w_in_ref,
    w_out_ref,
    gains_ref,
    told_ref,
    payload_ref,
    stage_s,
):
    slots, _, seq = items_ref.shape
    own, width = w_out_ref.shape
    blocks = told_ref.shape[0] // col_count
    per = seq // blocks
    payload_ref[:, 0 : 4 * width] = w_in_ref[...].astype(BF)
    payload_ref[:, 4 * width : 5 * width] = w_out_ref[...].astype(BF)
    neg_own = negs_ref.shape[0] // blocks
    row_place = spot_ref[1] * 2 + spot_ref[2]
    for index in range(neg_own):
        number = negs_ref[row_place * neg_own + index] - row_place * rows_dev
        stage_s[index : index + 1, :] = table_ref[pl.ds(number, 1), :]
    for index in range(neg_own // own):
        payload_ref[:, 5 * width + index * 128 : 5 * width + (index + 1) * 128] = stage_s[
            index * own : (index + 1) * own, :
        ].astype(BF)
    square = jnp.zeros((128, 128), F32)
    stage_s[...] = jnp.zeros_like(stage_s)
    stage_s[0 : gains_ref.shape[0], 0:own] = gains_ref[...]
    square = stage_s[0:128, :].T
    payload_ref[:, 6 * width : 6 * width + 128] = square[0:own, :].astype(BF)
    before = jnp.where(
        lax.broadcasted_iota(jnp.int32, (128, 128), 0) < lax.broadcasted_iota(jnp.int32, (128, 128), 1),
        1.0,
        0.0,
    ).astype(BF)
    block_row = lax.broadcasted_iota(jnp.int32, (blocks, seq), 0)
    time = lax.broadcasted_iota(jnp.int32, (1, seq), 1)
    lane = lax.broadcasted_iota(jnp.int32, (1, 128), 1)
    lengths = jnp.zeros((1, 128), jnp.int32)
    for slot in range(slots):
        lengths = jnp.where(lane == slot, len_ref[0, slot], lengths)
        item = items_ref[slot]
        block = jnp.zeros((1, seq), jnp.int32)
        for index in range(1, blocks):
            block = block + jnp.where(item >= index * rows_dev, 1, 0)
        place = item - block * rows_dev
        member = jnp.where(block_row == block, 1.0, 0.0)
        counts = []
        running = jnp.zeros((blocks, 1), F32)
        for part in range(seq // 128):
            piece = member[:, part * 128 : (part + 1) * 128]
            counts.append(dot_nn(piece.astype(BF), before) + running)
            running = running + jnp.sum(piece, axis=1, keepdims=True)
        rank = jnp.sum(member * jnp.concatenate(counts, axis=1), axis=0, keepdims=True)
        target = block * per + rank.astype(jnp.int32)
        upper = lax.shift_right_logical(place, 6)
        late = lax.shift_right_logical(time, 5)
        values = [upper, place - upper * 64, late, time - late * 32, times_ref[slot]]
        values = jnp.concatenate(values + [jnp.zeros((11, seq), jnp.int32)], axis=0)
        values = values.astype(F32).astype(BF)
        for index in range(seq // 256):
            span = slice(index * 256, (index + 1) * 256)
            hot = jnp.where(
                lax.broadcasted_iota(jnp.int32, (256, seq), 0) + index * 256 == target, 1.0, 0.0
            ).astype(BF)
            moved = dot_nt(values, hot).astype(jnp.int32)
            rows = [moved[0:1] * 64 + moved[1:2], moved[2:3] * 32 + moved[3:4], moved[4:5]]
            for inner in range(256 // per):
                cut = slice(inner * per, (inner + 1) * per)
                row = jnp.concatenate([one[:, cut] for one in rows], axis=0)
                if per < 128:
                    row = jnp.concatenate([row, jnp.zeros((3, 128 - per), jnp.int32)], axis=1)
                for one in range(col_count):
                    told_ref[one * blocks + index * (256 // per) + inner, 3 * slot : 3 * slot + 3, :] = row
    for index in range(told_ref.shape[0]):
        told_ref[index, 3 * slots : 3 * slots + 2, :] = jnp.broadcast_to(lengths, (2, 128))


def prepare_call(lengths, negs, spot, items, times, table, w_in, w_out, gains, devices, col_count):
    slots = items.shape[0]
    own, width = w_out.shape
    smem = pl.BlockSpec(memory_space=pltpu.SMEM)
    vmem = pl.BlockSpec(memory_space=pltpu.VMEM)
    return pl.pallas_call(
        functools.partial(prepare_kernel, table.shape[0], col_count),
        out_shape=(
            jax.ShapeDtypeStruct((devices, 3 * slots + 2, 128), jnp.int32),
            jax.ShapeDtypeStruct((own, 6 * width + 128), BF),
        ),
        in_specs=[smem, smem, smem] + [vmem] * 6,
        out_specs=(vmem, vmem),
        scratch_shapes=[pltpu.VMEM((128, 128), F32)],
        compiler_params=pltpu.CompilerParams(vmem_limit_bytes=60 * 1024 * 1024),
        name="prepare",
    )(lengths, negs, spot, items, times, table, w_in, w_out, gains)


def lookup_kernel(slot, slots, hist_ref, ids_ref, about_ref, table_ref, found_ref, stage_s):
    count, tall, piece = found_ref.shape
    per = tall - 8

    def one(place, _):
        number = hist_ref[slot, place]
        source = lax.div(number, slots)
        line = source * (3 * slots + 2) + 3 * (number - source * slots)
        for index in range(per):
            stage_s[index : index + 1, :] = table_ref[pl.ds(ids_ref[number, index], 1), :]
        found_ref[place, 0:per, :] = stage_s[...].astype(BF)
        spot = about_ref[pl.ds(line + 1, 1), :]
        upper = lax.shift_right_logical(spot, 5)
        times = about_ref[pl.ds(line + 2, 1), :]
        rows = [upper, spot - upper * 32, times, jnp.zeros((5, piece), jnp.int32)]
        found_ref[place, per:tall, :] = jnp.concatenate(rows, axis=0).astype(F32).astype(BF)
        return 0

    lax.fori_loop(0, count, one, 0)


def lookup_call(slot, hist, ids, about, table, per):
    slots, count = hist.shape
    smem = pl.BlockSpec(memory_space=pltpu.SMEM)
    vmem = pl.BlockSpec(memory_space=pltpu.VMEM)
    return pl.pallas_call(
        functools.partial(lookup_kernel, slot, slots),
        out_shape=jax.ShapeDtypeStruct((count, per + 8, table.shape[1]), BF),
        in_specs=[smem, smem, vmem, vmem],
        out_specs=vmem,
        scratch_shapes=[pltpu.VMEM((per, table.shape[1]), F32)],
        compiler_params=pltpu.CompilerParams(vmem_limit_bytes=63 * 1024 * 1024),
        cost_estimate=pl.CostEstimate(
            flops=5_000_000_000, bytes_accessed=4_000_000, transcendentals=0
        ),
        name="lookup",
    )(hist, ids, about, table)


def add_rows(slot, hist_ref, ids_ref, grads_ref, stage_s, sums):
    count = hist_ref.shape[1]
    per = stage_s.shape[0]
    for held in sums:
        held[...] = jnp.zeros_like(held)

    def one(place, _):
        number = hist_ref[slot, place]
        stage_s[...] = grads_ref[pl.ds(pl.multiple_of(place * per, per), per), :].astype(F32)
        for index in range(per):
            held = sums[index % len(sums)]
            spot = pl.ds(ids_ref[number, index], 1)
            held[spot, :] = held[spot, :] + stage_s[index : index + 1, :]
        return 0

    lax.fori_loop(0, count, one, 0)


def scatter_kernel(slot, hist_ref, ids_ref, grads_ref, *refs):
    total_ref, stage_s = refs[-6:-4]
    add_rows(slot, hist_ref, ids_ref, grads_ref, stage_s, refs[-4:])
    total = refs[-4][...]
    for held in refs[-3:]:
        total = total + held[...]
    for init_ref in refs[:-6]:
        total = total + init_ref[...]
    total_ref[...] = total


def scatter_call(slot, hist, heard, grads, rows, per, *init):
    smem = pl.BlockSpec(memory_space=pltpu.SMEM)
    vmem = pl.BlockSpec(memory_space=pltpu.VMEM)
    piece = grads.shape[1]
    return pl.pallas_call(
        functools.partial(scatter_kernel, slot),
        out_shape=jax.ShapeDtypeStruct((rows, piece), F32),
        in_specs=[smem, smem, vmem] + [vmem] * len(init),
        out_specs=vmem,
        scratch_shapes=[pltpu.VMEM((per, piece), F32)] + [pltpu.VMEM((rows, piece), F32)] * 4,
        compiler_params=pltpu.CompilerParams(vmem_limit_bytes=63 * 1024 * 1024),
        cost_estimate=pl.CostEstimate(
            flops=6_000_000_000, bytes_accessed=4_000_000, transcendentals=0
        ),
        name="scatter",
    )(hist, heard, grads, *init)


def gather_up_kernel(width, blocks, negs_ref, spot_ref, table_ref, misc_ref, base_ref, *refs):
    total_ref, shard_ref, gain_ref, told_ref = refs[-4:]
    shard = base_ref[...]
    for got in refs[:-4]:
        shard = shard + got[...].astype(F32)
    shard_ref[...] = shard
    own = shard.shape[0]
    total_ref[...] = table_ref[...]
    neg_own = negs_ref.shape[0] // blocks
    row_place = spot_ref[1] * 2 + spot_ref[2]
    for index in range(neg_own):
        number = negs_ref[row_place * neg_own + index] - row_place * total_ref.shape[0]
        spot = pl.ds(number, 1)
        row = index % own
        start = 5 * width + index // own * 128
        total_ref[spot, :] = total_ref[spot, :] + shard_ref[row : row + 1, start : start + 128]
    total = total_ref[...]
    squares = jnp.sum(total * total, axis=0, keepdims=True)
    for index in range(5 * width // 128):
        part = shard_ref[:, index * 128 : (index + 1) * 128]
        squares = squares + jnp.sum(part * part, axis=0, keepdims=True)
    part = shard_ref[:, 6 * width : 6 * width + 128]
    squares = squares + jnp.sum(part * part, axis=0, keepdims=True)
    turned = jnp.concatenate([part, jnp.zeros((128 - own, 128), F32)], axis=0).T
    gain_ref[...] = turned[0:8, :]
    spread = misc_ref[8:16, 0:128]
    lane = lax.broadcasted_iota(jnp.int32, (8, 128), 1)
    low = jnp.sum(jnp.where(lane < 63, spread, 0.0), axis=1, keepdims=True)
    high = jnp.sum(jnp.where(lane >= 62 + NB, spread, 0.0), axis=1, keepdims=True)
    folded = jnp.where(lane < NB - 1, pltpu.roll(spread, 65, 1), 0.0)
    folded = folded + jnp.where(lane == 0, low, 0.0) + jnp.where(lane == NB - 1, high, 0.0)
    rows = []
    for half in range(2):
        row = folded[4 * half : 4 * half + 1, :]
        for index in range(1, 4):
            row = row + pltpu.roll(folded[4 * half + index : 4 * half + index + 1, :], NB * index, 1)
        rows.append(row)
    rows += [misc_ref[3:4, 0:128], squares]
    told_ref[...] = jnp.broadcast_to(jnp.concatenate(rows, axis=0)[None], told_ref.shape)


def gather_up_call(negs, spot, table_sum, misc, base, gots, devices, row_count):
    smem = pl.BlockSpec(memory_space=pltpu.SMEM)
    vmem = pl.BlockSpec(memory_space=pltpu.VMEM)
    return pl.pallas_call(
        functools.partial(gather_up_kernel, misc.shape[1], row_count),
        out_shape=(
            jax.ShapeDtypeStruct(table_sum.shape, F32),
            jax.ShapeDtypeStruct(base.shape, F32),
            jax.ShapeDtypeStruct((8, 128), F32),
            jax.ShapeDtypeStruct((devices, 4, 128), F32),
        ),
        in_specs=[smem, smem] + [vmem] * (3 + len(gots)),
        out_specs=(vmem,) * 4,
        compiler_params=pltpu.CompilerParams(vmem_limit_bytes=63 * 1024 * 1024),
        name="gather_up",
    )(negs, spot, table_sum, misc, base, *gots)


def fold_kernel(parts, place_ref, base_ref, *refs):
    gots = refs[: len(refs) - parts]
    own_ref = refs[len(refs) - parts]
    sends = refs[len(refs) - parts + 1 :]
    tall = own_ref.shape[0]
    for offset in range(parts):
        span = pl.ds(pl.multiple_of(lax.bitwise_xor(place_ref[0], offset) * tall, tall), tall)
        total = base_ref[span, :].astype(F32)
        for got in gots:
            total = total + got[span, :].astype(F32)
        if offset == 0:
            own_ref[...] = total
        else:
            sends[offset - 1][...] = total.astype(BF)


def fold_call(place, base, gots, parts):
    tall = base.shape[0] // parts
    vmem = pl.BlockSpec(memory_space=pltpu.VMEM)
    shapes = [jax.ShapeDtypeStruct((tall, base.shape[1]), F32)]
    shapes += [jax.ShapeDtypeStruct((tall, base.shape[1]), BF)] * (parts - 1)
    return pl.pallas_call(
        functools.partial(fold_kernel, parts),
        out_shape=tuple(shapes),
        in_specs=[pl.BlockSpec(memory_space=pltpu.SMEM)] + [vmem] * (1 + len(gots)),
        out_specs=(vmem,) * parts,
        compiler_params=pltpu.CompilerParams(vmem_limit_bytes=63 * 1024 * 1024),
        name="fold",
    )(place, base, *gots)


def update_kernel(
    width,
    count_ref,
    heard_ref,
    shard_ref,
    sum_ref,
    table_ref,
    table_m_ref,
    table_v_ref,
    w_in_ref,
    w_in_m_ref,
    w_in_v_ref,
    w_out_ref,
    w_out_m_ref,
    w_out_v_ref,
    gain_grad_ref,
    gains_ref,
    gains_m_ref,
    gains_v_ref,
    rab_ref,
    rab_m_ref,
    rab_v_ref,
    scalars_ref,
    table_new_ref,
    table_m_new_ref,
    table_v_new_ref,
    table_low_ref,
    w_in_new_ref,
    w_in_m_new_ref,
    w_in_v_new_ref,
    w_in_low_ref,
    w_out_new_ref,
    w_out_m_new_ref,
    w_out_v_new_ref,
    w_out_low_ref,
    gains_new_ref,
    gains_m_new_ref,
    gains_v_new_ref,
    rab_new_ref,
    rab_m_new_ref,
    rab_v_new_ref,
    factor_s,
    rab_s,
):
    def update(weight_ref, first_ref, second_ref, grad, rate, outs):
        weight, first, second = adamw_update(
            weight_ref[...], first_ref[...], second_ref[...], grad, rate
        )
        outs[0][...] = weight
        outs[1][...] = first
        outs[2][...] = second
        if len(outs) > 3:
            outs[3][...] = weight.astype(BF)

    @pl.when(pl.program_id(0) == 0)
    def _():
        heard = jnp.sum(heard_ref[...], axis=0)
        for head in range(rab_s.shape[0]):
            rab_s[head : head + 1, :] = heard[
                head // 4 : head // 4 + 1, head % 4 * NB : (head % 4 + 1) * NB
            ]
        count = jnp.full((1, 1), count_ref[0].astype(F32))
        squares = jnp.sum(heard[3:4, :], axis=1, keepdims=True)
        squares = squares + jnp.sum(jnp.sum(heard[0:2, :] * heard[0:2, :], axis=1, keepdims=True), axis=0, keepdims=True)
        norm = jnp.sqrt(squares) / count
        factor = jnp.minimum(1.0, CLIP_NORM / norm) / count
        factor_s[...] = jnp.broadcast_to(factor, factor_s.shape)
        scalars = [jnp.broadcast_to(one, (1, 128)) for one in (heard[2:3, 0:1], count, norm)]
        scalars_ref[...] = jnp.concatenate(scalars + [jnp.zeros((5, 128), F32)], axis=0)
        update(
            w_in_ref,
            w_in_m_ref,
            w_in_v_ref,
            shard_ref[:, 0 : 4 * width] * factor,
            RATE_DENSE,
            (w_in_new_ref, w_in_m_new_ref, w_in_v_new_ref, w_in_low_ref),
        )
        update(
            w_out_ref,
            w_out_m_ref,
            w_out_v_ref,
            shard_ref[:, 4 * width : 5 * width] * factor,
            RATE_DENSE,
            (w_out_new_ref, w_out_m_new_ref, w_out_v_new_ref, w_out_low_ref),
        )
        update(
            gains_ref,
            gains_m_ref,
            gains_v_ref,
            gain_grad_ref[0:3, 0 : gains_ref.shape[1]] * factor,
            RATE_SMALL,
            (gains_new_ref, gains_m_new_ref, gains_v_new_ref),
        )
        update(
            rab_ref,
            rab_m_ref,
            rab_v_ref,
            rab_s[...] * factor,
            RATE_SMALL,
            (rab_new_ref, rab_m_new_ref, rab_v_new_ref),
        )

    update(
        table_ref,
        table_m_ref,
        table_v_ref,
        sum_ref[...] * factor_s[0:1, :],
        RATE_TABLE,
        (table_new_ref, table_m_new_ref, table_v_new_ref, table_low_ref),
    )


def update_call(count, heard, shard, table_sum, tables, w_ins, w_outs, gain_grad, gains, rabs):
    steps = 2
    rows, piece = table_sum.shape

    def whole(array):
        zeros = (0,) * len(array.shape)
        return pl.BlockSpec(array.shape, lambda step: zeros)

    def block(array):
        return pl.BlockSpec((rows // steps, piece), lambda step: (step, 0))

    operands = [heard, shard, table_sum, *tables, *w_ins, *w_outs, gain_grad, *gains, *rabs]
    specs = [pl.BlockSpec(memory_space=pltpu.SMEM)]
    specs += [block(one) if one.shape == (rows, piece) else whole(one) for one in operands]

    def like(array, kind=F32):
        return jax.ShapeDtypeStruct(array.shape, kind)

    shapes = [jax.ShapeDtypeStruct((8, 128), F32)]
    for group in (tables, w_ins, w_outs, gains, rabs):
        shapes += [like(group[0])] * 3
        if group is tables or group is w_ins or group is w_outs:
            shapes.append(like(group[0], BF))
    return pl.pallas_call(
        functools.partial(update_kernel, shard.shape[1] // 6 // 128 * 128),
        out_shape=tuple(shapes),
        grid=(steps,),
        in_specs=specs,
        out_specs=tuple(block(one) if one.shape == (rows, piece) else whole(one) for one in shapes),
        scratch_shapes=[pltpu.VMEM((8, 128), F32), pltpu.VMEM(rabs[0].shape, F32)],
        compiler_params=pltpu.CompilerParams(vmem_limit_bytes=63 * 1024 * 1024),
        name="update",
    )(count, *operands)


def bias_line(rab):
    first = jnp.broadcast_to(rab[:, :1], (rab.shape[0], 64))
    final = jnp.broadcast_to(rab[:, NB - 1 :], (rab.shape[0], 65 - NB))
    return 0.5 * jnp.concatenate([first, final, rab[:, NB - 1 : 0 : -1]], axis=1)


def adamw_update(weight, first, second, grad, rate):
    first = BETA_ONE * first + (1.0 - BETA_ONE) * grad
    second = BETA_TWO * second + (1.0 - BETA_TWO) * grad * grad
    fixed_first = first / (1.0 - BETA_ONE**STEP)
    fixed_second = second / (1.0 - BETA_TWO**STEP)
    weight = weight - rate * (
        fixed_first / (jnp.sqrt(fixed_second) + EPS_ADAM) + WEIGHT_DECAY * weight
    )
    return (weight, first, second)


def exchange(values, axes, groups=None):
    return lax.all_to_all(
        values, axes, split_axis=0, concat_axis=0, tiled=True, axis_index_groups=groups
    )


def swap_sum(values, axis, count, stride, parts):
    mine = (lax.axis_index(axis) // stride) % parts

    def part(index):
        return lax.dynamic_index_in_dim(values, index, axis=0, keepdims=False)

    total = part(mine).astype(F32)
    for offset in range(1, parts):
        pairs = []
        for place in range(count):
            spot = (place // stride) % parts
            pairs.append((place, place + ((spot ^ offset) - spot) * stride))
        got = lax.ppermute(part(mine ^ offset).astype(BF), axis, pairs)
        total = total + got.astype(F32)
    return total


def swap_parts(sends, axis, count, stride):
    gots = []
    for offset, send in enumerate(sends, 1):
        pairs = []
        for place in range(count):
            spot = place // stride
            pairs.append((place, place + ((spot ^ offset) - spot) * stride))
        gots.append(lax.ppermute(send, axis, pairs))
    return gots


def local(
    lengths,
    items,
    negatives,
    time_buckets,
    table,
    table_m,
    table_v,
    w_in,
    w_in_m,
    w_in_v,
    w_out,
    w_out_m,
    w_out_v,
    gains,
    gains_m,
    gains_v,
    rab,
    rab_m,
    rab_v,
):
    col_count = lax.axis_size("col")
    row_count = lax.axis_size("row")
    devices = col_count * row_count
    row_place = lax.axis_index("row")
    me = lax.axis_index("col") * row_count + row_place
    rows_dev, piece = table.shape
    own, width = w_out.shape
    slots, _, seq = items.shape
    per = seq // row_count
    neg_total = negatives.shape[0]
    neg_own = neg_total // row_count
    blocked = own % 16 == 0
    spot = jnp.stack([lax.axis_index("col"), row_place // 2, row_place % 2])
    told, payload = prepare_call(
        lengths.T,
        negatives,
        spot,
        items,
        time_buckets,
        table,
        w_in,
        w_out,
        gains,
        devices,
        col_count,
    )
    bias = bias_line(rab)
    heard = exchange(told, BOTH)
    if blocked:
        half = row_count // 2
        same = jnp.stack([payload] + swap_parts([payload] * (half - 1), "row", row_count, 2))
        same = jnp.stack([same] + swap_parts([same] * (col_count - 1), "col", col_count, 1))
        same = same.reshape(devices // 2, own, -1)
        other = lax.ppermute(same, "row", [(place, place ^ 1) for place in range(row_count)])
    else:
        dense = lax.all_gather(payload, BOTH, axis=0, tiled=True)
        neg_rows = (
            dense[:, 5 * width : 6 * width]
            .reshape(col_count, row_count, own, neg_own // own, piece)
            .transpose(1, 3, 2, 0, 4)
            .reshape(neg_total, width)
        )
        same = jnp.concatenate([dense[:, : 5 * width], neg_rows, dense[:, 6 * width :]], axis=1)
        other = same
    heard = heard.reshape(-1, 128)
    ids = heard.reshape(devices, -1, 128)[:, : 3 * slots]
    ids = ids.reshape(devices * slots, 3, 128)[:, 0]
    every_length = heard.reshape(devices, -1, 128)[:, 3 * slots, :slots].reshape(-1)
    total = devices * slots
    number = jnp.arange(total)
    ahead = (every_length[None, :] > every_length[:, None]) | (
        (every_length[None, :] == every_length[:, None]) & (number[None, :] < number[:, None])
    )
    rank = jnp.sum(ahead.astype(jnp.int32), axis=1)
    wanted = jnp.stack(
        [
            slot * devices + (jnp.arange(devices) if slot % 2 == 0 else devices - 1 - jnp.arange(devices))
            for slot in range(slots)
        ]
    )
    hist = jnp.sum(
        jnp.where(rank[None, None, :] == wanted[:, :, None], number[None, None, :], 0), axis=2
    )
    my_length = jnp.sum(
        jnp.where(
            rank[None, :] == lax.dynamic_slice_in_dim(wanted, me, 1, axis=1),
            every_length[None, :],
            0,
        ),
        axis=1,
    )
    sent = []
    for slot in range(slots):
        found = lookup_call(slot, hist, ids, heard, table, per)
        sent.append(exchange(found, BOTH).reshape(col_count, row_count, per + 8, piece))
    core = (row_place % 2).reshape(1)
    first = history_call(my_length[0:1], spot, sent[0], same, other, bias, None, blocked)
    back = [exchange(first[0].reshape(devices, per, piece), BOTH)]
    final = history_call(my_length[1:2], spot, sent[1], same, other, bias, first[1:], blocked)
    grad_misc, keep, send = final[1:]
    if not blocked:
        packed = jnp.concatenate([keep, send], axis=0)
        neg_part = (
            packed[:, 5 * width : 6 * width]
            .reshape(row_count, neg_own // own, own, col_count, piece)
            .transpose(3, 0, 2, 1, 4)
            .reshape(width, width)
        )
        packed = jnp.concatenate(
            [packed[:, : 5 * width], neg_part, packed[:, 6 * width :]], axis=1
        ).reshape(devices // 2, 2, own, -1)
        keep = lax.dynamic_index_in_dim(packed, core[0], axis=1, keepdims=False)
        send = lax.dynamic_index_in_dim(packed, 1 - core[0], axis=1, keepdims=False)
        keep = keep.reshape(width // 2, -1)
        send = send.reshape(width // 2, -1)
    loss_count = jnp.sum(jnp.maximum(every_length - 1, 0)).reshape(1)
    half = row_count // 2
    got = lax.ppermute(send, "row", [(place, place ^ 1) for place in range(row_count)])
    if blocked:
        base, *sends = fold_call(spot[0:1], keep, [got], col_count)
    else:
        sends = [got]
    final_rows, back[0] = lax.optimization_barrier((final[0], back[0]))
    back.append(exchange(final_rows.reshape(devices, per, piece), BOTH))
    table_part = scatter_call(
        0, hist, ids, back[0].reshape(devices * per, piece), rows_dev, per
    )
    if blocked:
        gots = swap_parts(sends, "col", col_count, 1)
        gots[0] = lax.optimization_barrier((gots[0], table_part))[0]
        base, *sends = fold_call(spot[1:2], base, gots, half)
        gots = swap_parts(sends, "row", row_count, 2)
    else:
        base = (keep.astype(F32) + sends[0].astype(F32)).reshape(col_count, half * own, -1)
        base = swap_sum(base, "col", col_count, 1, col_count)
        base = swap_sum(base.reshape(half, own, -1), "row", row_count, 2, half)
        gots = []
    table_sum = scatter_call(
        1, hist, ids, back[1].reshape(devices * per, piece), rows_dev, per, table_part
    )
    table_sum, shard, gain_grad, told = gather_up_call(
        negatives, spot, table_sum, grad_misc, base, gots, devices, row_count
    )
    heard = exchange(told, BOTH)
    scalars, *updated = update_call(
        loss_count,
        heard,
        shard,
        table_sum,
        (table, table_m, table_v),
        (w_in, w_in_m, w_in_v),
        (w_out, w_out_m, w_out_v),
        gain_grad,
        (gains, gains_m, gains_v),
        (rab, rab_m, rab_v),
    )
    return (scalars[0, 0], scalars[1, 0], scalars[2, 0], *updated)


def solution(mesh):
    placed = (
        P(None, ("col", "row")),
        P(None, ("col", "row"), None),
        P(),
        P(None, ("col", "row"), None),
        P("row", "col"),
        P("row", "col"),
        P("row", "col"),
        P(("col", "row"), None),
        P(("col", "row"), None),
        P(("col", "row"), None),
        P(("col", "row"), None),
        P(("col", "row"), None),
        P(("col", "row"), None),
        P(None, ("col", "row")),
        P(None, ("col", "row")),
        P(None, ("col", "row")),
        P(),
        P(),
        P(),
    )
    return jax.shard_map(
        local,
        mesh=mesh,
        in_specs=placed,
        out_specs=(
            P(),
            P(),
            P(),
            P("row", "col"),
            P("row", "col"),
            P("row", "col"),
            P("row", "col"),
            P(("col", "row"), None),
            P(("col", "row"), None),
            P(("col", "row"), None),
            P(("col", "row"), None),
            P(("col", "row"), None),
            P(("col", "row"), None),
            P(("col", "row"), None),
            P(("col", "row"), None),
            P(None, ("col", "row")),
            P(None, ("col", "row")),
            P(None, ("col", "row")),
            P(),
            P(),
            P(),
        ),
        check_vma=False,
    )
```
